512 devices in a mesh: group: 16 (over x, y), sub: 32 (over z, core).
Axes of the slice: x: 4, y: 4, z: 16, core: 2. Of those that a mesh axis runs over, the one named last changes fastest.
Arguments:
- source: float32 [128, 1024, 256], P('group', 'sub'), may hold values from -70 to 70
- perm: float32 [128, 1024, 256], P('group', 'sub'), may hold values from 0.2 to 5
- storage: float32 [128, 1024, 256], P('group', 'sub'), may hold values from 0.05 to 0.5
Outputs:
- pressure: float32 [128, 1024, 256], P('group', 'sub')
- preconditioned: float32 [128, 1024, 256], P('group', 'sub')
The draws below stay inside these ranges and needn't reach their ends.
All inputs are finite; a program needn't handle non-finite values.
Results may differ from the reference program's by a relative error of at most 0.0003.
Values sent between devices are 32-bit elements; how exact they have to be, the bound alone decides.
No kernel may reach another device: no remote copies, remote signals or barrier semaphores. Data moves between devices by JAX's collectives and lax.ppermute only.
A program may use at most 64 MiB of HBM per device.

```python
import math
import jax
import jax.numpy as jnp

CX = 8
CY = 32
CZ = 256
SWEEPS = 4
ITERS = 2
NX = 128
NY = 1024
NZ = 256
N_GROUP = 16
N_SUB = 32


def draw_source(key, part):
    key = jax.random.fold_in(key, 11)
    across_x = jnp.arange(NX, dtype=jnp.float32) / NX
    across_y = jnp.arange(NY, dtype=jnp.float32) / NY
    scale = 1.5 * jnp.exp(math.log(3.0) * (across_x[:, None, None] + across_y[None, :, None]))
    noise = jax.random.truncated_normal(key, -5.0, 5.0, (NX, NY, NZ), jnp.float32)
    return scale * noise


def levels(rng, shape, shards, least, high):
    level = 1.0
    for axis_at, blocks in shards:
        heights = jax.random.uniform(jax.random.fold_in(jax.random.fold_in(rng, 6), axis_at), (blocks,), jnp.float32, least / len(shards), high / len(shards))
        level = level * jnp.repeat(jnp.exp(heights), shape[axis_at] // blocks).reshape((-1,) + (1,) * (len(shape) - 1 - axis_at))
    return level


def setup_inputs(seed: int = 0) -> dict:
    arg_keys = jax.random.split(jax.random.key(seed), 4)
    return {
        "source": draw_source(jax.random.fold_in(arg_keys[3], 71), 0),
        "perm": jnp.clip(jnp.exp(math.log(5.0) - 3.218876 * jax.random.uniform(arg_keys[1], (NX, NY, NZ), jnp.float32) ** levels(arg_keys[1], (NX, NY, NZ), ((0, 16), (1, 32)), -0.2, 0.2)), 0.2, 5.0),
        "storage": jnp.clip(jnp.exp(math.log(0.5) - 2.3025851 * jax.random.uniform(arg_keys[2], (NX, NY, NZ), jnp.float32) ** levels(arg_keys[2], (NX, NY, NZ), ((0, 16), (1, 32)), -0.2, 0.2)), 0.05, 0.5),
    }


OMEGA = 0.8

def harmonic(left, right):
    return 2.0 * left * right / (left + right)

def assemble(diag_all, off_all):
    count = diag_all.shape[0]
    index = jnp.arange(count)
    following = (index + 1) % count
    rows = index[:, None]
    cols = index[None, :]
    matrix = jnp.where(rows == cols, diag_all[:, None], jnp.float32(0.0))
    matrix = matrix + jnp.where(cols == following[:, None], off_all[:, None], jnp.float32(0.0))
    matrix = matrix + jnp.where(rows == following[None, :], off_all[None, :], jnp.float32(0.0))
    return matrix

def solve_coarse(factor, sums):
    return jax.scipy.linalg.cho_solve((factor, True), sums)

def reference(source, perm, storage):
    east_face = harmonic(perm, jnp.roll(perm, -1, 0))
    west_face = jnp.roll(east_face, 1, 0)
    north_face = harmonic(perm, jnp.roll(perm, -1, 1))
    south_face = jnp.roll(north_face, 1, 1)
    upper_face = harmonic(perm, jnp.roll(perm, -1, 2))
    lower_face = jnp.roll(upper_face, 1, 2)
    diagonal = storage + east_face + west_face + north_face + south_face + upper_face + lower_face
    inside_east = (jnp.arange(NX) % CX != CX - 1).astype(jnp.float32)[:, None, None]
    inside_west = (jnp.arange(NX) % CX != 0).astype(jnp.float32)[:, None, None]
    inside_north = (jnp.arange(NY) % CY != CY - 1).astype(jnp.float32)[None, :, None]
    inside_south = (jnp.arange(NY) % CY != 0).astype(jnp.float32)[None, :, None]

    def operate(field):
        total = storage * field
        total = total + east_face * (field - jnp.roll(field, -1, 0)) + west_face * (field - jnp.roll(field, 1, 0))
        total = total + north_face * (field - jnp.roll(field, -1, 1)) + south_face * (field - jnp.roll(field, 1, 1))
        total = total + upper_face * (field - jnp.roll(field, -1, 2)) + lower_face * (field - jnp.roll(field, 1, 2))
        return total

    def local_operator(field):
        total = diagonal * field
        total = total - east_face * inside_east * jnp.roll(field, -1, 0) - west_face * inside_west * jnp.roll(field, 1, 0)
        total = total - north_face * inside_north * jnp.roll(field, -1, 1) - south_face * inside_south * jnp.roll(field, 1, 1)
        total = total - upper_face * jnp.roll(field, -1, 2) - lower_face * jnp.roll(field, 1, 2)
        return total

    def block_sum(field):
        return field.reshape(N_GROUP, CX, N_SUB, CY, CZ).sum(axis=(1, 3, 4))
    north_sum = block_sum(north_face * (1.0 - inside_north))
    south_sum = block_sum(south_face * (1.0 - inside_south))
    coarse_diag = block_sum(storage) / N_SUB + N_SUB * (north_sum + south_sum)
    coarse_off = -N_SUB * north_sum
    factors = jnp.linalg.cholesky(jax.vmap(assemble)(coarse_diag, coarse_off))

    def precondition(resid):
        smooth = OMEGA * resid / diagonal
        for sweep in range(SWEEPS - 1):
            smooth = smooth + OMEGA * (resid - local_operator(smooth)) / diagonal
        coarse = jax.vmap(solve_coarse)(factors, block_sum(resid))
        shaped = smooth.reshape(N_GROUP, CX, N_SUB, CY, CZ) + coarse[:, None, :, None, None]
        return shaped.reshape(NX, NY, NZ)
    pressure = jnp.zeros_like(source)
    resid = source
    precond = precondition(resid)
    direction = precond
    inner_now = jnp.sum(resid * precond)
    for step in range(ITERS):
        image = operate(direction)
        step_size = inner_now / jnp.sum(direction * image)
        pressure = pressure + step_size * direction
        resid = resid - step_size * image
        precond = precondition(resid)
        if step + 1 < ITERS:
            inner_next = jnp.sum(resid * precond)
            direction = precond + inner_next / inner_now * direction
            inner_now = inner_next
    return (pressure, precond)
```

```python
import functools

import jax
import jax.numpy as jnp
from jax import lax
from jax.experimental import pallas as pl
from jax.experimental.pallas import tpu as pltpu
from jax.sharding import PartitionSpec as P

OMEGA = 0.8
LANES = 128
VMEM = 24 * 2**20
STORED, COUPLING, SOURCE, PARTIAL, NORTH, SOUTH, EAST, WEST, EAST_T, WEST_T = range(10)
FROM_EAST, FROM_WEST = 16, 32


def harmonic(left, right):
    return 2.0 * left * right / (left + right)


def shift(value, by, axis):
    return pltpu.roll(value, by % value.shape[axis], axis)


def rows_of(shape):
    return lax.broadcasted_iota(jnp.int32, shape, 0)


def fold(value):
    total = None
    for y in range(0, value.shape[0], 8):
        for z in range(0, value.shape[1], LANES):
            tile = value[y : y + 8, z : z + LANES]
            total = tile if total is None else total + tile
    return total


def total_of(value):
    return jnp.sum(value, axis=(0, 1), keepdims=True)


def placed(totals):
    lane = lax.broadcasted_iota(jnp.int32, (1, LANES), 1)
    row = jnp.zeros((1, LANES), jnp.float32)
    for at, total in totals:
        row = jnp.where(lane == at, total, row)
    return row


def smooth(first, work, weights):
    cx = first.shape[0]
    east, west, north, south, upper, lower = weights

    def sweep(src, dst):
        def slab(x, carry):
            s = src[x + 1]
            total = (1.0 - OMEGA) * s + first[x]
            total = total + east[x] * src[x + 2] + west[x] * src[x]
            total = total + north[x] * shift(s, -1, 0) + south[x] * shift(s, 1, 0)
            total = total + upper[x] * shift(s, -1, 1) + lower[x] * shift(s, 1, 1)
            dst[x + 1] = total
            return carry

        lax.fori_loop(0, cx, slab, 0)

    sweep(work.at[0], work.at[1])
    sweep(work.at[1], work.at[0])
    sweep(work.at[0], work.at[1])


def apply(padded, north_halo, south_halo, storage, faces, out):
    cx, cy = storage.shape[:2]
    east_t, north_t, south_t, upper_t, lower_t = faces

    def slab(x, carry):
        u = padded[x + 1]
        row = rows_of(u.shape)
        north = jnp.where(row == cy - 1, north_halo[pl.ds(x, 1)], shift(u, -1, 0))
        south = jnp.where(row == 0, south_halo[pl.ds(x, 1)], shift(u, 1, 0))
        total = storage[x] * u
        total = total + east_t[x + 1] * (u - padded[x + 2]) + east_t[x] * (u - padded[x])
        total = total + north_t[x] * (u - north) + south_t[x] * (u - south)
        total = total + upper_t[x] * (u - shift(u, -1, 1)) + lower_t[x] * (u - shift(u, 1, 1))
        out[x] = total
        return carry

    lax.fori_loop(0, cx, slab, 0)


def assemble_kernel(
    source, perm, storage, perm_east, perm_west, perm_north, perm_south,
    east_t, north_t, south_t, upper_t, lower_t, scale, w_east, w_west, w_north, w_south, w_upper, w_lower,
    result, to_east, to_west, to_north, to_south, own, first, work,
):
    cx, cy, cz = source.shape
    row = rows_of((cy, cz))
    stored = total_r = inside = jnp.zeros((8, LANES), jnp.float32)
    coupling = jnp.zeros((1, cz), jnp.float32)
    east_t[0] = harmonic(perm_west[...], perm[0])
    for x in range(cx):
        k, w, r = perm[x], storage[x], source[x]
        east = harmonic(k, perm[x + 1] if x + 1 < cx else perm_east[...])
        west = east_t[x]
        north = harmonic(k, jnp.where(row == cy - 1, perm_north[x : x + 1], shift(k, -1, 0)))
        south = jnp.where(row == 0, harmonic(perm_south[x : x + 1], k[0:1]), shift(north, 1, 0))
        upper = harmonic(k, shift(k, -1, 1))
        lower = shift(upper, 1, 1)
        diagonal = w + east + west + north + south + upper + lower
        q = OMEGA / diagonal
        east_t[x + 1] = east
        north_t[x] = north
        south_t[x] = south
        upper_t[x] = upper
        lower_t[x] = lower
        scale[x] = q
        w_east[x] = q * east
        w_west[x] = q * west
        w_north[x] = jnp.where(row == cy - 1, 0.0, q * north)
        w_south[x] = jnp.where(row == 0, 0.0, q * south)
        w_upper[x] = q * upper
        w_lower[x] = q * lower
        s = q * r
        first[x] = s
        work[0, x + 1] = s
        stored = stored + fold(w)
        total_r = total_r + fold(r)
        coupling = coupling + north[cy - 1 : cy]
    outside = jnp.zeros((cy, cz), jnp.float32)
    for at in range(2):
        work[at, 0] = outside
        work[at, cx + 1] = outside
    smooth(first, work, (w_east, w_west, w_north, w_south, w_upper, w_lower))
    flux_north = flux_south = jnp.zeros((1, cz), jnp.float32)
    for x in range(cx):
        s = work[1, x + 1]
        result[x] = s
        inside = inside + fold(storage[x] * s)
        top, bottom = s[cy - 1 : cy], s[0:1]
        to_north[x : x + 1] = top
        to_south[x : x + 1] = bottom
        flux_north = flux_north + north_t[x, cy - 1 : cy] * top
        flux_south = flux_south + south_t[x, 0:1] * bottom
    flux_east = total_of(fold(east_t[cx] * work[1, cx]))
    flux_west = total_of(fold(east_t[0] * work[1, 1]))
    flux_north = total_of(flux_north)
    flux_south = total_of(flux_south)
    totals = (
        (STORED, total_of(stored)),
        (COUPLING, total_of(coupling)),
        (SOURCE, total_of(total_r)),
        (PARTIAL, total_of(inside) + flux_east + flux_west + flux_north + flux_south),
        (NORTH, flux_north),
        (SOUTH, flux_south),
        (EAST, flux_east),
        (WEST, flux_west),
        (EAST_T, total_of(fold(east_t[cx]))),
        (WEST_T, total_of(fold(east_t[0]))),
    )
    scalars = placed(totals)
    own[...] = scalars
    tail = rows_of((8, cz)) == 0
    for out, layer, at in ((to_east, cx, FROM_WEST), (to_west, 1, FROM_EAST)):
        out[0:cy] = work[1, layer]
        moved = pltpu.roll(scalars, at, 1)
        moved = jnp.concatenate([moved] + [jnp.zeros_like(moved)] * (cz // LANES - 1), axis=1)
        out[cy : cy + 8] = jnp.where(tail, moved, 0.0)


def reduce_rows(margin, coupling, steps):
    before, after = shift(coupling, 1, 0), coupling
    factors = []
    for step in range(steps):
        h = 2**step
        inverse = 1.0 / (margin + before + after)
        from_before = before * shift(inverse, h, 0)
        from_after = after * shift(inverse, -h, 0)
        margin = margin + from_before * shift(margin, h, 0) + from_after * shift(margin, -h, 0)
        before, after = from_before * shift(before, h, 0), from_after * shift(after, -h, 0)
        factors.append((from_before, from_after))
    return factors, 1.0 / margin


def solve_rows(factors, last, right):
    for step, (from_before, from_after) in enumerate(factors):
        h = 2**step
        right = right + from_before * shift(right, h, 0) + from_after * shift(right, -h, 0)
    return right * last


def first_kernel(
    steps, axis, table, halo_east, halo_west, halo_north, halo_south, source, storage,
    east_t, north_t, south_t, upper_t, lower_t, scale, w_east, w_west, w_north, w_south, w_upper, w_lower, result,
    u0_ref, u1_ref, to_east, to_west, to_north, to_south, dots, solver, padded, image, first, work, edges,
):
    cx, cy, cz = source.shape
    members = table.shape[0]
    me = lax.axis_index(axis)
    t = table[...]

    def column(at):
        return shift(t, -at, 1)

    factors, last = reduce_rows(column(STORED) / members, column(COUPLING) * members, steps)
    for step, pair in enumerate(factors):
        solver[2 * step] = pair[0]
        solver[2 * step + 1] = pair[1]
    solver[2 * steps] = last
    c0 = solve_rows(factors, last, column(SOURCE))
    c_east, c_west = shift(c0, -FROM_EAST, 1), shift(c0, -FROM_WEST, 1)
    c_north, c_south = shift(c0, -1, 0), shift(c0, 1, 0)
    after = column(COUPLING)
    sums = (
        column(PARTIAL) - shift(column(SOUTH), -1, 0) - shift(column(NORTH), 1, 0)
        - column(FROM_EAST + WEST) - column(FROM_WEST + EAST)
        + column(STORED) * c0 + after * (c0 - c_north) + shift(after, 1, 0) * (c0 - c_south)
        + column(EAST_T) * (c0 - c_east) + column(WEST_T) * (c0 - c_west)
    )
    c1 = solve_rows(factors, last, sums)
    mine = (rows_of(t.shape) == me) & (lax.broadcasted_iota(jnp.int32, t.shape, 1) == 0)

    def pick(value):
        return total_of(jnp.where(mine, value, 0.0))

    here, east, west, north, south, c1 = (pick(c) for c in (c0, c_east, c_west, c_north, c_south, c1))

    padded[0] = halo_west[0:cy] + west
    padded[cx + 1] = halo_east[0:cy] + east
    edges[0] = halo_north[...] + north
    edges[1] = halo_south[...] + south
    for x in range(cx):
        u = result[x] + here
        padded[x + 1] = u
        u0_ref[x] = u
    apply(padded, edges.at[0], edges.at[1], storage, (east_t, north_t, south_t, upper_t, lower_t), image)
    outside = jnp.zeros((cy, cz), jnp.float32)
    for at in range(2):
        work[at, 0] = outside
        work[at, cx + 1] = outside
    for x in range(cx):
        s = scale[x] * image[x]
        first[x] = s
        work[0, x + 1] = s
    smooth(first, work, (w_east, w_west, w_north, w_south, w_upper, w_lower))
    r_u0 = u0_v0 = v0_u1 = r_u1 = jnp.zeros((8, LANES), jnp.float32)
    for x in range(cx):
        u0, v0, r = padded[x + 1], image[x], source[x]
        u1 = work[1, x + 1] + c1
        u1_ref[x] = u1
        to_north[x : x + 1] = u1[cy - 1 : cy]
        to_south[x : x + 1] = u1[0:1]
        r_u0 = r_u0 + fold(r * u0)
        u0_v0 = u0_v0 + fold(u0 * v0)
        v0_u1 = v0_u1 + fold(v0 * u1)
        r_u1 = r_u1 + fold(r * u1)
    to_east[...] = u1_ref[cx - 1]
    to_west[...] = u1_ref[0]
    dots[...] = placed(((1, total_of(r_u0)), (2, total_of(u0_v0)), (3, total_of(v0_u1)), (4, total_of(r_u1))))


def second_kernel(
    halo_east, halo_west, halo_north, halo_south, u0_ref, u1_ref, dots, storage,
    east_t, north_t, south_t, upper_t, lower_t, scale, w_east, w_west, w_north, w_south, w_upper, w_lower,
    result, out, padded, image, first, work,
):
    cx, cy, cz = storage.shape
    padded[0] = halo_west[...]
    padded[cx + 1] = halo_east[...]
    for x in range(cx):
        padded[x + 1] = u1_ref[x]
    apply(padded, halo_north, halo_south, storage, (east_t, north_t, south_t, upper_t, lower_t), image)
    outside = jnp.zeros((cy, cz), jnp.float32)
    for at in range(2):
        work[at, 0] = outside
        work[at, cx + 1] = outside
    total = u1_v1 = u0_v1 = jnp.zeros((8, LANES), jnp.float32)
    for x in range(cx):
        v1 = image[x]
        s = scale[x] * v1
        first[x] = s
        work[0, x + 1] = s
        total = total + fold(v1)
        u1_v1 = u1_v1 + fold(u1_ref[x] * v1)
        u0_v1 = u0_v1 + fold(u0_ref[x] * v1)
    smooth(first, work, (w_east, w_west, w_north, w_south, w_upper, w_lower))
    for x in range(cx):
        result[x] = work[1, x + 1]
    out[...] = dots[...] + placed(((0, total_of(total)), (5, total_of(u1_v1)), (6, total_of(u0_v1))))


def last_kernel(steps, axis, table, solver, u0_ref, u1_ref, result, pressure, precond):
    t = table[...]
    me = lax.axis_index(axis)
    lane = lax.broadcasted_iota(jnp.int32, t.shape, 1)
    factors = [(solver[2 * step], solver[2 * step + 1]) for step in range(steps)]
    c2 = solve_rows(factors, solver[2 * steps], t)
    c2 = total_of(jnp.where((rows_of(t.shape) == me) & (lane == 0), c2, 0.0))
    sums = jnp.sum(t, axis=0, keepdims=True)
    r_u0, u0_v0, v0_u1, r_u1, u1_v1, u0_v1 = (sums[:, at : at + 1] for at in range(1, 7))
    a0 = r_u0 / u0_v0
    rz = r_u0 - a0 * r_u1 - a0 * u0_v0 + a0 * a0 * v0_u1
    keep = 1.0 + rz / r_u0
    a1 = rz / (keep * keep * u0_v0 - keep * a0 * (u0_v1 + v0_u1) + a0 * a0 * u1_v1)
    p0 = a0 + a1 * keep
    p1 = a1 * a0
    z1 = a0 + a1 * keep
    z2 = a1 * a0
    for x in range(u0_ref.shape[0]):
        u0, u1 = u0_ref[x], u1_ref[x]
        pressure[x] = p0 * u0 - p1 * u1
        precond[x] = u0 - z1 * u1 + z2 * (result[x] + c2)


def call(body, outs, scratch, *operands):
    space = pl.BlockSpec(memory_space=pltpu.VMEM)
    return pl.pallas_call(
        body,
        out_shape=[jax.ShapeDtypeStruct(s, jnp.float32) for s in outs],
        in_specs=[space] * len(operands),
        out_specs=[space] * len(outs),
        scratch_shapes=[pltpu.VMEM(s, jnp.float32) for s in scratch],
        compiler_params=pltpu.CompilerParams(vmem_limit_bytes=VMEM),
    )(*operands)


def exchange(to_east, to_west, to_north, to_south):
    def ring(axis):
        peers = lax.axis_size(axis)
        up = [(i, (i + 1) % peers) for i in range(peers)]
        return up, [(j, i) for i, j in up]

    up, down = ring("group")
    west = lax.ppermute(to_east, "group", up)
    east = lax.ppermute(to_west, "group", down)
    up, down = ring("sub")
    south = lax.ppermute(to_north, "sub", up)
    north = lax.ppermute(to_south, "sub", down)
    return east, west, north, south


def gather(row, axis):
    peers = lax.axis_size(axis)
    return lax.all_to_all(jnp.broadcast_to(row[None], (peers, 1, LANES)), axis, 0, 0).reshape(peers, LANES)


def shards(source, perm, storage):
    cx, cy, cz = source.shape
    members = lax.axis_size("sub")
    steps = members.bit_length() - 1
    full, wide, tall, layer, edge = (cx, cy, cz), (cx + 2, cy, cz), (cy + 8, cz), (cy, cz), (cx, cz)
    halos = exchange(perm[-1], perm[0], perm[:, -1], perm[:, 0])
    *shared, result, to_east, to_west, to_north, to_south, own = call(
        assemble_kernel,
        [(cx + 1, cy, cz)] + [full] * 12 + [tall, tall, edge, edge, (1, LANES)],
        [full, (2,) + wide],
        source, perm, storage, *halos,
    )
    halos = exchange(to_east, to_west, to_north, to_south)
    table = gather(own + halos[0][cy : cy + 1, :LANES] + halos[1][cy : cy + 1, :LANES], "sub")
    u0, u1, to_east, to_west, to_north, to_south, dots, solver = call(
        functools.partial(first_kernel, steps, "sub"),
        [full, full, layer, layer, edge, edge, (1, LANES), (2 * steps + 1, members, LANES)],
        [wide, full, full, (2,) + wide, (2,) + edge],
        table, *halos, source, storage, *shared, result,
    )
    halos = exchange(to_east, to_west, to_north, to_south)
    result, row = call(
        second_kernel,
        [full, (1, LANES)],
        [wide, full, full, (2,) + wide],
        *halos, u0, u1, dots, storage, *shared,
    )
    over_groups = jnp.sum(gather(row, "group"), axis=0, keepdims=True)
    row = jnp.where(jnp.arange(LANES)[None] == 0, row, over_groups)
    return tuple(
        call(functools.partial(last_kernel, steps, "sub"), [full, full], [], gather(row, "sub"), solver, u0, u1, result)
    )


def solution(mesh):
    spec = P("group", "sub", None)
    return jax.shard_map(shards, mesh=mesh, in_specs=(spec,) * 3, out_specs=(spec,) * 2, check_vma=False)
```

```python
import functools

import jax
import jax.numpy as jnp
from jax import lax
from jax.experimental import pallas as pl
from jax.experimental.pallas import tpu as pltpu
from jax.sharding import PartitionSpec as P

OMEGA = 0.8
LANES = 128
VMEM = 16 * 2**20
UNROLL = 1
STORED, COUPLING, SOURCE, PARTIAL, NORTH, SOUTH, EAST, WEST, EAST_T, WEST_T = range(10)
FROM_EAST, FROM_WEST = 16, 32


def harmonic(left, right):
    return 2.0 * left * right / (left + right)


def shift(value, by, axis):
    return pltpu.roll(value, by % value.shape[axis], axis)


def rows_of(shape):
    return lax.broadcasted_iota(jnp.int32, shape, 0)


def fold(value):
    total = None
    for y in range(0, value.shape[0], 8):
        for z in range(0, value.shape[1], LANES):
            tile = value[y : y + 8, z : z + LANES]
            total = tile if total is None else total + tile
    return total


def total_of(value):
    return jnp.sum(value, axis=(0, 1), keepdims=True)


def placed(totals):
    lane = lax.broadcasted_iota(jnp.int32, (1, LANES), 1)
    row = jnp.zeros((1, LANES), jnp.float32)
    for at, total in totals:
        row = jnp.where(lane == at, total, row)
    return row


def smooth(first, work, weights):
    cx = first.shape[0]
    east, west, north, south, upper, lower = weights

    def sweep(src, dst):
        def slab(x, carry):
            s = src[x + 1]
            total = (1.0 - OMEGA) * s + first[x]
            total = total + east[x] * src[x + 2] + west[x] * src[x]
            total = total + north[x] * shift(s, -1, 0) + south[x] * shift(s, 1, 0)
            total = total + upper[x] * shift(s, -1, 1) + lower[x] * shift(s, 1, 1)
            dst[x + 1] = total
            return carry

        lax.fori_loop(0, cx, slab, 0, unroll=UNROLL)

    sweep(work.at[0], work.at[1])
    sweep(work.at[1], work.at[0])
    sweep(work.at[0], work.at[1])


def clear_ends(work):
    for at in range(2):
        for end in (0, work.shape[1] - 1):
            work[at, end] = jnp.zeros(work.shape[2:], jnp.float32)


def apply(padded, north_halo, south_halo, storage, inner, edges, out):
    cx, cy = storage.shape[:2]
    east_t, north_t, south_t, upper_t, lower_t = inner
    edge_east, edge_west, edge_north, edge_south = edges

    def slab(x, carry):
        u = padded[x + 1]
        row = rows_of(u.shape)
        total = storage[x] * u
        total = total + east_t[x + 1] * (u - padded[x + 2]) + east_t[x] * (u - padded[x])
        total = total + north_t[x] * (u - shift(u, -1, 0)) + south_t[x] * (u - shift(u, 1, 0))
        total = total + upper_t[x] * (u - shift(u, -1, 1)) + lower_t[x] * (u - shift(u, 1, 1))
        one = pl.ds(x, 1)
        north = jnp.where(row == cy - 1, edge_north[one] * (u - north_halo[one]), 0.0)
        total = total + jnp.where(row == 0, edge_south[one] * (u - south_halo[one]), north)
        out[x] = total
        return carry

    lax.fori_loop(0, cx, slab, 0, unroll=UNROLL)
    out[0] = out[0] + edge_west[...] * (padded[1] - padded[0])
    out[cx - 1] = out[cx - 1] + edge_east[...] * (padded[cx] - padded[cx + 1])


def inner_kernel(perm, storage, east_t, north_t, south_t, upper_t, lower_t, diagonal):
    cx, cy, cz = perm.shape
    row = rows_of((cy, cz))
    west = jnp.zeros((cy, cz), jnp.float32)
    for x in range(cx):
        k = perm[x]
        east = harmonic(k, perm[x + 1]) if x + 1 < cx else jnp.zeros((cy, cz), jnp.float32)
        north = jnp.where(row == cy - 1, 0.0, harmonic(k, shift(k, -1, 0)))
        south = shift(north, 1, 0)
        upper = harmonic(k, shift(k, -1, 1))
        lower = shift(upper, 1, 1)
        east_t[x + 1] = east
        north_t[x] = north
        south_t[x] = south
        upper_t[x] = upper
        lower_t[x] = lower
        diagonal[x] = storage[x] + east + west + north + south + upper + lower
        west = east
    east_t[0] = jnp.zeros((cy, cz), jnp.float32)


def sums_kernel(source, storage, out):
    stored = total_r = jnp.zeros((8, LANES), jnp.float32)
    for x in range(source.shape[0]):
        stored = stored + fold(storage[x])
        total_r = total_r + fold(source[x])
    out[...] = placed(((STORED, total_of(stored)), (SOURCE, total_of(total_r))))


def assemble_kernel(
    perm_a, perm_b, perm_north, perm_south, source, perm, storage, sums,
    east_in, north_in, south_in, upper_t, lower_t, diagonal,
    edge_east, edge_west, edge_north, edge_south,
    scale, w_east, w_west, w_north, w_south, w_upper, w_lower, result, to_a, to_b, to_north, to_south, own, first, work,
):
    cx, cy, cz = source.shape
    odd = lax.axis_index("group") % 2 == 1
    row = rows_of((cy, cz))
    a, b = perm_a[...], perm_b[...]
    edge_east[...] = harmonic(perm[cx - 1], jnp.where(odd, b, a))
    edge_west[...] = harmonic(jnp.where(odd, a, b), perm[0])
    top = jnp.concatenate([perm[x, cy - 1 : cy] for x in range(cx)], axis=0)
    bottom = jnp.concatenate([perm[x, 0:1] for x in range(cx)], axis=0)
    edge_north[...] = harmonic(top, perm_north[...])
    edge_south[...] = harmonic(perm_south[...], bottom)
    for x in range(cx):
        d = diagonal[x]
        d = d + jnp.where(row == cy - 1, edge_north[x : x + 1], jnp.where(row == 0, edge_south[x : x + 1], 0.0))
        if x == 0:
            d = d + edge_west[...]
        if x == cx - 1:
            d = d + edge_east[...]
        q = OMEGA / d
        scale[x] = q
        w_east[x] = q * east_in[x + 1]
        w_west[x] = q * east_in[x]
        w_north[x] = q * north_in[x]
        w_south[x] = q * south_in[x]
        w_upper[x] = q * upper_t[x]
        w_lower[x] = q * lower_t[x]
        s = q * source[x]
        first[x] = s
        work[0, x + 1] = s
    clear_ends(work)
    smooth(first, work, (w_east, w_west, w_north, w_south, w_upper, w_lower))
    inside = jnp.zeros((8, LANES), jnp.float32)
    for x in range(cx):
        s = work[1, x + 1]
        result[x] = s
        inside = inside + fold(storage[x] * s)
        to_north[x : x + 1] = s[cy - 1 : cy]
        to_south[x : x + 1] = s[0:1]
    flux_east = total_of(fold(edge_east[...] * work[1, cx]))
    flux_west = total_of(fold(edge_west[...] * work[1, 1]))
    flux_north = total_of(edge_north[...] * to_north[...])
    flux_south = total_of(edge_south[...] * to_south[...])
    totals = (
        (COUPLING, total_of(edge_north[...])),
        (PARTIAL, total_of(inside) + flux_east + flux_west + flux_north + flux_south),
        (NORTH, flux_north),
        (SOUTH, flux_south),
        (EAST, flux_east),
        (WEST, flux_west),
        (EAST_T, total_of(fold(edge_east[...]))),
        (WEST_T, total_of(fold(edge_west[...]))),
    )
    scalars = sums[...] + placed(totals)
    own[...] = scalars
    tail = rows_of((8, cz)) == 0

    def message(layer, at):
        moved = pltpu.roll(scalars, at, 1)
        moved = jnp.concatenate([moved] + [jnp.zeros_like(moved)] * (cz // LANES - 1), axis=1)
        return layer, jnp.where(tail, moved, 0.0)

    east, west = message(work[1, cx], FROM_WEST), message(work[1, 1], FROM_EAST)
    for part, place in ((0, slice(0, cy)), (1, slice(cy, cy + 8))):
        to_a[place] = jnp.where(odd, west[part], east[part])
        to_b[place] = jnp.where(odd, east[part], west[part])


def reduce_rows(margin, coupling, steps):
    before, after = shift(coupling, 1, 0), coupling
    factors = []
    for step in range(steps):
        h = 2**step
        inverse = 1.0 / (margin + before + after)
        from_before = before * shift(inverse, h, 0)
        from_after = after * shift(inverse, -h, 0)
        margin = margin + from_before * shift(margin, h, 0) + from_after * shift(margin, -h, 0)
        before, after = from_before * shift(before, h, 0), from_after * shift(after, -h, 0)
        factors.append((from_before, from_after))
    return factors, 1.0 / margin


def solve_rows(factors, last, right):
    for step, (from_before, from_after) in enumerate(factors):
        h = 2**step
        right = right + from_before * shift(right, h, 0) + from_after * shift(right, -h, 0)
    return right * last


def first_kernel(
    steps, table, halo_a, halo_b, halo_north, halo_south, storage,
    east_t, north_t, south_t, upper_t, lower_t, edge_east, edge_west, edge_north, edge_south,
    scale, w_east, w_west, w_north, w_south, w_upper, w_lower, result,
    u0_ref, image, u1_ref, to_a, to_b, to_north, to_south, solver, padded, first, work, edges,
):
    cx, cy, cz = storage.shape
    members = table.shape[0]
    me = lax.axis_index("sub")
    odd = lax.axis_index("group") % 2 == 1
    t = table[...]

    def column(at):
        return shift(t, -at, 1)

    factors, last = reduce_rows(column(STORED) / members, column(COUPLING) * members, steps)
    for step, pair in enumerate(factors):
        solver[2 * step] = pair[0]
        solver[2 * step + 1] = pair[1]
    solver[2 * steps] = last
    c0 = solve_rows(factors, last, column(SOURCE))
    c_east, c_west = shift(c0, -FROM_EAST, 1), shift(c0, -FROM_WEST, 1)
    c_north, c_south = shift(c0, -1, 0), shift(c0, 1, 0)
    after = column(COUPLING)
    sums = (
        column(PARTIAL) - shift(column(SOUTH), -1, 0) - shift(column(NORTH), 1, 0)
        - column(FROM_EAST + WEST) - column(FROM_WEST + EAST)
        + column(STORED) * c0 + after * (c0 - c_north) + shift(after, 1, 0) * (c0 - c_south)
        + column(EAST_T) * (c0 - c_east) + column(WEST_T) * (c0 - c_west)
    )
    c1 = solve_rows(factors, last, sums)
    mine = (rows_of(t.shape) == me) & (lax.broadcasted_iota(jnp.int32, t.shape, 1) == 0)

    def pick(value):
        return total_of(jnp.where(mine, value, 0.0))

    here, east, west, north, south, c1 = (pick(c) for c in (c0, c_east, c_west, c_north, c_south, c1))

    a, b = halo_a[0:cy], halo_b[0:cy]
    padded[0] = jnp.where(odd, a, b) + west
    padded[cx + 1] = jnp.where(odd, b, a) + east
    edges[0] = halo_north[...] + north
    edges[1] = halo_south[...] + south
    for x in range(cx):
        u = result[x] + here
        padded[x + 1] = u
        u0_ref[x] = u
    inner, outer = (east_t, north_t, south_t, upper_t, lower_t), (edge_east, edge_west, edge_north, edge_south)
    apply(padded, edges.at[0], edges.at[1], storage, inner, outer, image)
    for x in range(cx):
        s = scale[x] * image[x]
        first[x] = s
        work[0, x + 1] = s
    clear_ends(work)
    smooth(first, work, (w_east, w_west, w_north, w_south, w_upper, w_lower))
    for x in range(cx):
        u1 = work[1, x + 1] + c1
        u1_ref[x] = u1
        to_north[x : x + 1] = u1[cy - 1 : cy]
        to_south[x : x + 1] = u1[0:1]
    east, west = u1_ref[cx - 1], u1_ref[0]
    to_a[...] = jnp.where(odd, west, east)
    to_b[...] = jnp.where(odd, east, west)


def dots_kernel(source, u0_ref, image, u1_ref, out):
    r_u0 = u0_v0 = v0_u1 = r_u1 = jnp.zeros((8, LANES), jnp.float32)
    for x in range(source.shape[0]):
        r, u0, v0, u1 = source[x], u0_ref[x], image[x], u1_ref[x]
        r_u0 = r_u0 + fold(r * u0)
        u0_v0 = u0_v0 + fold(u0 * v0)
        v0_u1 = v0_u1 + fold(v0 * u1)
        r_u1 = r_u1 + fold(r * u1)
    out[...] = placed(((1, total_of(r_u0)), (2, total_of(u0_v0)), (3, total_of(v0_u1)), (4, total_of(r_u1))))


def second_kernel(
    halo_a, halo_b, halo_north, halo_south, u0_ref, u1_ref, dots, storage,
    east_t, north_t, south_t, upper_t, lower_t, edge_east, edge_west, edge_north, edge_south,
    scale, w_east, w_west, w_north, w_south, w_upper, w_lower,
    result, out, padded, image, first, work,
):
    cx = storage.shape[0]
    odd = lax.axis_index("group") % 2 == 1
    a, b = halo_a[...], halo_b[...]
    padded[0] = jnp.where(odd, a, b)
    padded[cx + 1] = jnp.where(odd, b, a)
    for x in range(cx):
        padded[x + 1] = u1_ref[x]
    inner, outer = (east_t, north_t, south_t, upper_t, lower_t), (edge_east, edge_west, edge_north, edge_south)
    apply(padded, halo_north, halo_south, storage, inner, outer, image)
    total = u1_v1 = u0_v1 = jnp.zeros((8, LANES), jnp.float32)
    for x in range(cx):
        v1 = image[x]
        s = scale[x] * v1
        first[x] = s
        work[0, x + 1] = s
        total = total + fold(v1)
        u1_v1 = u1_v1 + fold(u1_ref[x] * v1)
        u0_v1 = u0_v1 + fold(u0_ref[x] * v1)
    clear_ends(work)
    smooth(first, work, (w_east, w_west, w_north, w_south, w_upper, w_lower))
    for x in range(cx):
        result[x] = work[1, x + 1]
    out[...] = dots[...] + placed(((0, total_of(total)), (5, total_of(u1_v1)), (6, total_of(u0_v1))))


def last_kernel(steps, table, solver, u0_ref, u1_ref, result, pressure, precond):
    t = table[...]
    me = lax.axis_index("sub")
    lane = lax.broadcasted_iota(jnp.int32, t.shape, 1)
    factors = [(solver[2 * step], solver[2 * step + 1]) for step in range(steps)]
    c2 = solve_rows(factors, solver[2 * steps], t)
    c2 = total_of(jnp.where((rows_of(t.shape) == me) & (lane == 0), c2, 0.0))
    sums = jnp.sum(t, axis=0, keepdims=True)
    r_u0, u0_v0, v0_u1, r_u1, u1_v1, u0_v1 = (sums[:, at : at + 1] for at in range(1, 7))
    a0 = r_u0 / u0_v0
    rz = r_u0 - a0 * r_u1 - a0 * u0_v0 + a0 * a0 * v0_u1
    keep = 1.0 + rz / r_u0
    a1 = rz / (keep * keep * u0_v0 - keep * a0 * (u0_v1 + v0_u1) + a0 * a0 * u1_v1)
    p0 = a0 + a1 * keep
    p1 = a1 * a0
    z1 = a0 + a1 * keep
    z2 = a1 * a0
    for x in range(u0_ref.shape[0]):
        u0, u1 = u0_ref[x], u1_ref[x]
        pressure[x] = p0 * u0 - p1 * u1
        precond[x] = u0 - z1 * u1 + z2 * (result[x] + c2)


def call(body, outs, scratch, *operands, cost=0):
    space = pl.BlockSpec(memory_space=pltpu.VMEM)
    estimate = pl.CostEstimate(flops=cost, bytes_accessed=4 * cost, transcendentals=0) if cost else None
    return pl.pallas_call(
        body,
        out_shape=[jax.ShapeDtypeStruct(s, jnp.float32) for s in outs],
        in_specs=[space] * len(operands),
        out_specs=[space] * len(outs),
        scratch_shapes=[pltpu.VMEM(s, jnp.float32) for s in scratch],
        compiler_params=pltpu.CompilerParams(vmem_limit_bytes=VMEM),
        cost_estimate=estimate,
    )(*operands)


def exchange(to_a, to_b, to_north, to_south):
    groups, peers = lax.axis_size("group"), lax.axis_size("sub")
    a = lax.ppermute(to_a, "group", [(i, i ^ 1) for i in range(groups)])
    b = lax.ppermute(to_b, "group", [(i, (((i + 1) ^ 1) - 1) % groups) for i in range(groups)])
    up = [(i, (i + 1) % peers) for i in range(peers)]
    south = lax.ppermute(to_north, "sub", up)
    north = lax.ppermute(to_south, "sub", [(j, i) for i, j in up])
    return a, b, north, south


def gather(row, axis):
    peers = lax.axis_size(axis)
    return lax.all_to_all(jnp.broadcast_to(row[None], (peers, 1, LANES)), axis, 0, 0).reshape(peers, LANES)


def shards(source, perm, storage):
    cx, cy, cz = source.shape
    members = lax.axis_size("sub")
    steps = members.bit_length() - 1
    full, wide, tall, layer, edge = (cx, cy, cz), (cx + 2, cy, cz), (cy + 8, cz), (cy, cz), (cx, cz)
    row, rounds = (1, LANES), [full, (2,) + wide]
    odd = lax.axis_index("group") % 2
    to_a = lax.dynamic_index_in_dim(perm, (1 - odd) * (cx - 1), 0, keepdims=False)
    to_b = lax.dynamic_index_in_dim(perm, odd * (cx - 1), 0, keepdims=False)
    halos = exchange(to_a, to_b, perm[:, -1], perm[:, 0])
    *inner, diagonal = call(inner_kernel, [(cx + 1, cy, cz)] + [full] * 5, [], perm, storage, cost=2**21)
    (sums,) = call(sums_kernel, [row], [], source, storage, cost=2**19)
    *made, result, to_a, to_b, to_north, to_south, own = call(
        assemble_kernel,
        [layer, layer, edge, edge] + [full] * 8 + [tall, tall, edge, edge, row],
        rounds,
        *halos, source, perm, storage, sums, *inner, diagonal,
    )
    shared = [storage, *inner, *made]
    halos = exchange(to_a, to_b, to_north, to_south)
    mixed = own + halos[0][cy : cy + 1, :LANES] + halos[1][cy : cy + 1, :LANES]
    mixed = jnp.where(jnp.arange(LANES)[None] < 64, mixed, halos[2][:1, :LANES] + halos[3][:1, :LANES])
    u0, image, u1, to_a, to_b, to_north, to_south, solver = call(
        functools.partial(first_kernel, steps),
        [full, full, full, layer, layer, edge, edge, (2 * steps + 1, members, LANES)],
        [wide] + rounds + [(2,) + edge],
        gather(mixed, "sub"), *halos, *shared, result,
    )
    halos = exchange(to_a, to_b, to_north, to_south)
    (dots,) = call(dots_kernel, [row], [], source, u0, image, u1, cost=2**20)
    result, mixed = call(second_kernel, [full, row], [wide, full] + rounds, *halos, u0, u1, dots, *shared)
    by_group = gather(mixed, "group")
    over_groups = sum(by_group[i : i + 1] for i in range(by_group.shape[0]))
    mixed = jnp.where(jnp.arange(LANES)[None] == 0, mixed, over_groups)
    table = gather(mixed, "sub")
    return tuple(call(functools.partial(last_kernel, steps), [full, full], [], table, solver, u0, u1, result))


def solution(mesh):
    spec = P("group", "sub", None)
    return jax.shard_map(shards, mesh=mesh, in_specs=(spec,) * 3, out_specs=(spec,) * 2, check_vma=False)
```

```python
import functools

import jax
import jax.numpy as jnp
from jax import lax
from jax.experimental import pallas as pl
from jax.experimental.pallas import tpu as pltpu
from jax.sharding import PartitionSpec as P

OMEGA = 0.8
LANES = 128
VMEM = 16 * 2**20
UNROLL = True
STORED, COUPLING, SOURCE, PARTIAL, NORTH, SOUTH, EAST, WEST, EAST_T, WEST_T = range(10)
FROM_EAST, FROM_WEST = 16, 32


def harmonic(left, right):
    return 2.0 * left * right / (left + right)


def shift(value, by, axis):
    return pltpu.roll(value, by % value.shape[axis], axis)


def rows_of(shape):
    return lax.broadcasted_iota(jnp.int32, shape, 0)


def fold(value):
    total = None
    for y in range(0, value.shape[0], 8):
        for z in range(0, value.shape[1], LANES):
            tile = value[y : y + 8, z : z + LANES]
            total = tile if total is None else total + tile
    return total


def total_of(value):
    return jnp.sum(value, axis=(0, 1), keepdims=True)


def placed(totals):
    lane = lax.broadcasted_iota(jnp.int32, (1, LANES), 1)
    row = jnp.zeros((1, LANES), jnp.float32)
    for at, total in totals:
        row = jnp.where(lane == at, total, row)
    return row


def smooth(first, work, weights):
    cx = first.shape[0]
    east, west, north, south, upper, lower = weights

    def sweep(src, dst):
        def slab(x, carry):
            s = src[x + 1]
            total = (1.0 - OMEGA) * s + first[x]
            total = total + east[x] * src[x + 2] + west[x] * src[x]
            total = total + north[x] * shift(s, -1, 0) + south[x] * shift(s, 1, 0)
            total = total + upper[x] * shift(s, -1, 1) + lower[x] * shift(s, 1, 1)
            dst[x + 1] = total
            return carry

        lax.fori_loop(0, cx, slab, 0, unroll=UNROLL)

    sweep(work.at[0], work.at[1])
    sweep(work.at[1], work.at[0])
    sweep(work.at[0], work.at[1])


def clear_ends(work):
    for at in range(2):
        for end in (0, work.shape[1] - 1):
            work[at, end] = jnp.zeros(work.shape[2:], jnp.float32)


def apply(padded, north_halo, south_halo, storage, inner, edges, out):
    cx, cy = storage.shape[:2]
    east_t, north_t, south_t, upper_t, lower_t = inner
    edge_east, edge_west, edge_north, edge_south = edges

    def slab(x, carry):
        u = padded[x + 1]
        row = rows_of(u.shape)
        total = storage[x] * u
        total = total + east_t[x + 1] * (u - padded[x + 2]) + east_t[x] * (u - padded[x])
        total = total + north_t[x] * (u - shift(u, -1, 0)) + south_t[x] * (u - shift(u, 1, 0))
        total = total + upper_t[x] * (u - shift(u, -1, 1)) + lower_t[x] * (u - shift(u, 1, 1))
        one = pl.ds(x, 1)
        north = jnp.where(row == cy - 1, edge_north[one] * (u - north_halo[one]), 0.0)
        total = total + jnp.where(row == 0, edge_south[one] * (u - south_halo[one]), north)
        out[x] = total
        return carry

    lax.fori_loop(0, cx, slab, 0, unroll=UNROLL)
    out[0] = out[0] + edge_west[...] * (padded[1] - padded[0])
    out[cx - 1] = out[cx - 1] + edge_east[...] * (padded[cx] - padded[cx + 1])


def inner_kernel(perm, storage, east_t, north_t, south_t, upper_t, lower_t, diagonal):
    cx, cy, cz = perm.shape
    row = rows_of((cy, cz))
    west = jnp.zeros((cy, cz), jnp.float32)
    for x in range(cx):
        k = perm[x]
        east = harmonic(k, perm[x + 1]) if x + 1 < cx else jnp.zeros((cy, cz), jnp.float32)
        north = jnp.where(row == cy - 1, 0.0, harmonic(k, shift(k, -1, 0)))
        south = shift(north, 1, 0)
        upper = harmonic(k, shift(k, -1, 1))
        lower = shift(upper, 1, 1)
        east_t[x + 1] = east
        north_t[x] = north
        south_t[x] = south
        upper_t[x] = upper
        lower_t[x] = lower
        diagonal[x] = storage[x] + east + west + north + south + upper + lower
        west = east
    east_t[0] = jnp.zeros((cy, cz), jnp.float32)


def sums_kernel(source, storage, out):
    stored = total_r = jnp.zeros((8, LANES), jnp.float32)
    for x in range(source.shape[0]):
        stored = stored + fold(storage[x])
        total_r = total_r + fold(source[x])
    out[...] = placed(((STORED, total_of(stored)), (SOURCE, total_of(total_r))))


def assemble_kernel(
    perm_a, perm_b, perm_north, perm_south, source, perm,
    east_in, north_in, south_in, upper_t, lower_t, diagonal,
    edge_east, edge_west, edge_north, edge_south,
    scale, w_east, w_west, w_north, w_south, w_upper, w_lower, result, to_north, to_south, first, work,
):
    cx, cy, cz = source.shape
    odd = lax.axis_index("group") % 2 == 1
    row = rows_of((cy, cz))
    a, b = perm_a[...], perm_b[...]
    edge_east[...] = harmonic(perm[cx - 1], jnp.where(odd, b, a))
    edge_west[...] = harmonic(jnp.where(odd, a, b), perm[0])
    top = jnp.concatenate([perm[x, cy - 1 : cy] for x in range(cx)], axis=0)
    bottom = jnp.concatenate([perm[x, 0:1] for x in range(cx)], axis=0)
    edge_north[...] = harmonic(top, perm_north[...])
    edge_south[...] = harmonic(perm_south[...], bottom)
    for x in range(cx):
        d = diagonal[x]
        d = d + jnp.where(row == cy - 1, edge_north[x : x + 1], jnp.where(row == 0, edge_south[x : x + 1], 0.0))
        if x == 0:
            d = d + edge_west[...]
        if x == cx - 1:
            d = d + edge_east[...]
        q = OMEGA / d
        scale[x] = q
        w_east[x] = q * east_in[x + 1]
        w_west[x] = q * east_in[x]
        w_north[x] = q * north_in[x]
        w_south[x] = q * south_in[x]
        w_upper[x] = q * upper_t[x]
        w_lower[x] = q * lower_t[x]
        s = q * source[x]
        first[x] = s
        work[0, x + 1] = s
    clear_ends(work)
    smooth(first, work, (w_east, w_west, w_north, w_south, w_upper, w_lower))
    for x in range(cx):
        s = work[1, x + 1]
        result[x] = s
        to_north[x : x + 1] = s[cy - 1 : cy]
        to_south[x : x + 1] = s[0:1]


def pack_kernel(
    storage, sums, result, to_north, to_south, edge_east, edge_west, edge_north, edge_south, to_a, to_b, own
):
    cx, cy, cz = storage.shape
    odd = lax.axis_index("group") % 2 == 1
    inside = jnp.zeros((8, LANES), jnp.float32)
    for x in range(cx):
        inside = inside + fold(storage[x] * result[x])
    flux_east = total_of(fold(edge_east[...] * result[cx - 1]))
    flux_west = total_of(fold(edge_west[...] * result[0]))
    flux_north = total_of(edge_north[...] * to_north[...])
    flux_south = total_of(edge_south[...] * to_south[...])
    totals = (
        (COUPLING, total_of(edge_north[...])),
        (PARTIAL, total_of(inside) + flux_east + flux_west + flux_north + flux_south),
        (NORTH, flux_north),
        (SOUTH, flux_south),
        (EAST, flux_east),
        (WEST, flux_west),
        (EAST_T, total_of(fold(edge_east[...]))),
        (WEST_T, total_of(fold(edge_west[...]))),
    )
    scalars = sums[...] + placed(totals)
    own[...] = scalars
    tail = rows_of((8, cz)) == 0

    def message(layer, at):
        moved = pltpu.roll(scalars, at, 1)
        moved = jnp.concatenate([moved] + [jnp.zeros_like(moved)] * (cz // LANES - 1), axis=1)
        return layer, jnp.where(tail, moved, 0.0)

    east, west = message(result[cx - 1], FROM_WEST), message(result[0], FROM_EAST)
    for part, place in ((0, slice(0, cy)), (1, slice(cy, cy + 8))):
        to_a[place] = jnp.where(odd, west[part], east[part])
        to_b[place] = jnp.where(odd, east[part], west[part])


def reduce_rows(margin, coupling, steps):
    before, after = shift(coupling, 1, 0), coupling
    factors = []
    for step in range(steps):
        h = 2**step
        inverse = 1.0 / (margin + before + after)
        from_before = before * shift(inverse, h, 0)
        from_after = after * shift(inverse, -h, 0)
        margin = margin + from_before * shift(margin, h, 0) + from_after * shift(margin, -h, 0)
        before, after = from_before * shift(before, h, 0), from_after * shift(after, -h, 0)
        factors.append((from_before, from_after))
    return factors, 1.0 / margin


def solve_rows(factors, last, right):
    for step, (from_before, from_after) in enumerate(factors):
        h = 2**step
        right = right + from_before * shift(right, h, 0) + from_after * shift(right, -h, 0)
    return right * last


def first_kernel(
    steps, table, halo_a, halo_b, halo_north, halo_south, storage,
    east_t, north_t, south_t, upper_t, lower_t, edge_east, edge_west, edge_north, edge_south,
    scale, w_east, w_west, w_north, w_south, w_upper, w_lower, result,
    u0_ref, image, u1_ref, to_north, to_south, solver, padded, first, work, edges,
):
    cx, cy, cz = storage.shape
    members = table.shape[0]
    me = lax.axis_index("sub")
    odd = lax.axis_index("group") % 2 == 1
    t = table[...]

    def column(at):
        return shift(t, -at, 1)

    factors, last = reduce_rows(column(STORED) / members, column(COUPLING) * members, steps)
    for step, pair in enumerate(factors):
        solver[2 * step] = pair[0]
        solver[2 * step + 1] = pair[1]
    solver[2 * steps] = last
    c0 = solve_rows(factors, last, column(SOURCE))
    c_east, c_west = shift(c0, -FROM_EAST, 1), shift(c0, -FROM_WEST, 1)
    c_north, c_south = shift(c0, -1, 0), shift(c0, 1, 0)
    after = column(COUPLING)
    sums = (
        column(PARTIAL) - shift(column(SOUTH), -1, 0) - shift(column(NORTH), 1, 0)
        - column(FROM_EAST + WEST) - column(FROM_WEST + EAST)
        + column(STORED) * c0 + after * (c0 - c_north) + shift(after, 1, 0) * (c0 - c_south)
        + column(EAST_T) * (c0 - c_east) + column(WEST_T) * (c0 - c_west)
    )
    c1 = solve_rows(factors, last, sums)
    mine = (rows_of(t.shape) == me) & (lax.broadcasted_iota(jnp.int32, t.shape, 1) == 0)

    def pick(value):
        return total_of(jnp.where(mine, value, 0.0))

    here, east, west, north, south, c1 = (pick(c) for c in (c0, c_east, c_west, c_north, c_south, c1))

    a, b = halo_a[0:cy], halo_b[0:cy]
    padded[0] = jnp.where(odd, a, b) + west
    padded[cx + 1] = jnp.where(odd, b, a) + east
    edges[0] = halo_north[...] + north
    edges[1] = halo_south[...] + south
    for x in range(cx):
        u = result[x] + here
        padded[x + 1] = u
        u0_ref[x] = u
    inner, outer = (east_t, north_t, south_t, upper_t, lower_t), (edge_east, edge_west, edge_north, edge_south)
    apply(padded, edges.at[0], edges.at[1], storage, inner, outer, image)
    for x in range(cx):
        s = scale[x] * image[x]
        first[x] = s
        work[0, x + 1] = s
    clear_ends(work)
    smooth(first, work, (w_east, w_west, w_north, w_south, w_upper, w_lower))
    for x in range(cx):
        u1 = work[1, x + 1] + c1
        u1_ref[x] = u1
        to_north[x : x + 1] = u1[cy - 1 : cy]
        to_south[x : x + 1] = u1[0:1]


def layers_kernel(field, to_a, to_b):
    odd = lax.axis_index("group") % 2 == 1
    west, east = field[0], field[field.shape[0] - 1]
    to_a[...] = jnp.where(odd, west, east)
    to_b[...] = jnp.where(odd, east, west)


def dots_kernel(source, u0_ref, image, u1_ref, out):
    r_u0 = u0_v0 = v0_u1 = r_u1 = jnp.zeros((8, LANES), jnp.float32)
    for x in range(source.shape[0]):
        r, u0, v0, u1 = source[x], u0_ref[x], image[x], u1_ref[x]
        r_u0 = r_u0 + fold(r * u0)
        u0_v0 = u0_v0 + fold(u0 * v0)
        v0_u1 = v0_u1 + fold(v0 * u1)
        r_u1 = r_u1 + fold(r * u1)
    out[...] = placed(((1, total_of(r_u0)), (2, total_of(u0_v0)), (3, total_of(v0_u1)), (4, total_of(r_u1))))


def second_kernel(
    halo_a, halo_b, halo_north, halo_south, u0_ref, u1_ref, dots, storage,
    east_t, north_t, south_t, upper_t, lower_t, edge_east, edge_west, edge_north, edge_south,
    scale, w_east, w_west, w_north, w_south, w_upper, w_lower,
    result, out, padded, image, first, work,
):
    cx = storage.shape[0]
    odd = lax.axis_index("group") % 2 == 1
    a, b = halo_a[...], halo_b[...]
    padded[0] = jnp.where(odd, a, b)
    padded[cx + 1] = jnp.where(odd, b, a)
    for x in range(cx):
        padded[x + 1] = u1_ref[x]
    inner, outer = (east_t, north_t, south_t, upper_t, lower_t), (edge_east, edge_west, edge_north, edge_south)
    apply(padded, halo_north, halo_south, storage, inner, outer, image)
    total = u1_v1 = u0_v1 = jnp.zeros((8, LANES), jnp.float32)
    for x in range(cx):
        v1 = image[x]
        s = scale[x] * v1
        first[x] = s
        work[0, x + 1] = s
        total = total + fold(v1)
        u1_v1 = u1_v1 + fold(u1_ref[x] * v1)
        u0_v1 = u0_v1 + fold(u0_ref[x] * v1)
    clear_ends(work)
    smooth(first, work, (w_east, w_west, w_north, w_south, w_upper, w_lower))
    for x in range(cx):
        result[x] = work[1, x + 1]
    out[...] = dots[...] + placed(((0, total_of(total)), (5, total_of(u1_v1)), (6, total_of(u0_v1))))


def last_kernel(steps, table, solver, u0_ref, u1_ref, result, pressure, precond):
    t = table[...]
    me = lax.axis_index("sub")
    lane = lax.broadcasted_iota(jnp.int32, t.shape, 1)
    factors = [(solver[2 * step], solver[2 * step + 1]) for step in range(steps)]
    c2 = solve_rows(factors, solver[2 * steps], t)
    c2 = total_of(jnp.where((rows_of(t.shape) == me) & (lane == 0), c2, 0.0))
    sums = jnp.sum(t, axis=0, keepdims=True)
    r_u0, u0_v0, v0_u1, r_u1, u1_v1, u0_v1 = (sums[:, at : at + 1] for at in range(1, 7))
    a0 = r_u0 / u0_v0
    rz = r_u0 - a0 * r_u1 - a0 * u0_v0 + a0 * a0 * v0_u1
    keep = 1.0 + rz / r_u0
    a1 = rz / (keep * keep * u0_v0 - keep * a0 * (u0_v1 + v0_u1) + a0 * a0 * u1_v1)
    p0 = a0 + a1 * keep
    p1 = a1 * a0
    z1 = a0 + a1 * keep
    z2 = a1 * a0
    for x in range(u0_ref.shape[0]):
        u0, u1 = u0_ref[x], u1_ref[x]
        pressure[x] = p0 * u0 - p1 * u1
        precond[x] = u0 - z1 * u1 + z2 * (result[x] + c2)


def call(body, outs, scratch, *operands, cost=0):
    space = pl.BlockSpec(memory_space=pltpu.VMEM)
    estimate = pl.CostEstimate(flops=cost, bytes_accessed=4 * cost, transcendentals=0) if cost else None
    return pl.pallas_call(
        body,
        out_shape=[jax.ShapeDtypeStruct(s, jnp.float32) for s in outs],
        in_specs=[space] * len(operands),
        out_specs=[space] * len(outs),
        scratch_shapes=[pltpu.VMEM(s, jnp.float32) for s in scratch],
        compiler_params=pltpu.CompilerParams(vmem_limit_bytes=VMEM),
        cost_estimate=estimate,
    )(*operands)


def exchange(to_a, to_b, to_north, to_south):
    groups, peers = lax.axis_size("group"), lax.axis_size("sub")
    a = lax.ppermute(to_a, "group", [(i, i ^ 1) for i in range(groups)])
    b = lax.ppermute(to_b, "group", [(i, (((i + 1) ^ 1) - 1) % groups) for i in range(groups)])
    up = [(i, (i + 1) % peers) for i in range(peers)]
    south = lax.ppermute(to_north, "sub", up)
    north = lax.ppermute(to_south, "sub", [(j, i) for i, j in up])
    return a, b, north, south


def gather(row, axis):
    peers = lax.axis_size(axis)
    return lax.all_to_all(jnp.broadcast_to(row[None], (peers, 1, LANES)), axis, 0, 0).reshape(peers, LANES)


def shards(source, perm, storage):
    cx, cy, cz = source.shape
    members = lax.axis_size("sub")
    steps = members.bit_length() - 1
    full, wide, tall, layer, edge = (cx, cy, cz), (cx + 2, cy, cz), (cy + 8, cz), (cy, cz), (cx, cz)
    row, rounds = (1, LANES), [full, (2,) + wide]
    odd = lax.axis_index("group") % 2
    to_a = lax.dynamic_index_in_dim(perm, (1 - odd) * (cx - 1), 0, keepdims=False)
    to_b = lax.dynamic_index_in_dim(perm, odd * (cx - 1), 0, keepdims=False)
    halos = exchange(to_a, to_b, perm[:, -1], perm[:, 0])
    *inner, diagonal = call(inner_kernel, [(cx + 1, cy, cz)] + [full] * 5, [], perm, storage, cost=2**21)
    (sums,) = call(sums_kernel, [row], [], source, storage, cost=2**19)
    *made, result, to_north, to_south = call(
        assemble_kernel,
        [layer, layer, edge, edge] + [full] * 8 + [edge, edge],
        rounds,
        *halos, source, perm, *inner, diagonal,
    )
    to_a, to_b, own = call(
        pack_kernel, [tall, tall, row], [], storage, sums, result, to_north, to_south, *made[:4]
    )
    shared = [storage, *inner, *made]
    halos = exchange(to_a, to_b, to_north, to_south)
    mixed = own + halos[0][cy : cy + 1, :LANES] + halos[1][cy : cy + 1, :LANES]
    mixed = jnp.where(jnp.arange(LANES)[None] < 64, mixed, halos[2][:1, :LANES] + halos[3][:1, :LANES])
    u0, image, u1, to_north, to_south, solver = call(
        functools.partial(first_kernel, steps),
        [full, full, full, edge, edge, (2 * steps + 1, members, LANES)],
        [wide] + rounds + [(2,) + edge],
        gather(mixed, "sub"), *halos, *shared, result,
    )
    to_a, to_b = call(layers_kernel, [layer, layer], [], u1)
    halos = exchange(to_a, to_b, to_north, to_south)
    (dots,) = call(dots_kernel, [row], [], source, u0, image, u1, cost=2**20)
    result, mixed = call(second_kernel, [full, row], [wide, full] + rounds, *halos, u0, u1, dots, *shared)
    by_group = gather(mixed, "group")
    over_groups = sum(by_group[i : i + 1] for i in range(by_group.shape[0]))
    mixed = jnp.where(jnp.arange(LANES)[None] == 0, mixed, over_groups)
    table = gather(mixed, "sub")
    return tuple(call(functools.partial(last_kernel, steps), [full, full], [], table, solver, u0, u1, result))


def solution(mesh):
    spec = P("group", "sub", None)
    return jax.shard_map(shards, mesh=mesh, in_specs=(spec,) * 3, out_specs=(spec,) * 2, check_vma=False)
```

```python
import functools

import jax
import jax.numpy as jnp
from jax import lax
from jax.experimental import pallas as pl
from jax.experimental.pallas import tpu as pltpu
from jax.sharding import PartitionSpec as P

OMEGA = 0.8
LANES = 128
VMEM = 16 * 2**20
UNROLL = True
AGAINST, IMAGE, STORED, COUPLING, EAST = range(5)
DOTS = 120


def harmonic(left, right):
    return 2.0 * left * right / (left + right)


def shift(value, by, axis):
    return pltpu.roll(value, by % value.shape[axis], axis)


def rows_of(shape):
    return lax.broadcasted_iota(jnp.int32, shape, 0)


def fold(value):
    total = None
    for y in range(0, value.shape[0], 8):
        for z in range(0, value.shape[1], LANES):
            tile = value[y : y + 8, z : z + LANES]
            total = tile if total is None else total + tile
    return total


def total_of(value):
    return jnp.sum(value, axis=(0, 1), keepdims=True)


def placed(totals):
    lane = lax.broadcasted_iota(jnp.int32, (1, LANES), 1)
    row = jnp.zeros((1, LANES), jnp.float32)
    for at, total in totals:
        row = jnp.where(lane == at, total, row)
    return row


def smooth(first, work, weights):
    cx = first.shape[0]
    east, west, north, south, upper, lower = weights

    def sweep(src, dst):
        def slab(x, carry):
            s = src[x + 1]
            total = (1.0 - OMEGA) * s + first[x]
            total = total + east[x] * src[x + 2] + west[x] * src[x]
            total = total + north[x] * shift(s, -1, 0) + south[x] * shift(s, 1, 0)
            total = total + upper[x] * shift(s, -1, 1) + lower[x] * shift(s, 1, 1)
            dst[x + 1] = total
            return carry

        lax.fori_loop(0, cx, slab, 0, unroll=UNROLL)

    sweep(work.at[0], work.at[1])
    sweep(work.at[1], work.at[0])
    sweep(work.at[0], work.at[1])


def clear_ends(work):
    for at in range(2):
        for end in (0, work.shape[1] - 1):
            work[at, end] = jnp.zeros(work.shape[2:], jnp.float32)


def apply(padded, north_halo, south_halo, storage, inner, edges, out):
    cx, cy = storage.shape[:2]
    east_t, north_t, south_t, upper_t, lower_t = inner
    edge_east, edge_west, edge_north, edge_south = edges

    def slab(x, carry):
        u = padded[x + 1]
        row = rows_of(u.shape)
        total = storage[x] * u
        total = total + east_t[x + 1] * (u - padded[x + 2]) + east_t[x] * (u - padded[x])
        total = total + north_t[x] * (u - shift(u, -1, 0)) + south_t[x] * (u - shift(u, 1, 0))
        total = total + upper_t[x] * (u - shift(u, -1, 1)) + lower_t[x] * (u - shift(u, 1, 1))
        one = pl.ds(x, 1)
        north = jnp.where(row == cy - 1, edge_north[one] * (u - north_halo[one]), 0.0)
        total = total + jnp.where(row == 0, edge_south[one] * (u - south_halo[one]), north)
        out[x] = total
        return carry

    lax.fori_loop(0, cx, slab, 0, unroll=UNROLL)
    out[0] = out[0] + edge_west[...] * (padded[1] - padded[0])
    out[cx - 1] = out[cx - 1] + edge_east[...] * (padded[cx] - padded[cx + 1])


def load_kernel(
    source_in, perm_in, storage_in,
    source, perm, storage, east_t, north_t, south_t, upper_t, lower_t, diagonal, sums, sems,
):
    cx, cy, cz = source.shape
    pairs = ((perm_in, perm), (storage_in, storage), (source_in, source))
    copies = [pltpu.make_async_copy(src, dst, sems.at[at]) for at, (src, dst) in enumerate(pairs)]
    for copy in copies:
        copy.start()
    row = rows_of((cy, cz))
    west = jnp.zeros((cy, cz), jnp.float32)
    east_t[0] = west
    copies[0].wait()
    copies[1].wait()
    stored = total_r = jnp.zeros((8, LANES), jnp.float32)
    for x in range(cx):
        k = perm[x]
        east = harmonic(k, perm[x + 1]) if x + 1 < cx else jnp.zeros((cy, cz), jnp.float32)
        north = jnp.where(row == cy - 1, 0.0, harmonic(k, shift(k, -1, 0)))
        south = shift(north, 1, 0)
        upper = harmonic(k, shift(k, -1, 1))
        lower = shift(upper, 1, 1)
        east_t[x + 1] = east
        north_t[x] = north
        south_t[x] = south
        upper_t[x] = upper
        lower_t[x] = lower
        diagonal[x] = storage[x] + east + west + north + south + upper + lower
        stored = stored + fold(storage[x])
        west = east
    copies[2].wait()
    for x in range(cx):
        total_r = total_r + fold(source[x])
    sums[...] = placed(((0, total_of(stored)), (2, total_of(total_r))))


def edge_kernel(perm_north, perm_south, perm, sums, edge_north, edge_south, to_a, to_b, out):
    cx, cy = perm.shape[:2]
    top = jnp.concatenate([perm[x, cy - 1 : cy] for x in range(cx)], axis=0)
    bottom = jnp.concatenate([perm[x, 0:1] for x in range(cx)], axis=0)
    north = harmonic(top, perm_north[...])
    edge_north[...] = north
    edge_south[...] = harmonic(perm_south[...], bottom)
    out[...] = sums[...] + placed(((1, total_of(north)),))
    layers_kernel(perm, to_a, to_b)


def layers_kernel(field, to_a, to_b):
    odd = lax.axis_index("group") % 2 == 1
    west, east = field[0], field[field.shape[0] - 1]
    to_a[...] = jnp.where(odd, west, east)
    to_b[...] = jnp.where(odd, east, west)


def assemble_kernel(
    perm_a, perm_b, source, perm, east_in, north_in, south_in, upper_t, lower_t, diagonal, edge_north, edge_south,
    edge_east, edge_west, scale, w_east, w_west, w_north, w_south, w_upper, w_lower, result, first, work,
):
    cx, cy, cz = source.shape
    odd = lax.axis_index("group") % 2 == 1
    row = rows_of((cy, cz))
    a, b = perm_a[...], perm_b[...]
    edge_east[...] = harmonic(perm[cx - 1], jnp.where(odd, b, a))
    edge_west[...] = harmonic(jnp.where(odd, a, b), perm[0])
    for x in range(cx):
        d = diagonal[x]
        d = d + jnp.where(row == cy - 1, edge_north[x : x + 1], jnp.where(row == 0, edge_south[x : x + 1], 0.0))
        if x == 0:
            d = d + edge_west[...]
        if x == cx - 1:
            d = d + edge_east[...]
        q = OMEGA / d
        scale[x] = q
        w_east[x] = q * east_in[x + 1]
        w_west[x] = q * east_in[x]
        w_north[x] = q * north_in[x]
        w_south[x] = q * south_in[x]
        w_upper[x] = q * upper_t[x]
        w_lower[x] = q * lower_t[x]
        s = q * source[x]
        first[x] = s
        work[0, x + 1] = s
    clear_ends(work)
    smooth(first, work, (w_east, w_west, w_north, w_south, w_upper, w_lower))
    for x in range(cx):
        result[x] = work[1, x + 1]


def reduce_rows(margin, coupling, steps):
    before, after = shift(coupling, 1, 0), coupling
    factors = []
    for step in range(steps):
        h = 2**step
        inverse = 1.0 / (margin + before + after)
        from_before = before * shift(inverse, h, 0)
        from_after = after * shift(inverse, -h, 0)
        margin = margin + from_before * shift(margin, h, 0) + from_after * shift(margin, -h, 0)
        before, after = from_before * shift(before, h, 0), from_after * shift(after, -h, 0)
        factors.append((from_before, from_after))
    return factors, 1.0 / margin


def solve_rows(factors, last, right):
    for step, (from_before, from_after) in enumerate(factors):
        h = 2**step
        right = right + from_before * shift(right, h, 0) + from_after * shift(right, -h, 0)
    return right * last


def coarse_kernel(steps, table, result, u0_ref, to_a, to_b, to_north, to_south):
    cx, cy = result.shape[:2]
    members = table.shape[0]
    t = table[...]
    factors, last = reduce_rows(t / members, shift(t, -1, 1) * members, steps)
    c0 = solve_rows(factors, last, shift(t, -2, 1))
    lane = lax.broadcasted_iota(jnp.int32, t.shape, 1)
    c0 = total_of(jnp.where((rows_of(t.shape) == lax.axis_index("sub")) & (lane == 0), c0, 0.0))
    for x in range(cx):
        u = result[x] + c0
        u0_ref[x] = u
        to_north[x : x + 1] = u[cy - 1 : cy]
        to_south[x : x + 1] = u[0:1]
    layers_kernel(u0_ref, to_a, to_b)


def fill(padded, field, halo_a, halo_b):
    odd = lax.axis_index("group") % 2 == 1
    cx = field.shape[0]
    a, b = halo_a[...], halo_b[...]
    padded[0] = jnp.where(odd, a, b)
    padded[cx + 1] = jnp.where(odd, b, a)
    for x in range(cx):
        padded[x + 1] = field[x]


def first_kernel(
    halo_a, halo_b, halo_north, halo_south, u0_ref, storage,
    east_t, north_t, south_t, upper_t, lower_t, edge_east, edge_west, edge_north, edge_south,
    scale, w_east, w_west, w_north, w_south, w_upper, w_lower,
    image, result, to_north, to_south, padded, first, work,
):
    cx, cy, cz = storage.shape
    fill(padded, u0_ref, halo_a, halo_b)
    inner, outer = (east_t, north_t, south_t, upper_t, lower_t), (edge_east, edge_west, edge_north, edge_south)
    apply(padded, halo_north, halo_south, storage, inner, outer, image)
    for x in range(cx):
        s = scale[x] * image[x]
        first[x] = s
        work[0, x + 1] = s
    clear_ends(work)
    smooth(first, work, (w_east, w_west, w_north, w_south, w_upper, w_lower))
    for x in range(cx):
        f1 = work[1, x + 1]
        result[x] = f1
        to_north[x : x + 1] = f1[cy - 1 : cy]
        to_south[x : x + 1] = f1[0:1]


def dots_kernel(groups, source, u0_ref, image, f1_ref, edge_east, edge_north, sums, out):
    r_u0 = u0_v0 = v0_f1 = total = jnp.zeros((8, LANES), jnp.float32)
    for x in range(source.shape[0]):
        r, u0, v0, f1 = source[x], u0_ref[x], image[x], f1_ref[x]
        r_u0 = r_u0 + fold(r * u0)
        u0_v0 = u0_v0 + fold(u0 * v0)
        v0_f1 = v0_f1 + fold(v0 * f1)
        total = total + fold(v0)
    me = lax.axis_index("group")
    totals = (
        (AGAINST * groups + me, total_of(total)),
        (STORED * groups + me, sums[0:1, 0:1]),
        (COUPLING * groups + me, total_of(edge_north[...])),
        (EAST * groups + me, total_of(fold(edge_east[...]))),
        (DOTS, total_of(r_u0)),
        (DOTS + 1, total_of(u0_v0)),
        (DOTS + 2, total_of(v0_f1)),
    )
    out[...] = placed(totals)


def second_kernel(
    groups, halo_a, halo_b, halo_north, halo_south, f1_ref, dots, storage,
    east_t, north_t, south_t, upper_t, lower_t, edge_east, edge_west, edge_north, edge_south,
    image, out, padded,
):
    fill(padded, f1_ref, halo_a, halo_b)
    inner, outer = (east_t, north_t, south_t, upper_t, lower_t), (edge_east, edge_west, edge_north, edge_south)
    apply(padded, halo_north, halo_south, storage, inner, outer, image)
    total = f1_g1 = jnp.zeros((8, LANES), jnp.float32)
    for x in range(storage.shape[0]):
        g1 = image[x]
        total = total + fold(g1)
        f1_g1 = f1_g1 + fold(f1_ref[x] * g1)
    me = lax.axis_index("group")
    out[...] = dots[...] + placed(((IMAGE * groups + me, total_of(total)), (DOTS + 3, total_of(f1_g1))))


def last_kernel(
    steps, groups, table, u0_ref, f1_ref, image, storage, edge_east, edge_west, edge_north, edge_south,
    scale, w_east, w_west, w_north, w_south, w_upper, w_lower, pressure, precond, first, work,
):
    cx, cy, cz = storage.shape
    t = table[...]
    members = t.shape[0]
    lane = lax.broadcasted_iota(jnp.int32, t.shape, 1)
    mine = (rows_of(t.shape) == lax.axis_index("sub")) & (lane == lax.axis_index("group"))

    def column(at):
        return shift(t, -at * groups, 1)

    def pick(value):
        return total_of(jnp.where(mine, value, 0.0))

    def to_the_east(value):
        return jnp.where(lane == groups - 1, shift(value, groups - 1, 1), shift(value, -1, 1))

    def to_the_west(value):
        return jnp.where(lane == 0, shift(value, 1 - groups, 1), shift(value, 1, 1))

    against, image_sum, stored, after, right = (column(at) for at in (AGAINST, IMAGE, STORED, COUPLING, EAST))
    factors, last = reduce_rows(stored / members, after * members, steps)
    c1 = solve_rows(factors, last, against)
    c_east, c_west, c_north, c_south = to_the_east(c1), to_the_west(c1), shift(c1, -1, 0), shift(c1, 1, 0)
    coupled = (
        stored * c1 + after * (c1 - c_north) + shift(after, 1, 0) * (c1 - c_south)
        + right * (c1 - c_east) + to_the_west(right) * (c1 - c_west)
    )
    c2 = solve_rows(factors, last, image_sum + coupled)
    valid = lane < groups
    sums = jnp.sum(t, axis=0, keepdims=True)
    r_u0, u0_v0, v0_u1, u1_v1 = (sums[:, DOTS + at : DOTS + at + 1] for at in range(4))
    v0_u1 = v0_u1 + total_of(jnp.where(valid, c1 * against, 0.0))
    u1_v1 = u1_v1 + total_of(jnp.where(valid, c1 * (2.0 * image_sum + coupled), 0.0))
    c1, c_east, c_west, c_north, c_south, c2 = (pick(c) for c in (c1, c_east, c_west, c_north, c_south, c2))

    row = rows_of((cy, cz))
    for x in range(cx):
        one = slice(x, x + 1)
        edge = jnp.where(row == 0, edge_south[one] * (c1 - c_south), 0.0)
        edge = jnp.where(row == cy - 1, edge_north[one] * (c1 - c_north), edge)
        v1 = image[x] + storage[x] * c1 + edge
        if x == 0:
            v1 = v1 + edge_west[...] * (c1 - c_west)
        if x == cx - 1:
            v1 = v1 + edge_east[...] * (c1 - c_east)
        s = scale[x] * v1
        first[x] = s
        work[0, x + 1] = s
    clear_ends(work)
    smooth(first, work, (w_east, w_west, w_north, w_south, w_upper, w_lower))

    a0 = r_u0 / u0_v0
    rz = a0 * a0 * v0_u1 - r_u0
    keep = 1.0 + rz / r_u0
    a1 = rz / (keep * keep * u0_v0 - 2.0 * keep * a0 * v0_u1 + a0 * a0 * u1_v1)
    p0, p1, z2 = a0 + a1 * keep, a1 * a0, a1 * a0
    for x in range(cx):
        u0, u1 = u0_ref[x], f1_ref[x] + c1
        pressure[x] = p0 * u0 - p1 * u1
        precond[x] = u0 - p0 * u1 + z2 * (work[1, x + 1] + c2)


def call(body, outs, scratch, *operands, cost=0, hbm=False):
    space = pl.BlockSpec(memory_space=pltpu.VMEM)
    return pl.pallas_call(
        body,
        out_shape=[jax.ShapeDtypeStruct(s, jnp.float32) for s in outs],
        in_specs=[pl.BlockSpec(memory_space=pl.ANY) if hbm else space] * len(operands),
        out_specs=[space] * len(outs),
        scratch_shapes=[pltpu.VMEM(s, jnp.float32) if isinstance(s, tuple) else s for s in scratch],
        compiler_params=pltpu.CompilerParams(vmem_limit_bytes=VMEM),
        cost_estimate=pl.CostEstimate(flops=cost, bytes_accessed=4 * cost, transcendentals=0) if cost else None,
    )(*operands)


def over_group(to_a, to_b):
    groups = lax.axis_size("group")
    a = lax.ppermute(to_a, "group", [(i, i ^ 1) for i in range(groups)])
    b = lax.ppermute(to_b, "group", [(i, (((i + 1) ^ 1) - 1) % groups) for i in range(groups)])
    return a, b


def over_sub(to_north, to_south):
    peers = lax.axis_size("sub")
    up = [(i, (i + 1) % peers) for i in range(peers)]
    south = lax.ppermute(to_north, "sub", up)
    north = lax.ppermute(to_south, "sub", [(j, i) for i, j in up])
    return north, south


def gather(row, axis):
    peers = lax.axis_size(axis)
    return lax.all_to_all(jnp.broadcast_to(row[None], (peers, 1, LANES)), axis, 0, 0).reshape(peers, LANES)


def shards(source, perm, storage):
    cx, cy, cz = source.shape
    groups, members = lax.axis_size("group"), lax.axis_size("sub")
    steps = members.bit_length() - 1
    full, wide, layer, edge, row = (cx, cy, cz), (cx + 2, cy, cz), (cy, cz), (cx, cz), (1, LANES)
    rounds = [full, (2,) + wide]
    halos = over_sub(perm[:, -1], perm[:, 0])
    source, perm, storage, *inner, diagonal, sums = call(
        load_kernel,
        [full] * 3 + [(cx + 1, cy, cz)] + [full] * 5 + [row],
        [pltpu.SemaphoreType.DMA((3,))],
        source, perm, storage, cost=2**21, hbm=True,
    )
    edge_north, edge_south, to_a, to_b, scalars = call(
        edge_kernel, [edge, edge, layer, layer, row], [], *halos, perm, sums
    )
    table = gather(scalars, "sub")
    edge_east, edge_west, *weights, result = call(
        assemble_kernel,
        [layer, layer] + [full] * 8,
        rounds,
        *over_group(to_a, to_b), source, perm, *inner, diagonal, edge_north, edge_south, cost=2**21,
    )
    outer = [edge_east, edge_west, edge_north, edge_south]
    u0, to_a, to_b, to_north, to_south = call(
        functools.partial(coarse_kernel, steps), [full, layer, layer, edge, edge], [], table, result
    )
    halos = over_group(to_a, to_b) + over_sub(to_north, to_south)
    v0, f1, to_north, to_south = call(
        first_kernel, [full, full, edge, edge], [wide] + rounds, *halos, u0, storage, *inner, *outer, *weights
    )
    to_a, to_b = call(layers_kernel, [layer, layer], [], f1)
    halos = over_group(to_a, to_b) + over_sub(to_north, to_south)
    (dots,) = call(
        functools.partial(dots_kernel, groups), [row], [],
        source, u0, v0, f1, edge_east, edge_north, sums, cost=2**20,
    )
    g1, scalars = call(
        functools.partial(second_kernel, groups), [full, row], [wide], *halos, f1, dots, storage, *inner, *outer
    )
    by_group = gather(scalars, "group")
    table = gather(sum(by_group[i : i + 1] for i in range(groups)), "sub")
    return tuple(
        call(
            functools.partial(last_kernel, steps, groups),
            [full, full],
            rounds,
            table, u0, f1, g1, storage, *outer, *weights,
        )
    )


def solution(mesh):
    spec = P("group", "sub", None)
    return jax.shard_map(shards, mesh=mesh, in_specs=(spec,) * 3, out_specs=(spec,) * 2, check_vma=False)
```

```python
import functools

import jax
import jax.numpy as jnp
from jax import lax
from jax.experimental import pallas as pl
from jax.experimental.pallas import tpu as pltpu
from jax.sharding import PartitionSpec as P

OMEGA = 0.8
LANES = 128
VMEM = 16 * 2**20
UNROLL = True
AGAINST, IMAGE, STORED, COUPLING, EAST = range(5)
DOTS = 120


def harmonic(left, right):
    return 2.0 * left * right / (left + right)


def shift(value, by, axis):
    return pltpu.roll(value, by % value.shape[axis], axis)


def rows_of(shape):
    return lax.broadcasted_iota(jnp.int32, shape, 0)


def fold(value):
    total = None
    for y in range(0, value.shape[0], 8):
        for z in range(0, value.shape[1], LANES):
            tile = value[y : y + 8, z : z + LANES]
            total = tile if total is None else total + tile
    return total


def total_of(value):
    return jnp.sum(value, axis=(0, 1), keepdims=True)


def placed(totals):
    lane = lax.broadcasted_iota(jnp.int32, (1, LANES), 1)
    row = jnp.zeros((1, LANES), jnp.float32)
    for at, total in totals:
        row = jnp.where(lane == at, total, row)
    return row


def smooth(first, work, weights):
    cx = first.shape[0]
    east, west, north, south, upper, lower = weights

    def sweep(src, dst):
        def slab(x, carry):
            s = src[x + 1]
            total = (1.0 - OMEGA) * s + first[x]
            total = total + east[x] * src[x + 2] + west[x] * src[x]
            total = total + north[x] * shift(s, -1, 0) + south[x] * shift(s, 1, 0)
            total = total + upper[x] * shift(s, -1, 1) + lower[x] * shift(s, 1, 1)
            dst[x + 1] = total
            return carry

        lax.fori_loop(0, cx, slab, 0, unroll=UNROLL)

    sweep(work.at[0], work.at[1])
    sweep(work.at[1], work.at[0])
    sweep(work.at[0], work.at[1])


def clear_ends(work):
    for at in range(2):
        for end in (0, work.shape[1] - 1):
            work[at, end] = jnp.zeros(work.shape[2:], jnp.float32)


def apply(padded, north_halo, south_halo, storage, inner, edges, out):
    cx, cy = storage.shape[:2]
    east_t, north_t, south_t, upper_t, lower_t = inner
    edge_east, edge_west, edge_north, edge_south = edges

    def slab(x, carry):
        u = padded[x + 1]
        row = rows_of(u.shape)
        total = storage[x] * u
        total = total + east_t[x + 1] * (u - padded[x + 2]) + east_t[x] * (u - padded[x])
        total = total + north_t[x] * (u - shift(u, -1, 0)) + south_t[x] * (u - shift(u, 1, 0))
        total = total + upper_t[x] * (u - shift(u, -1, 1)) + lower_t[x] * (u - shift(u, 1, 1))
        one = pl.ds(x, 1)
        north = jnp.where(row == cy - 1, edge_north[one] * (u - north_halo[one]), 0.0)
        total = total + jnp.where(row == 0, edge_south[one] * (u - south_halo[one]), north)
        out[x] = total
        return carry

    lax.fori_loop(0, cx, slab, 0, unroll=UNROLL)
    out[0] = out[0] + edge_west[...] * (padded[1] - padded[0])
    out[cx - 1] = out[cx - 1] + edge_east[...] * (padded[cx] - padded[cx + 1])


def inner_kernel(
    source, perm, storage,
    source_out, storage_out, west_out, east_out, east_t, north_t, south_t, upper_t, lower_t, diagonal, sums,
):
    cx, cy, cz = source.shape
    west_out[...] = perm[0]
    east_out[...] = perm[cx - 1]
    row = rows_of((cy, cz))
    west = jnp.zeros((cy, cz), jnp.float32)
    east_t[0] = west
    stored = total_r = jnp.zeros((8, LANES), jnp.float32)
    for x in range(cx):
        k = perm[x]
        east = harmonic(k, perm[x + 1]) if x + 1 < cx else jnp.zeros((cy, cz), jnp.float32)
        north = jnp.where(row == cy - 1, 0.0, harmonic(k, shift(k, -1, 0)))
        south = shift(north, 1, 0)
        upper = harmonic(k, shift(k, -1, 1))
        lower = shift(upper, 1, 1)
        east_t[x + 1] = east
        north_t[x] = north
        south_t[x] = south
        upper_t[x] = upper
        lower_t[x] = lower
        w, r = storage[x], source[x]
        diagonal[x] = w + east + west + north + south + upper + lower
        storage_out[x] = w
        source_out[x] = r
        stored = stored + fold(w)
        total_r = total_r + fold(r)
        west = east
    sums[...] = placed(((0, total_of(stored)), (2, total_of(total_r))))


def edge_kernel(
    perm_north, perm_south, strip_north, strip_south, west, east, sums, edge_north, edge_south, to_a, to_b, out
):
    north = harmonic(strip_north[...], perm_north[...])
    edge_north[...] = north
    edge_south[...] = harmonic(perm_south[...], strip_south[...])
    out[...] = jnp.broadcast_to(sums[...] + placed(((1, total_of(north)),)), out.shape)
    by_side(west[...], east[...], to_a, to_b)


def by_side(west, east, to_a, to_b):
    odd = lax.axis_index("group") % 2 == 1
    to_a[...] = jnp.where(odd, west, east)
    to_b[...] = jnp.where(odd, east, west)


def layers_kernel(field, to_a, to_b):
    by_side(field[0], field[field.shape[0] - 1], to_a, to_b)


def reduce_rows(margin, coupling, steps):
    before, after = shift(coupling, 1, 0), coupling
    factors = []
    for step in range(steps):
        h = 2**step
        inverse = 1.0 / (margin + before + after)
        from_before = before * shift(inverse, h, 0)
        from_after = after * shift(inverse, -h, 0)
        margin = margin + from_before * shift(margin, h, 0) + from_after * shift(margin, -h, 0)
        before, after = from_before * shift(before, h, 0), from_after * shift(after, -h, 0)
        factors.append((from_before, from_after))
    return factors, 1.0 / margin


def solve_rows(factors, last, right):
    for step, (from_before, from_after) in enumerate(factors):
        h = 2**step
        right = right + from_before * shift(right, h, 0) + from_after * shift(right, -h, 0)
    return right * last


def assemble_kernel(
    steps, perm_a, perm_b, table, source, perm_west, perm_east,
    east_in, north_in, south_in, upper_t, lower_t, diagonal, edge_north, edge_south,
    edge_east, edge_west, scale, w_east, w_west, w_north, w_south, w_upper, w_lower,
    u0_ref, to_a, to_b, to_north, to_south, first, work,
):
    cx, cy, cz = source.shape
    odd = lax.axis_index("group") % 2 == 1
    row = rows_of((cy, cz))
    a, b = perm_a[...], perm_b[...]
    edge_east[...] = harmonic(perm_east[...], jnp.where(odd, b, a))
    edge_west[...] = harmonic(jnp.where(odd, a, b), perm_west[...])
    for x in range(cx):
        d = diagonal[x]
        d = d + jnp.where(row == cy - 1, edge_north[x : x + 1], jnp.where(row == 0, edge_south[x : x + 1], 0.0))
        if x == 0:
            d = d + edge_west[...]
        if x == cx - 1:
            d = d + edge_east[...]
        q = OMEGA / d
        scale[x] = q
        w_east[x] = q * east_in[x + 1]
        w_west[x] = q * east_in[x]
        w_north[x] = q * north_in[x]
        w_south[x] = q * south_in[x]
        w_upper[x] = q * upper_t[x]
        w_lower[x] = q * lower_t[x]
        s = q * source[x]
        first[x] = s
        work[0, x + 1] = s
    clear_ends(work)
    smooth(first, work, (w_east, w_west, w_north, w_south, w_upper, w_lower))

    t = table[...]
    members = t.shape[0]
    factors, last = reduce_rows(t / members, shift(t, -1, 1) * members, steps)
    c0 = solve_rows(factors, last, shift(t, -2, 1))
    lane = lax.broadcasted_iota(jnp.int32, t.shape, 1)
    c0 = total_of(jnp.where((rows_of(t.shape) == lax.axis_index("sub")) & (lane == 0), c0, 0.0))
    for x in range(cx):
        u = work[1, x + 1] + c0
        u0_ref[x] = u
        to_north[x : x + 1] = u[cy - 1 : cy]
        to_south[x : x + 1] = u[0:1]
    layers_kernel(u0_ref, to_a, to_b)


def fill(padded, field, halo_a, halo_b):
    odd = lax.axis_index("group") % 2 == 1
    cx = field.shape[0]
    a, b = halo_a[...], halo_b[...]
    padded[0] = jnp.where(odd, a, b)
    padded[cx + 1] = jnp.where(odd, b, a)
    for x in range(cx):
        padded[x + 1] = field[x]


def first_kernel(
    halo_a, halo_b, halo_north, halo_south, u0_ref, storage,
    east_t, north_t, south_t, upper_t, lower_t, edge_east, edge_west, edge_north, edge_south,
    scale, w_east, w_west, w_north, w_south, w_upper, w_lower,
    image, result, to_north, to_south, padded, first, work,
):
    cx, cy, cz = storage.shape
    fill(padded, u0_ref, halo_a, halo_b)
    inner, outer = (east_t, north_t, south_t, upper_t, lower_t), (edge_east, edge_west, edge_north, edge_south)
    apply(padded, halo_north, halo_south, storage, inner, outer, image)
    for x in range(cx):
        s = scale[x] * image[x]
        first[x] = s
        work[0, x + 1] = s
    clear_ends(work)
    smooth(first, work, (w_east, w_west, w_north, w_south, w_upper, w_lower))
    for x in range(cx):
        f1 = work[1, x + 1]
        result[x] = f1
        to_north[x : x + 1] = f1[cy - 1 : cy]
        to_south[x : x + 1] = f1[0:1]


def dots_kernel(groups, source, u0_ref, image, f1_ref, edge_east, edge_north, sums, out):
    r_u0 = u0_v0 = v0_f1 = total = jnp.zeros((8, LANES), jnp.float32)
    for x in range(source.shape[0]):
        r, u0, v0, f1 = source[x], u0_ref[x], image[x], f1_ref[x]
        r_u0 = r_u0 + fold(r * u0)
        u0_v0 = u0_v0 + fold(u0 * v0)
        v0_f1 = v0_f1 + fold(v0 * f1)
        total = total + fold(v0)
    me = lax.axis_index("group")
    totals = (
        (AGAINST * groups + me, total_of(total)),
        (STORED * groups + me, sums[0:1, 0:1]),
        (COUPLING * groups + me, total_of(edge_north[...])),
        (EAST * groups + me, total_of(fold(edge_east[...]))),
        (DOTS, total_of(r_u0)),
        (DOTS + 1, total_of(u0_v0)),
        (DOTS + 2, total_of(v0_f1)),
    )
    out[...] = placed(totals)


def second_kernel(
    groups, halo_a, halo_b, halo_north, halo_south, f1_ref, dots, storage,
    east_t, north_t, south_t, upper_t, lower_t, edge_east, edge_west, edge_north, edge_south,
    image, out, padded,
):
    fill(padded, f1_ref, halo_a, halo_b)
    inner, outer = (east_t, north_t, south_t, upper_t, lower_t), (edge_east, edge_west, edge_north, edge_south)
    apply(padded, halo_north, halo_south, storage, inner, outer, image)
    total = f1_g1 = jnp.zeros((8, LANES), jnp.float32)
    for x in range(storage.shape[0]):
        g1 = image[x]
        total = total + fold(g1)
        f1_g1 = f1_g1 + fold(f1_ref[x] * g1)
    me = lax.axis_index("group")
    out[...] = dots[...] + placed(((IMAGE * groups + me, total_of(total)), (DOTS + 3, total_of(f1_g1))))


def last_kernel(
    steps, groups, table, u0_ref, f1_ref, image, storage, edge_east, edge_west, edge_north, edge_south,
    scale, w_east, w_west, w_north, w_south, w_upper, w_lower, pressure, precond, first, work,
):
    cx, cy, cz = storage.shape
    t = table[...]
    members = t.shape[0]
    lane = lax.broadcasted_iota(jnp.int32, t.shape, 1)
    mine = (rows_of(t.shape) == lax.axis_index("sub")) & (lane == lax.axis_index("group"))

    def column(at):
        return shift(t, -at * groups, 1)

    def pick(value):
        return total_of(jnp.where(mine, value, 0.0))

    def to_the_east(value):
        return jnp.where(lane == groups - 1, shift(value, groups - 1, 1), shift(value, -1, 1))

    def to_the_west(value):
        return jnp.where(lane == 0, shift(value, 1 - groups, 1), shift(value, 1, 1))

    against, image_sum, stored, after, right = (column(at) for at in (AGAINST, IMAGE, STORED, COUPLING, EAST))
    factors, last = reduce_rows(stored / members, after * members, steps)
    c1 = solve_rows(factors, last, against)
    c_east, c_west, c_north, c_south = to_the_east(c1), to_the_west(c1), shift(c1, -1, 0), shift(c1, 1, 0)
    coupled = (
        stored * c1 + after * (c1 - c_north) + shift(after, 1, 0) * (c1 - c_south)
        + right * (c1 - c_east) + to_the_west(right) * (c1 - c_west)
    )
    c2 = solve_rows(factors, last, image_sum + coupled)
    valid = lane < groups
    sums = jnp.sum(t, axis=0, keepdims=True)
    r_u0, u0_v0, v0_u1, u1_v1 = (sums[:, DOTS + at : DOTS + at + 1] for at in range(4))
    v0_u1 = v0_u1 + total_of(jnp.where(valid, c1 * against, 0.0))
    u1_v1 = u1_v1 + total_of(jnp.where(valid, c1 * (2.0 * image_sum + coupled), 0.0))
    c1, c_east, c_west, c_north, c_south, c2 = (pick(c) for c in (c1, c_east, c_west, c_north, c_south, c2))

    row = rows_of((cy, cz))
    for x in range(cx):
        one = slice(x, x + 1)
        edge = jnp.where(row == 0, edge_south[one] * (c1 - c_south), 0.0)
        edge = jnp.where(row == cy - 1, edge_north[one] * (c1 - c_north), edge)
        v1 = image[x] + storage[x] * c1 + edge
        if x == 0:
            v1 = v1 + edge_west[...] * (c1 - c_west)
        if x == cx - 1:
            v1 = v1 + edge_east[...] * (c1 - c_east)
        s = scale[x] * v1
        first[x] = s
        work[0, x + 1] = s
    clear_ends(work)
    smooth(first, work, (w_east, w_west, w_north, w_south, w_upper, w_lower))

    a0 = r_u0 / u0_v0
    rz = a0 * a0 * v0_u1 - r_u0
    keep = 1.0 + rz / r_u0
    a1 = rz / (keep * keep * u0_v0 - 2.0 * keep * a0 * v0_u1 + a0 * a0 * u1_v1)
    p0, p1, z2 = a0 + a1 * keep, a1 * a0, a1 * a0
    for x in range(cx):
        u0, u1 = u0_ref[x], f1_ref[x] + c1
        pressure[x] = p0 * u0 - p1 * u1
        precond[x] = u0 - p0 * u1 + z2 * (work[1, x + 1] + c2)


def call(body, outs, scratch, *operands, cost=0):
    space = pl.BlockSpec(memory_space=pltpu.VMEM)
    return pl.pallas_call(
        body,
        out_shape=[jax.ShapeDtypeStruct(s, jnp.float32) for s in outs],
        in_specs=[space] * len(operands),
        out_specs=[space] * len(outs),
        scratch_shapes=[pltpu.VMEM(s, jnp.float32) for s in scratch],
        compiler_params=pltpu.CompilerParams(vmem_limit_bytes=VMEM),
        cost_estimate=pl.CostEstimate(flops=cost, bytes_accessed=4 * cost, transcendentals=0) if cost else None,
    )(*operands)


def over_group(to_a, to_b):
    groups = lax.axis_size("group")
    a = lax.ppermute(to_a, "group", [(i, i ^ 1) for i in range(groups)])
    b = lax.ppermute(to_b, "group", [(i, (((i + 1) ^ 1) - 1) % groups) for i in range(groups)])
    return a, b


def over_sub(to_north, to_south):
    peers = lax.axis_size("sub")
    up = [(i, (i + 1) % peers) for i in range(peers)]
    south = lax.ppermute(to_north, "sub", up)
    north = lax.ppermute(to_south, "sub", [(j, i) for i, j in up])
    return north, south


def gather(row, axis):
    peers = lax.axis_size(axis)
    rows = jnp.broadcast_to(row, (peers, LANES)).reshape(peers, 1, LANES)
    return lax.all_to_all(rows, axis, 0, 0).reshape(peers, LANES)


def shards(source, perm, storage):
    cx, cy, cz = source.shape
    groups, members = lax.axis_size("group"), lax.axis_size("sub")
    steps = members.bit_length() - 1
    full, wide, layer, edge, row = (cx, cy, cz), (cx + 2, cy, cz), (cy, cz), (cx, cz), (1, LANES)
    rounds = [full, (2,) + wide]
    strip_north, strip_south = perm[:, -1], perm[:, 0]
    halos = over_sub(strip_north, strip_south)
    source, storage, west, east, *inner, diagonal, sums = call(
        inner_kernel,
        [full, full, layer, layer, (cx + 1, cy, cz)] + [full] * 5 + [row],
        [],
        source, perm, storage, cost=2**21,
    )
    edge_north, edge_south, to_a, to_b, scalars = call(
        edge_kernel,
        [edge, edge, layer, layer, (members, LANES)],
        [],
        *halos, strip_north, strip_south, west, east, sums,
    )
    table = gather(scalars, "sub")
    edge_east, edge_west, *weights, u0, to_a, to_b, to_north, to_south = call(
        functools.partial(assemble_kernel, steps),
        [layer, layer] + [full] * 8 + [layer, layer, edge, edge],
        rounds,
        *over_group(to_a, to_b), table, source, west, east, *inner, diagonal, edge_north, edge_south,
    )
    outer = [edge_east, edge_west, edge_north, edge_south]
    halos = over_group(to_a, to_b) + over_sub(to_north, to_south)
    v0, f1, to_north, to_south = call(
        first_kernel, [full, full, edge, edge], [wide] + rounds, *halos, u0, storage, *inner, *outer, *weights
    )
    to_a, to_b = call(layers_kernel, [layer, layer], [], f1)
    halos = over_group(to_a, to_b) + over_sub(to_north, to_south)
    (dots,) = call(
        functools.partial(dots_kernel, groups), [row], [],
        source, u0, v0, f1, edge_east, edge_north, sums, cost=2**20,
    )
    g1, scalars = call(
        functools.partial(second_kernel, groups), [full, row], [wide], *halos, f1, dots, storage, *inner, *outer
    )
    by_group = gather(scalars, "group")
    table = gather(sum(by_group[i : i + 1] for i in range(groups)), "sub")
    return tuple(
        call(
            functools.partial(last_kernel, steps, groups),
            [full, full],
            rounds,
            table, u0, f1, g1, storage, *outer, *weights,
        )
    )


def solution(mesh):
    spec = P("group", "sub", None)
    return jax.shard_map(shards, mesh=mesh, in_specs=(spec,) * 3, out_specs=(spec,) * 2, check_vma=False)
```

```python
import functools

import jax
import jax.numpy as jnp
from jax import lax
from jax.experimental import pallas as pl
from jax.experimental.pallas import tpu as pltpu
from jax.sharding import PartitionSpec as P

OMEGA = 0.8
LANES = 128
VMEM = 16 * 2**20
UNROLL = True
SUB = ("z", "core")
AGAINST, IMAGE, STORED, COUPLING, EAST = range(5)
DOTS = 120


def harmonic(left, right):
    return 2.0 * left * right / (left + right)


def shift(value, by, axis):
    return pltpu.roll(value, by % value.shape[axis], axis)


def my_sub():
    return lax.axis_index("z") * lax.axis_size("core") + lax.axis_index("core")


def rows_of(shape):
    return lax.broadcasted_iota(jnp.int32, shape, 0)


def fold(value):
    total = None
    for y in range(0, value.shape[0], 8):
        for z in range(0, value.shape[1], LANES):
            tile = value[y : y + 8, z : z + LANES]
            total = tile if total is None else total + tile
    return total


def total_of(value):
    return jnp.sum(value, axis=(0, 1), keepdims=True)


def placed(totals):
    lane = lax.broadcasted_iota(jnp.int32, (1, LANES), 1)
    row = jnp.zeros((1, LANES), jnp.float32)
    for at, total in totals:
        row = jnp.where(lane == at, total, row)
    return row


def smooth(first, work, weights):
    cx = first.shape[0]
    east, west, north, south, upper, lower = weights

    def sweep(src, dst):
        def slab(x, carry):
            s = src[x + 1]
            total = (1.0 - OMEGA) * s + first[x]
            total = total + east[x] * src[x + 2] + west[x] * src[x]
            total = total + north[x] * shift(s, -1, 0) + south[x] * shift(s, 1, 0)
            total = total + upper[x] * shift(s, -1, 1) + lower[x] * shift(s, 1, 1)
            dst[x + 1] = total
            return carry

        lax.fori_loop(0, cx, slab, 0, unroll=UNROLL)

    sweep(work.at[0], work.at[1])
    sweep(work.at[1], work.at[0])
    sweep(work.at[0], work.at[1])


def clear_ends(work):
    for at in range(2):
        for end in (0, work.shape[1] - 1):
            work[at, end] = jnp.zeros(work.shape[2:], jnp.float32)


def apply(padded, north_halo, south_halo, storage, inner, edges, out):
    cx, cy = storage.shape[:2]
    east_t, north_t, south_t, upper_t, lower_t = inner
    edge_east, edge_west, edge_north, edge_south = edges

    def slab(x, carry):
        u = padded[x + 1]
        row = rows_of(u.shape)
        total = storage[x] * u
        total = total + east_t[x + 1] * (u - padded[x + 2]) + east_t[x] * (u - padded[x])
        total = total + north_t[x] * (u - shift(u, -1, 0)) + south_t[x] * (u - shift(u, 1, 0))
        total = total + upper_t[x] * (u - shift(u, -1, 1)) + lower_t[x] * (u - shift(u, 1, 1))
        one = pl.ds(x, 1)
        north = jnp.where(row == cy - 1, edge_north[one] * (u - north_halo[one]), 0.0)
        total = total + jnp.where(row == 0, edge_south[one] * (u - south_halo[one]), north)
        out[x] = total
        return carry

    lax.fori_loop(0, cx, slab, 0, unroll=UNROLL)
    out[0] = out[0] + edge_west[...] * (padded[1] - padded[0])
    out[cx - 1] = out[cx - 1] + edge_east[...] * (padded[cx] - padded[cx + 1])


def inner_kernel(
    source, perm, storage,
    source_out, storage_out, west_out, east_out, east_t, north_t, south_t, upper_t, lower_t, diagonal, sums,
):
    cx, cy, cz = source.shape
    west_out[...] = perm[0]
    east_out[...] = perm[cx - 1]
    row = rows_of((cy, cz))
    west = jnp.zeros((cy, cz), jnp.float32)
    east_t[0] = west
    stored = total_r = jnp.zeros((8, LANES), jnp.float32)
    for x in range(cx):
        k = perm[x]
        east = harmonic(k, perm[x + 1]) if x + 1 < cx else jnp.zeros((cy, cz), jnp.float32)
        north = jnp.where(row == cy - 1, 0.0, harmonic(k, shift(k, -1, 0)))
        south = shift(north, 1, 0)
        upper = harmonic(k, shift(k, -1, 1))
        lower = shift(upper, 1, 1)
        east_t[x + 1] = east
        north_t[x] = north
        south_t[x] = south
        upper_t[x] = upper
        lower_t[x] = lower
        w, r = storage[x], source[x]
        diagonal[x] = w + east + west + north + south + upper + lower
        storage_out[x] = w
        source_out[x] = r
        stored = stored + fold(w)
        total_r = total_r + fold(r)
        west = east
    sums[...] = placed(((0, total_of(stored)), (2, total_of(total_r))))


def edge_kernel(
    perm_north, perm_south, strip_north, strip_south, west, east, sums, edge_north, edge_south, to_a, to_b, out
):
    north = harmonic(strip_north[...], perm_north[...])
    edge_north[...] = north
    edge_south[...] = harmonic(perm_south[...], strip_south[...])
    out[...] = jnp.broadcast_to(sums[...] + placed(((1, total_of(north)),)), out.shape)
    by_side(west[...], east[...], to_a, to_b)


def by_side(west, east, to_a, to_b):
    odd = lax.axis_index("group") % 2 == 1
    to_a[...] = jnp.where(odd, east, west)
    to_b[...] = jnp.where(odd, west, east)


def layers_kernel(field, to_a, to_b):
    by_side(field[0], field[field.shape[0] - 1], to_a, to_b)


def reduce_rows(margin, coupling, steps):
    before, after = shift(coupling, 1, 0), coupling
    factors = []
    for step in range(steps):
        h = 2**step
        inverse = 1.0 / (margin + before + after)
        from_before = before * shift(inverse, h, 0)
        from_after = after * shift(inverse, -h, 0)
        margin = margin + from_before * shift(margin, h, 0) + from_after * shift(margin, -h, 0)
        before, after = from_before * shift(before, h, 0), from_after * shift(after, -h, 0)
        factors.append((from_before, from_after))
    return factors, 1.0 / margin


def solve_rows(factors, last, right):
    for step, (from_before, from_after) in enumerate(factors):
        h = 2**step
        right = right + from_before * shift(right, h, 0) + from_after * shift(right, -h, 0)
    return right * last


def assemble_kernel(
    steps, perm_a, perm_b, table, source, perm_west, perm_east,
    east_in, north_in, south_in, upper_t, lower_t, diagonal, edge_north, edge_south,
    edge_east, edge_west, scale, w_east, w_west, w_north, w_south, w_upper, w_lower,
    u0_ref, to_a, to_b, to_north, to_south, first, work,
):
    cx, cy, cz = source.shape
    odd = lax.axis_index("group") % 2 == 1
    row = rows_of((cy, cz))
    a, b = perm_a[...], perm_b[...]
    edge_east[...] = harmonic(perm_east[...], jnp.where(odd, a, b))
    edge_west[...] = harmonic(jnp.where(odd, b, a), perm_west[...])
    for x in range(cx):
        d = diagonal[x]
        d = d + jnp.where(row == cy - 1, edge_north[x : x + 1], jnp.where(row == 0, edge_south[x : x + 1], 0.0))
        if x == 0:
            d = d + edge_west[...]
        if x == cx - 1:
            d = d + edge_east[...]
        q = OMEGA / d
        scale[x] = q
        w_east[x] = q * east_in[x + 1]
        w_west[x] = q * east_in[x]
        w_north[x] = q * north_in[x]
        w_south[x] = q * south_in[x]
        w_upper[x] = q * upper_t[x]
        w_lower[x] = q * lower_t[x]
        s = q * source[x]
        first[x] = s
        work[0, x + 1] = s
    clear_ends(work)
    smooth(first, work, (w_east, w_west, w_north, w_south, w_upper, w_lower))

    t = table[...]
    members = t.shape[0]
    factors, last = reduce_rows(t / members, shift(t, -1, 1) * members, steps)
    c0 = solve_rows(factors, last, shift(t, -2, 1))
    lane = lax.broadcasted_iota(jnp.int32, t.shape, 1)
    c0 = total_of(jnp.where((rows_of(t.shape) == my_sub()) & (lane == 0), c0, 0.0))
    for x in range(cx):
        u = work[1, x + 1] + c0
        u0_ref[x] = u
        to_north[x : x + 1] = u[cy - 1 : cy]
        to_south[x : x + 1] = u[0:1]
    layers_kernel(u0_ref, to_a, to_b)


def fill(padded, field, halo_a, halo_b):
    odd = lax.axis_index("group") % 2 == 1
    cx = field.shape[0]
    a, b = halo_a[...], halo_b[...]
    padded[0] = jnp.where(odd, b, a)
    padded[cx + 1] = jnp.where(odd, a, b)
    for x in range(cx):
        padded[x + 1] = field[x]


def first_kernel(
    halo_a, halo_b, halo_north, halo_south, u0_ref, storage,
    east_t, north_t, south_t, upper_t, lower_t, edge_east, edge_west, edge_north, edge_south,
    scale, w_east, w_west, w_north, w_south, w_upper, w_lower,
    image, result, to_north, to_south, padded, first, work,
):
    cx, cy, cz = storage.shape
    fill(padded, u0_ref, halo_a, halo_b)
    inner, outer = (east_t, north_t, south_t, upper_t, lower_t), (edge_east, edge_west, edge_north, edge_south)
    apply(padded, halo_north, halo_south, storage, inner, outer, image)
    for x in range(cx):
        s = scale[x] * image[x]
        first[x] = s
        work[0, x + 1] = s
    clear_ends(work)
    smooth(first, work, (w_east, w_west, w_north, w_south, w_upper, w_lower))
    for x in range(cx):
        f1 = work[1, x + 1]
        result[x] = f1
        to_north[x : x + 1] = f1[cy - 1 : cy]
        to_south[x : x + 1] = f1[0:1]


def dots_kernel(groups, source, u0_ref, image, f1_ref, edge_east, edge_north, sums, out):
    r_u0 = u0_v0 = v0_f1 = total = jnp.zeros((8, LANES), jnp.float32)
    for x in range(source.shape[0]):
        r, u0, v0, f1 = source[x], u0_ref[x], image[x], f1_ref[x]
        r_u0 = r_u0 + fold(r * u0)
        u0_v0 = u0_v0 + fold(u0 * v0)
        v0_f1 = v0_f1 + fold(v0 * f1)
        total = total + fold(v0)
    me = lax.axis_index("group")
    totals = (
        (AGAINST * groups + me, total_of(total)),
        (STORED * groups + me, sums[0:1, 0:1]),
        (COUPLING * groups + me, total_of(edge_north[...])),
        (EAST * groups + me, total_of(fold(edge_east[...]))),
        (DOTS, total_of(r_u0)),
        (DOTS + 1, total_of(u0_v0)),
        (DOTS + 2, total_of(v0_f1)),
    )
    out[...] = placed(totals)


def second_kernel(
    groups, halo_a, halo_b, halo_north, halo_south, f1_ref, dots, storage,
    east_t, north_t, south_t, upper_t, lower_t, edge_east, edge_west, edge_north, edge_south,
    image, out, padded,
):
    fill(padded, f1_ref, halo_a, halo_b)
    inner, outer = (east_t, north_t, south_t, upper_t, lower_t), (edge_east, edge_west, edge_north, edge_south)
    apply(padded, halo_north, halo_south, storage, inner, outer, image)
    total = f1_g1 = jnp.zeros((8, LANES), jnp.float32)
    for x in range(storage.shape[0]):
        g1 = image[x]
        total = total + fold(g1)
        f1_g1 = f1_g1 + fold(f1_ref[x] * g1)
    me = lax.axis_index("group")
    scalars = dots[...] + placed(((IMAGE * groups + me, total_of(total)), (DOTS + 3, total_of(f1_g1))))
    core = lax.axis_index("core")
    cores = out.shape[1] // LANES
    out[...] = jnp.concatenate([jnp.where(core == at, scalars, 0.0) for at in range(cores)], axis=1)


def last_kernel(
    steps, groups, table, u0_ref, f1_ref, image, storage, edge_east, edge_west, edge_north, edge_south,
    scale, w_east, w_west, w_north, w_south, w_upper, w_lower, pressure_out, precond_out,
    first, work, pressure, precond, sems,
):
    cx, cy, cz = storage.shape
    t = table[...]
    members = t.shape[0]
    lane = lax.broadcasted_iota(jnp.int32, t.shape, 1)
    mine = (rows_of(t.shape) == my_sub()) & (lane == lax.axis_index("group"))

    def column(at):
        return shift(t, -at * groups, 1)

    def pick(value):
        return total_of(jnp.where(mine, value, 0.0))

    def to_the_east(value):
        return jnp.where(lane == groups - 1, shift(value, groups - 1, 1), shift(value, -1, 1))

    def to_the_west(value):
        return jnp.where(lane == 0, shift(value, 1 - groups, 1), shift(value, 1, 1))

    against, image_sum, stored, after, right = (column(at) for at in (AGAINST, IMAGE, STORED, COUPLING, EAST))
    factors, last = reduce_rows(stored / members, after * members, steps)
    c1 = solve_rows(factors, last, against)
    c_east, c_west, c_north, c_south = to_the_east(c1), to_the_west(c1), shift(c1, -1, 0), shift(c1, 1, 0)
    coupled = (
        stored * c1 + after * (c1 - c_north) + shift(after, 1, 0) * (c1 - c_south)
        + right * (c1 - c_east) + to_the_west(right) * (c1 - c_west)
    )
    c2 = solve_rows(factors, last, image_sum + coupled)
    valid = lane < groups
    sums = jnp.sum(t, axis=0, keepdims=True)
    r_u0, u0_v0, v0_u1, u1_v1 = (sums[:, DOTS + at : DOTS + at + 1] for at in range(4))
    v0_u1 = v0_u1 + total_of(jnp.where(valid, c1 * against, 0.0))
    u1_v1 = u1_v1 + total_of(jnp.where(valid, c1 * (2.0 * image_sum + coupled), 0.0))
    c1, c_east, c_west, c_north, c_south, c2 = (pick(c) for c in (c1, c_east, c_west, c_north, c_south, c2))

    a0 = r_u0 / u0_v0
    rz = a0 * a0 * v0_u1 - r_u0
    keep = 1.0 + rz / r_u0
    a1 = rz / (keep * keep * u0_v0 - 2.0 * keep * a0 * v0_u1 + a0 * a0 * u1_v1)
    p0, p1 = a0 + a1 * keep, a1 * a0

    def send(at, x):
        src, dst = ((pressure, pressure_out), (precond, precond_out))[at]
        copy = pltpu.make_async_copy(src.at[x], dst.at[x], sems.at[at, x])
        copy.start()
        return copy

    copies = []
    row = rows_of((cy, cz))
    for x in range(cx):
        pressure[x] = p0 * u0_ref[x] - p1 * (f1_ref[x] + c1)
        copies.append(send(0, x))
        one = slice(x, x + 1)
        edge = jnp.where(row == 0, edge_south[one] * (c1 - c_south), 0.0)
        edge = jnp.where(row == cy - 1, edge_north[one] * (c1 - c_north), edge)
        v1 = image[x] + storage[x] * c1 + edge
        if x == 0:
            v1 = v1 + edge_west[...] * (c1 - c_west)
        if x == cx - 1:
            v1 = v1 + edge_east[...] * (c1 - c_east)
        s = scale[x] * v1
        first[x] = s
        work[0, x + 1] = s
    clear_ends(work)
    smooth(first, work, (w_east, w_west, w_north, w_south, w_upper, w_lower))
    for x in range(cx):
        precond[x] = u0_ref[x] - p0 * (f1_ref[x] + c1) + p1 * (work[1, x + 1] + c2)
        copies.append(send(1, x))
    for copy in copies:
        copy.wait()


def call(body, outs, scratch, *operands, cost=0, hbm=False):
    space = pl.BlockSpec(memory_space=pltpu.VMEM)
    return pl.pallas_call(
        body,
        out_shape=[jax.ShapeDtypeStruct(s, jnp.float32) for s in outs],
        in_specs=[space] * len(operands),
        out_specs=[pl.BlockSpec(memory_space=pl.ANY) if hbm else space] * len(outs),
        scratch_shapes=[pltpu.VMEM(s, jnp.float32) if isinstance(s, tuple) else s for s in scratch],
        compiler_params=pltpu.CompilerParams(vmem_limit_bytes=VMEM),
        cost_estimate=pl.CostEstimate(flops=cost, bytes_accessed=4 * cost, transcendentals=0) if cost else None,
    )(*operands)


def over_group(to_a, to_b):
    groups = lax.axis_size("group")
    a = lax.ppermute(to_a, "group", [(i, (((i + 1) ^ 1) - 1) % groups) for i in range(groups)])
    b = lax.ppermute(to_b, "group", [(i, i ^ 1) for i in range(groups)])
    return a, b


def over_sub(to_north, to_south):
    peers = lax.axis_size(SUB)
    up = [(i, (i + 1) % peers) for i in range(peers)]
    south = lax.ppermute(to_north, SUB, up)
    north = lax.ppermute(to_south, SUB, [(j, i) for i, j in up])
    return north, south


def gather(row, axis):
    peers = lax.axis_size(axis)
    rows = jnp.broadcast_to(row, (peers, row.shape[1]))[:, None]
    return lax.all_to_all(rows, axis, 0, 0).reshape(peers, row.shape[1])


def shards(source, perm, storage):
    cx, cy, cz = source.shape
    groups, members = lax.axis_size("group"), lax.axis_size(SUB)
    steps = members.bit_length() - 1
    full, wide, layer, edge, row = (cx, cy, cz), (cx + 2, cy, cz), (cy, cz), (cx, cz), (1, LANES)
    rounds = [full, (2,) + wide]
    strip_north, strip_south = perm[:, -1], perm[:, 0]
    halos = over_sub(strip_north, strip_south)
    source, storage, west, east, *inner, diagonal, sums = call(
        inner_kernel,
        [full, full, layer, layer, (cx + 1, cy, cz)] + [full] * 5 + [row],
        [],
        source, perm, storage, cost=2**21,
    )
    edge_north, edge_south, to_a, to_b, scalars = call(
        edge_kernel,
        [edge, edge, layer, layer, (members, LANES)],
        [],
        *halos, strip_north, strip_south, west, east, sums,
    )
    table = gather(scalars, SUB)
    edge_east, edge_west, *weights, u0, to_a, to_b, to_north, to_south = call(
        functools.partial(assemble_kernel, steps),
        [layer, layer] + [full] * 8 + [layer, layer, edge, edge],
        rounds,
        *over_group(to_a, to_b), table, source, west, east, *inner, diagonal, edge_north, edge_south,
    )
    outer = [edge_east, edge_west, edge_north, edge_south]
    halos = over_group(to_a, to_b) + over_sub(to_north, to_south)
    v0, f1, to_north, to_south = call(
        first_kernel, [full, full, edge, edge], [wide] + rounds, *halos, u0, storage, *inner, *outer, *weights
    )
    to_a, to_b = call(layers_kernel, [layer, layer], [], f1)
    halos = over_group(to_a, to_b) + over_sub(to_north, to_south)
    (dots,) = call(
        functools.partial(dots_kernel, groups), [row], [],
        source, u0, v0, f1, edge_east, edge_north, sums, cost=2**20,
    )
    cores = lax.axis_size("core")
    g1, scalars = call(
        functools.partial(second_kernel, groups),
        [full, (1, cores * LANES)],
        [wide],
        *halos, f1, dots, storage, *inner, *outer,
    )
    scalars = gather(scalars, ("group", "core"))
    scalars = sum(scalars[i : i + 1] for i in range(groups * cores))
    table = gather(scalars, "z").reshape(members, LANES)
    return tuple(
        call(
            functools.partial(last_kernel, steps, groups),
            [full, full],
            rounds + [full, full, pltpu.SemaphoreType.DMA((2, cx))],
            table, u0, f1, g1, storage, *outer, *weights, hbm=True,
        )
    )


def solution(mesh):
    groups, members = (mesh.shape[axis] for axis in ("group", "sub"))
    cores = 2
    mesh = jax.sharding.Mesh(mesh.devices.reshape(groups, members // cores, cores), ("group", "z", "core"))
    spec = P("group", SUB, None)
    return jax.shard_map(shards, mesh=mesh, in_specs=(spec,) * 3, out_specs=(spec,) * 2, check_vma=False)
```

```python
import functools

import jax
import jax.numpy as jnp
from jax import lax
from jax.experimental import pallas as pl
from jax.experimental.pallas import tpu as pltpu
from jax.sharding import PartitionSpec as P

OMEGA = 0.8
LANES = 128
VMEM = 16 * 2**20
UNROLL = True
SUB = ("z", "core")
AGAINST, IMAGE, STORED, COUPLING, EAST = range(5)
DOTS = 120


def harmonic(left, right):
    return 2.0 * left * right / (left + right)


def shift(value, by, axis):
    return pltpu.roll(value, by % value.shape[axis], axis)


def my_sub():
    return lax.axis_index("z") * lax.axis_size("core") + lax.axis_index("core")


def rows_of(shape):
    return lax.broadcasted_iota(jnp.int32, shape, 0)


def fold(value):
    total = None
    for y in range(0, value.shape[0], 8):
        for z in range(0, value.shape[1], LANES):
            tile = value[y : y + 8, z : z + LANES]
            total = tile if total is None else total + tile
    return total


def total_of(value):
    return jnp.sum(value, axis=(0, 1), keepdims=True)


def placed(totals):
    lane = lax.broadcasted_iota(jnp.int32, (1, LANES), 1)
    row = jnp.zeros((1, LANES), jnp.float32)
    for at, total in totals:
        row = jnp.where(lane == at, total, row)
    return row


def smooth(first, work, weights):
    cx = first.shape[0]
    east, west, north, south, upper, lower = weights

    def sweep(src, dst):
        def slab(x, carry):
            s = src[x + 1]
            total = (1.0 - OMEGA) * s + first[x]
            total = total + east[x] * src[x + 2] + west[x] * src[x]
            total = total + north[x] * shift(s, -1, 0) + south[x] * shift(s, 1, 0)
            total = total + upper[x] * shift(s, -1, 1) + lower[x] * shift(s, 1, 1)
            dst[x + 1] = total
            return carry

        lax.fori_loop(0, cx, slab, 0, unroll=UNROLL)

    sweep(work.at[0], work.at[1])
    sweep(work.at[1], work.at[0])
    sweep(work.at[0], work.at[1])


def clear_ends(work):
    for at in range(2):
        for end in (0, work.shape[1] - 1):
            work[at, end] = jnp.zeros(work.shape[2:], jnp.float32)


def apply(padded, north_halo, south_halo, storage, inner, edges, out):
    cx, cy = storage.shape[:2]
    east_t, north_t, south_t, upper_t, lower_t = inner
    edge_east, edge_west, edge_north, edge_south = edges

    def slab(x, carry):
        u = padded[x + 1]
        row = rows_of(u.shape)
        total = storage[x] * u
        total = total + east_t[x + 1] * (u - padded[x + 2]) + east_t[x] * (u - padded[x])
        total = total + north_t[x] * (u - shift(u, -1, 0)) + south_t[x] * (u - shift(u, 1, 0))
        total = total + upper_t[x] * (u - shift(u, -1, 1)) + lower_t[x] * (u - shift(u, 1, 1))
        one = pl.ds(x, 1)
        north = jnp.where(row == cy - 1, edge_north[one] * (u - north_halo[one]), 0.0)
        total = total + jnp.where(row == 0, edge_south[one] * (u - south_halo[one]), north)
        out[x] = total
        return carry

    lax.fori_loop(0, cx, slab, 0, unroll=UNROLL)
    out[0] = out[0] + edge_west[...] * (padded[1] - padded[0])
    out[cx - 1] = out[cx - 1] + edge_east[...] * (padded[cx] - padded[cx + 1])


def inner_kernel(
    source, perm, storage,
    source_out, storage_out, west_out, east_out, east_t, north_t, south_t, upper_t, lower_t, diagonal, sums,
):
    cx, cy, cz = source.shape
    west_out[...] = perm[0]
    east_out[...] = perm[cx - 1]
    row = rows_of((cy, cz))
    west = jnp.zeros((cy, cz), jnp.float32)
    east_t[0] = west
    stored = total_r = jnp.zeros((8, LANES), jnp.float32)
    for x in range(cx):
        k = perm[x]
        east = harmonic(k, perm[x + 1]) if x + 1 < cx else jnp.zeros((cy, cz), jnp.float32)
        north = jnp.where(row == cy - 1, 0.0, harmonic(k, shift(k, -1, 0)))
        south = shift(north, 1, 0)
        upper = harmonic(k, shift(k, -1, 1))
        lower = shift(upper, 1, 1)
        east_t[x + 1] = east
        north_t[x] = north
        south_t[x] = south
        upper_t[x] = upper
        lower_t[x] = lower
        w, r = storage[x], source[x]
        diagonal[x] = w + east + west + north + south + upper + lower
        storage_out[x] = w
        source_out[x] = r
        stored = stored + fold(w)
        total_r = total_r + fold(r)
        west = east
    sums[...] = placed(((0, total_of(stored)), (2, total_of(total_r))))


def edge_kernel(
    perm_north, perm_south, strip_north, strip_south, west, east, sums, edge_north, edge_south, to_a, to_b, out
):
    north = harmonic(strip_north[...], perm_north[...])
    edge_north[...] = north
    edge_south[...] = harmonic(perm_south[...], strip_south[...])
    out[...] = jnp.broadcast_to(sums[...] + placed(((1, total_of(north)),)), out.shape)
    by_side(west[...], east[...], to_a, to_b)


def by_side(west, east, to_a, to_b):
    odd = lax.axis_index("group") % 2 == 1
    to_a[...] = jnp.where(odd, east, west)
    to_b[...] = jnp.where(odd, west, east)


def layers_kernel(field, to_a, to_b):
    by_side(field[0], field[field.shape[0] - 1], to_a, to_b)


def reduce_rows(margin, coupling, steps):
    before, after = shift(coupling, 1, 0), coupling
    factors = []
    for step in range(steps):
        h = 2**step
        inverse = 1.0 / (margin + before + after)
        from_before = before * shift(inverse, h, 0)
        from_after = after * shift(inverse, -h, 0)
        margin = margin + from_before * shift(margin, h, 0) + from_after * shift(margin, -h, 0)
        before, after = from_before * shift(before, h, 0), from_after * shift(after, -h, 0)
        factors.append((from_before, from_after))
    return factors, 1.0 / margin


def solve_rows(factors, last, right):
    for step, (from_before, from_after) in enumerate(factors):
        h = 2**step
        right = right + from_before * shift(right, h, 0) + from_after * shift(right, -h, 0)
    return right * last


def assemble_kernel(
    steps, perm_a, perm_b, table, source, perm_west, perm_east,
    east_in, north_in, south_in, upper_t, lower_t, diagonal, edge_north, edge_south,
    edge_east, edge_west, scale, w_east, w_west, w_north, w_south, w_upper, w_lower,
    u0_ref, to_a, to_b, to_north, to_south, first, work,
):
    cx, cy, cz = source.shape
    odd = lax.axis_index("group") % 2 == 1
    row = rows_of((cy, cz))
    a, b = perm_a[...], perm_b[...]
    edge_east[...] = harmonic(perm_east[...], jnp.where(odd, a, b))
    edge_west[...] = harmonic(jnp.where(odd, b, a), perm_west[...])
    for x in range(cx):
        d = diagonal[x]
        d = d + jnp.where(row == cy - 1, edge_north[x : x + 1], jnp.where(row == 0, edge_south[x : x + 1], 0.0))
        if x == 0:
            d = d + edge_west[...]
        if x == cx - 1:
            d = d + edge_east[...]
        q = OMEGA / d
        scale[x] = q
        w_east[x] = q * east_in[x + 1]
        w_west[x] = q * east_in[x]
        w_north[x] = q * north_in[x]
        w_south[x] = q * south_in[x]
        w_upper[x] = q * upper_t[x]
        w_lower[x] = q * lower_t[x]
        s = q * source[x]
        first[x] = s
        work[0, x + 1] = s
    clear_ends(work)
    smooth(first, work, (w_east, w_west, w_north, w_south, w_upper, w_lower))

    t = table[...]
    members = t.shape[0]
    factors, last = reduce_rows(t / members, shift(t, -1, 1) * members, steps)
    c0 = solve_rows(factors, last, shift(t, -2, 1))
    lane = lax.broadcasted_iota(jnp.int32, t.shape, 1)
    c0 = total_of(jnp.where((rows_of(t.shape) == my_sub()) & (lane == 0), c0, 0.0))
    for x in range(cx):
        u = work[1, x + 1] + c0
        u0_ref[x] = u
        to_north[x : x + 1] = u[cy - 1 : cy]
        to_south[x : x + 1] = u[0:1]
    layers_kernel(u0_ref, to_a, to_b)


def fill(padded, field, halo_a, halo_b):
    odd = lax.axis_index("group") % 2 == 1
    cx = field.shape[0]
    a, b = halo_a[...], halo_b[...]
    padded[0] = jnp.where(odd, b, a)
    padded[cx + 1] = jnp.where(odd, a, b)
    for x in range(cx):
        padded[x + 1] = field[x]


def first_kernel(
    halo_a, halo_b, halo_north, halo_south, u0_ref, storage,
    east_t, north_t, south_t, upper_t, lower_t, edge_east, edge_west, edge_north, edge_south,
    scale, w_east, w_west, w_north, w_south, w_upper, w_lower,
    image, result, to_north, to_south, padded, first, work,
):
    cx, cy, cz = storage.shape
    fill(padded, u0_ref, halo_a, halo_b)
    inner, outer = (east_t, north_t, south_t, upper_t, lower_t), (edge_east, edge_west, edge_north, edge_south)
    apply(padded, halo_north, halo_south, storage, inner, outer, image)
    for x in range(cx):
        s = scale[x] * image[x]
        first[x] = s
        work[0, x + 1] = s
    clear_ends(work)
    smooth(first, work, (w_east, w_west, w_north, w_south, w_upper, w_lower))
    for x in range(cx):
        f1 = work[1, x + 1]
        result[x] = f1
        to_north[x : x + 1] = f1[cy - 1 : cy]
        to_south[x : x + 1] = f1[0:1]


def dots_kernel(groups, source, u0_ref, image, f1_ref, edge_east, edge_north, sums, out):
    r_u0 = u0_v0 = v0_f1 = total = jnp.zeros((8, LANES), jnp.float32)
    for x in range(source.shape[0]):
        r, u0, v0, f1 = source[x], u0_ref[x], image[x], f1_ref[x]
        r_u0 = r_u0 + fold(r * u0)
        u0_v0 = u0_v0 + fold(u0 * v0)
        v0_f1 = v0_f1 + fold(v0 * f1)
        total = total + fold(v0)
    me = lax.axis_index("group")
    totals = (
        (AGAINST * groups + me, total_of(total)),
        (STORED * groups + me, sums[0:1, 0:1]),
        (COUPLING * groups + me, total_of(edge_north[...])),
        (EAST * groups + me, total_of(fold(edge_east[...]))),
        (DOTS, total_of(r_u0)),
        (DOTS + 1, total_of(u0_v0)),
        (DOTS + 2, total_of(v0_f1)),
    )
    out[...] = placed(totals)


def second_kernel(
    groups, halo_a, halo_b, halo_north, halo_south, f1_ref, dots, storage,
    east_t, north_t, south_t, upper_t, lower_t, edge_east, edge_west, edge_north, edge_south,
    image, out, padded,
):
    fill(padded, f1_ref, halo_a, halo_b)
    inner, outer = (east_t, north_t, south_t, upper_t, lower_t), (edge_east, edge_west, edge_north, edge_south)
    apply(padded, halo_north, halo_south, storage, inner, outer, image)
    total = f1_g1 = jnp.zeros((8, LANES), jnp.float32)
    for x in range(storage.shape[0]):
        g1 = image[x]
        total = total + fold(g1)
        f1_g1 = f1_g1 + fold(f1_ref[x] * g1)
    me = lax.axis_index("group")
    scalars = dots[...] + placed(((IMAGE * groups + me, total_of(total)), (DOTS + 3, total_of(f1_g1))))
    core = lax.axis_index("core")
    cores = out.shape[1] // LANES
    out[...] = jnp.concatenate([jnp.where(core == at, scalars, 0.0) for at in range(cores)], axis=1)


def last_kernel(
    steps, groups, table, u0_ref, f1_ref, image, storage, edge_east, edge_west, edge_north, edge_south,
    scale, w_east, w_west, w_north, w_south, w_upper, w_lower, pressure_out, precond_out,
    first, work, pressure, precond, sems,
):
    cx, cy, cz = storage.shape
    t = table[...]
    members = t.shape[0]
    lane = lax.broadcasted_iota(jnp.int32, t.shape, 1)
    mine = (rows_of(t.shape) == (my_sub() + members // 2) % members) & (lane == lax.axis_index("group"))

    def column(at):
        return shift(t, -at * groups, 1)

    def pick(value):
        return total_of(jnp.where(mine, value, 0.0))

    def to_the_east(value):
        return jnp.where(lane == groups - 1, shift(value, groups - 1, 1), shift(value, -1, 1))

    def to_the_west(value):
        return jnp.where(lane == 0, shift(value, 1 - groups, 1), shift(value, 1, 1))

    against, image_sum, stored, after, right = (column(at) for at in (AGAINST, IMAGE, STORED, COUPLING, EAST))
    factors, last = reduce_rows(stored / members, after * members, steps)
    c1 = solve_rows(factors, last, against)
    c_east, c_west, c_north, c_south = to_the_east(c1), to_the_west(c1), shift(c1, -1, 0), shift(c1, 1, 0)
    coupled = (
        stored * c1 + after * (c1 - c_north) + shift(after, 1, 0) * (c1 - c_south)
        + right * (c1 - c_east) + to_the_west(right) * (c1 - c_west)
    )
    c2 = solve_rows(factors, last, image_sum + coupled)
    valid = lane < groups
    sums = jnp.sum(t, axis=0, keepdims=True)
    r_u0, u0_v0, v0_u1, u1_v1 = (sums[:, DOTS + at : DOTS + at + 1] for at in range(4))
    v0_u1 = v0_u1 + total_of(jnp.where(valid, c1 * against, 0.0))
    u1_v1 = u1_v1 + total_of(jnp.where(valid, c1 * (2.0 * image_sum + coupled), 0.0))
    c1, c_east, c_west, c_north, c_south, c2 = (pick(c) for c in (c1, c_east, c_west, c_north, c_south, c2))

    a0 = r_u0 / u0_v0
    rz = a0 * a0 * v0_u1 - r_u0
    keep = 1.0 + rz / r_u0
    a1 = rz / (keep * keep * u0_v0 - 2.0 * keep * a0 * v0_u1 + a0 * a0 * u1_v1)
    p0, p1 = a0 + a1 * keep, a1 * a0

    def send(at, x):
        src, dst = ((pressure, pressure_out), (precond, precond_out))[at]
        copy = pltpu.make_async_copy(src.at[x], dst.at[x], sems.at[at, x])
        copy.start()
        return copy

    copies = []
    row = rows_of((cy, cz))
    for x in range(cx):
        pressure[x] = p0 * u0_ref[x] - p1 * (f1_ref[x] + c1)
        copies.append(send(0, x))
        one = slice(x, x + 1)
        edge = jnp.where(row == 0, edge_south[one] * (c1 - c_south), 0.0)
        edge = jnp.where(row == cy - 1, edge_north[one] * (c1 - c_north), edge)
        v1 = image[x] + storage[x] * c1 + edge
        if x == 0:
            v1 = v1 + edge_west[...] * (c1 - c_west)
        if x == cx - 1:
            v1 = v1 + edge_east[...] * (c1 - c_east)
        s = scale[x] * v1
        first[x] = s
        work[0, x + 1] = s
    clear_ends(work)
    smooth(first, work, (w_east, w_west, w_north, w_south, w_upper, w_lower))
    for x in range(cx):
        precond[x] = u0_ref[x] - p0 * (f1_ref[x] + c1) + p1 * (work[1, x + 1] + c2)
        copies.append(send(1, x))
    for copy in copies:
        copy.wait()


def call(body, outs, scratch, *operands, cost=0, hbm=False):
    space = pl.BlockSpec(memory_space=pltpu.VMEM)
    return pl.pallas_call(
        body,
        out_shape=[jax.ShapeDtypeStruct(s, jnp.float32) for s in outs],
        in_specs=[space] * len(operands),
        out_specs=[pl.BlockSpec(memory_space=pl.ANY) if hbm else space] * len(outs),
        scratch_shapes=[pltpu.VMEM(s, jnp.float32) if isinstance(s, tuple) else s for s in scratch],
        compiler_params=pltpu.CompilerParams(vmem_limit_bytes=VMEM),
        cost_estimate=pl.CostEstimate(flops=cost, bytes_accessed=4 * cost, transcendentals=0) if cost else None,
    )(*operands)


def over_group(to_a, to_b):
    groups = lax.axis_size("group")
    a = lax.ppermute(to_a, "group", [(i, (((i + 1) ^ 1) - 1) % groups) for i in range(groups)])
    b = lax.ppermute(to_b, "group", [(i, i ^ 1) for i in range(groups)])
    return a, b


def over_sub(to_north, to_south):
    peers = lax.axis_size(SUB)
    up = [(i, (i + 1) % peers) for i in range(peers)]
    south = lax.ppermute(to_north, SUB, up)
    north = lax.ppermute(to_south, SUB, [(j, i) for i, j in up])
    return north, south


def gather(row, axis, first=0):
    peers = lax.axis_size(axis)
    order = [[(first + i) % peers for i in range(peers)]] if first else None
    rows = jnp.broadcast_to(row, (peers, row.shape[1]))[:, None]
    return lax.all_to_all(rows, axis, 0, 0, axis_index_groups=order).reshape(peers, row.shape[1])


def shards(source, perm, storage):
    cx, cy, cz = source.shape
    groups, members = lax.axis_size("group"), lax.axis_size(SUB)
    steps = members.bit_length() - 1
    full, wide, layer, edge, row = (cx, cy, cz), (cx + 2, cy, cz), (cy, cz), (cx, cz), (1, LANES)
    rounds = [full, (2,) + wide]
    strip_north, strip_south = perm[:, -1], perm[:, 0]
    halos = over_sub(strip_north, strip_south)
    source, storage, west, east, *inner, diagonal, sums = call(
        inner_kernel,
        [full, full, layer, layer, (cx + 1, cy, cz)] + [full] * 5 + [row],
        [],
        source, perm, storage, cost=2**21,
    )
    edge_north, edge_south, to_a, to_b, scalars = call(
        edge_kernel,
        [edge, edge, layer, layer, (members, LANES)],
        [],
        *halos, strip_north, strip_south, west, east, sums,
    )
    table = gather(scalars, SUB)
    edge_east, edge_west, *weights, u0, to_a, to_b, to_north, to_south = call(
        functools.partial(assemble_kernel, steps),
        [layer, layer] + [full] * 8 + [layer, layer, edge, edge],
        rounds,
        *over_group(to_a, to_b), table, source, west, east, *inner, diagonal, edge_north, edge_south,
    )
    outer = [edge_east, edge_west, edge_north, edge_south]
    halos = over_group(to_a, to_b) + over_sub(to_north, to_south)
    v0, f1, to_north, to_south = call(
        first_kernel, [full, full, edge, edge], [wide] + rounds, *halos, u0, storage, *inner, *outer, *weights
    )
    to_a, to_b = call(layers_kernel, [layer, layer], [], f1)
    halos = over_group(to_a, to_b) + over_sub(to_north, to_south)
    (dots,) = call(
        functools.partial(dots_kernel, groups), [row], [],
        source, u0, v0, f1, edge_east, edge_north, sums, cost=2**20,
    )
    cores = lax.axis_size("core")
    g1, scalars = call(
        functools.partial(second_kernel, groups),
        [full, (1, cores * LANES)],
        [wide],
        *halos, f1, dots, storage, *inner, *outer,
    )
    scalars = gather(scalars, ("group", "core"), groups * 5 // 8 * cores)
    scalars = sum(scalars[i : i + 1] for i in range(groups * cores))
    table = gather(scalars, "z", lax.axis_size("z") // 2).reshape(members, LANES)
    return tuple(
        call(
            functools.partial(last_kernel, steps, groups),
            [full, full],
            rounds + [full, full, pltpu.SemaphoreType.DMA((2, cx))],
            table, u0, f1, g1, storage, *outer, *weights, hbm=True,
        )
    )


def solution(mesh):
    groups, members = (mesh.shape[axis] for axis in ("group", "sub"))
    cores = 2
    mesh = jax.sharding.Mesh(mesh.devices.reshape(groups, members // cores, cores), ("group", "z", "core"))
    spec = P("group", SUB, None)
    return jax.shard_map(shards, mesh=mesh, in_specs=(spec,) * 3, out_specs=(spec,) * 2, check_vma=False)
```

```python
import functools

import jax
import jax.numpy as jnp
from jax import lax
from jax.experimental import pallas as pl
from jax.experimental.pallas import tpu as pltpu
from jax.sharding import PartitionSpec as P

OMEGA = 0.8
LANES = 128
VMEM = 16 * 2**20
UNROLL = True
SUB = ("z", "core")
AGAINST, IMAGE, STORED, COUPLING, EAST = range(5)
DOTS = 120


def harmonic(left, right):
    return 2.0 * left * right / (left + right)


def shift(value, by, axis):
    return pltpu.roll(value, by % value.shape[axis], axis)


def my_sub():
    return lax.axis_index("z") * lax.axis_size("core") + lax.axis_index("core")


def rows_of(shape):
    return lax.broadcasted_iota(jnp.int32, shape, 0)


def fold(value):
    total = None
    for y in range(0, value.shape[0], 8):
        for z in range(0, value.shape[1], LANES):
            tile = value[y : y + 8, z : z + LANES]
            total = tile if total is None else total + tile
    return total


def total_of(value):
    return jnp.sum(value, axis=(0, 1), keepdims=True)


def placed(totals):
    lane = lax.broadcasted_iota(jnp.int32, (1, LANES), 1)
    row = jnp.zeros((1, LANES), jnp.float32)
    for at, total in totals:
        row = jnp.where(lane == at, total, row)
    return row


def smooth(first, work, weights):
    cx = first.shape[0]
    east, west, north, south, upper, lower = weights

    def sweep(src, dst):
        def slab(x, carry):
            s = src[x + 1]
            total = (1.0 - OMEGA) * s + first[x]
            total = total + east[x] * src[x + 2] + west[x] * src[x]
            total = total + north[x] * shift(s, -1, 0) + south[x] * shift(s, 1, 0)
            total = total + upper[x] * shift(s, -1, 1) + lower[x] * shift(s, 1, 1)
            dst[x + 1] = total
            return carry

        lax.fori_loop(0, cx, slab, 0, unroll=UNROLL)

    sweep(work.at[0], work.at[1])
    sweep(work.at[1], work.at[0])
    sweep(work.at[0], work.at[1])


def clear_ends(work):
    for at in range(2):
        for end in (0, work.shape[1] - 1):
            work[at, end] = jnp.zeros(work.shape[2:], jnp.float32)


def apply(padded, north_halo, south_halo, storage, inner, edges, out):
    cx, cy = storage.shape[:2]
    east_t, north_t, south_t, upper_t, lower_t = inner
    edge_east, edge_west, edge_north, edge_south = edges

    def slab(x, carry):
        u = padded[x + 1]
        row = rows_of(u.shape)
        total = storage[x] * u
        total = total + east_t[x + 1] * (u - padded[x + 2]) + east_t[x] * (u - padded[x])
        total = total + north_t[x] * (u - shift(u, -1, 0)) + south_t[x] * (u - shift(u, 1, 0))
        total = total + upper_t[x] * (u - shift(u, -1, 1)) + lower_t[x] * (u - shift(u, 1, 1))
        one = pl.ds(x, 1)
        north = jnp.where(row == cy - 1, edge_north[one] * (u - north_halo[one]), 0.0)
        total = total + jnp.where(row == 0, edge_south[one] * (u - south_halo[one]), north)
        out[x] = total
        return carry

    lax.fori_loop(0, cx, slab, 0, unroll=UNROLL)
    out[0] = out[0] + edge_west[...] * (padded[1] - padded[0])
    out[cx - 1] = out[cx - 1] + edge_east[...] * (padded[cx] - padded[cx + 1])


def strips_kernel(field, to_north, to_south):
    for x in range(field.shape[0]):
        to_north[x : x + 1] = field[x, field.shape[1] - 1 :]
        to_south[x : x + 1] = field[x, 0:1]


def inner_kernel(
    source, perm, storage,
    source_out, storage_out, west_out, east_out, east_t, north_t, south_t, upper_t, lower_t, diagonal, sums,
):
    cx, cy, cz = source.shape
    west_out[...] = perm[0]
    east_out[...] = perm[cx - 1]
    row = rows_of((cy, cz))
    west = jnp.zeros((cy, cz), jnp.float32)
    east_t[0] = west
    stored = total_r = jnp.zeros((8, LANES), jnp.float32)
    for x in range(cx):
        k = perm[x]
        east = harmonic(k, perm[x + 1]) if x + 1 < cx else jnp.zeros((cy, cz), jnp.float32)
        north = jnp.where(row == cy - 1, 0.0, harmonic(k, shift(k, -1, 0)))
        south = shift(north, 1, 0)
        upper = harmonic(k, shift(k, -1, 1))
        lower = shift(upper, 1, 1)
        east_t[x + 1] = east
        north_t[x] = north
        south_t[x] = south
        upper_t[x] = upper
        lower_t[x] = lower
        w, r = storage[x], source[x]
        diagonal[x] = w + east + west + north + south + upper + lower
        storage_out[x] = w
        source_out[x] = r
        stored = stored + fold(w)
        total_r = total_r + fold(r)
        west = east
    sums[...] = placed(((0, total_of(stored)), (2, total_of(total_r))))


def edge_kernel(
    perm_north, perm_south, strip_north, strip_south, west, east, sums, edge_north, edge_south, to_a, to_b, out
):
    north = harmonic(strip_north[...], perm_north[...])
    edge_north[...] = north
    edge_south[...] = harmonic(perm_south[...], strip_south[...])
    out[...] = jnp.broadcast_to(sums[...] + placed(((1, total_of(north)),)), out.shape)
    by_side(west[...], east[...], to_a, to_b)


def by_side(west, east, to_a, to_b):
    odd = lax.axis_index("group") % 2 == 1
    to_a[...] = jnp.where(odd, east, west)
    to_b[...] = jnp.where(odd, west, east)


def layers_kernel(field, to_a, to_b):
    by_side(field[0], field[field.shape[0] - 1], to_a, to_b)


def reduce_rows(margin, coupling, steps):
    before, after = shift(coupling, 1, 0), coupling
    factors = []
    for step in range(steps):
        h = 2**step
        inverse = 1.0 / (margin + before + after)
        from_before = before * shift(inverse, h, 0)
        from_after = after * shift(inverse, -h, 0)
        margin = margin + from_before * shift(margin, h, 0) + from_after * shift(margin, -h, 0)
        before, after = from_before * shift(before, h, 0), from_after * shift(after, -h, 0)
        factors.append((from_before, from_after))
    return factors, 1.0 / margin


def solve_rows(factors, last, right):
    for step, (from_before, from_after) in enumerate(factors):
        h = 2**step
        right = right + from_before * shift(right, h, 0) + from_after * shift(right, -h, 0)
    return right * last


def assemble_kernel(
    steps, perm_a, perm_b, table, source, perm_west, perm_east,
    east_in, north_in, south_in, upper_t, lower_t, diagonal, edge_north, edge_south,
    edge_east, edge_west, scale, w_east, w_west, w_north, w_south, w_upper, w_lower,
    u0_ref, to_a, to_b, to_north, to_south, first, work,
):
    cx, cy, cz = source.shape
    odd = lax.axis_index("group") % 2 == 1
    row = rows_of((cy, cz))
    a, b = perm_a[...], perm_b[...]
    edge_east[...] = harmonic(perm_east[...], jnp.where(odd, a, b))
    edge_west[...] = harmonic(jnp.where(odd, b, a), perm_west[...])
    for x in range(cx):
        d = diagonal[x]
        d = d + jnp.where(row == cy - 1, edge_north[x : x + 1], jnp.where(row == 0, edge_south[x : x + 1], 0.0))
        if x == 0:
            d = d + edge_west[...]
        if x == cx - 1:
            d = d + edge_east[...]
        q = OMEGA / d
        scale[x] = q
        w_east[x] = q * east_in[x + 1]
        w_west[x] = q * east_in[x]
        w_north[x] = q * north_in[x]
        w_south[x] = q * south_in[x]
        w_upper[x] = q * upper_t[x]
        w_lower[x] = q * lower_t[x]
        s = q * source[x]
        first[x] = s
        work[0, x + 1] = s
    clear_ends(work)
    smooth(first, work, (w_east, w_west, w_north, w_south, w_upper, w_lower))

    t = table[...]
    members = t.shape[0]
    factors, last = reduce_rows(t / members, shift(t, -1, 1) * members, steps)
    c0 = solve_rows(factors, last, shift(t, -2, 1))
    lane = lax.broadcasted_iota(jnp.int32, t.shape, 1)
    c0 = total_of(jnp.where((rows_of(t.shape) == (my_sub() + members - 28) % members) & (lane == 0), c0, 0.0))
    for x in range(cx):
        u = work[1, x + 1] + c0
        u0_ref[x] = u
        to_north[x : x + 1] = u[cy - 1 : cy]
        to_south[x : x + 1] = u[0:1]
    layers_kernel(u0_ref, to_a, to_b)


def fill(padded, field, halo_a, halo_b):
    odd = lax.axis_index("group") % 2 == 1
    cx = field.shape[0]
    a, b = halo_a[...], halo_b[...]
    padded[0] = jnp.where(odd, b, a)
    padded[cx + 1] = jnp.where(odd, a, b)
    for x in range(cx):
        padded[x + 1] = field[x]


def first_kernel(
    halo_a, halo_b, halo_north, halo_south, u0_ref, storage,
    east_t, north_t, south_t, upper_t, lower_t, edge_east, edge_west, edge_north, edge_south,
    scale, w_east, w_west, w_north, w_south, w_upper, w_lower,
    image, result, to_north, to_south, padded, first, work,
):
    cx, cy, cz = storage.shape
    fill(padded, u0_ref, halo_a, halo_b)
    inner, outer = (east_t, north_t, south_t, upper_t, lower_t), (edge_east, edge_west, edge_north, edge_south)
    apply(padded, halo_north, halo_south, storage, inner, outer, image)
    for x in range(cx):
        s = scale[x] * image[x]
        first[x] = s
        work[0, x + 1] = s
    clear_ends(work)
    smooth(first, work, (w_east, w_west, w_north, w_south, w_upper, w_lower))
    for x in range(cx):
        f1 = work[1, x + 1]
        result[x] = f1
        to_north[x : x + 1] = f1[cy - 1 : cy]
        to_south[x : x + 1] = f1[0:1]


def dots_kernel(groups, source, u0_ref, image, f1_ref, edge_east, edge_north, sums, out):
    r_u0 = u0_v0 = v0_f1 = total = jnp.zeros((8, LANES), jnp.float32)
    for x in range(source.shape[0]):
        r, u0, v0, f1 = source[x], u0_ref[x], image[x], f1_ref[x]
        r_u0 = r_u0 + fold(r * u0)
        u0_v0 = u0_v0 + fold(u0 * v0)
        v0_f1 = v0_f1 + fold(v0 * f1)
        total = total + fold(v0)
    me = lax.axis_index("group")
    totals = (
        (AGAINST * groups + me, total_of(total)),
        (STORED * groups + me, sums[0:1, 0:1]),
        (COUPLING * groups + me, total_of(edge_north[...])),
        (EAST * groups + me, total_of(fold(edge_east[...]))),
        (DOTS, total_of(r_u0)),
        (DOTS + 1, total_of(u0_v0)),
        (DOTS + 2, total_of(v0_f1)),
    )
    out[...] = placed(totals)


def second_kernel(
    groups, halo_a, halo_b, halo_north, halo_south, f1_ref, dots, storage,
    east_t, north_t, south_t, upper_t, lower_t, edge_east, edge_west, edge_north, edge_south,
    image, out, padded,
):
    fill(padded, f1_ref, halo_a, halo_b)
    inner, outer = (east_t, north_t, south_t, upper_t, lower_t), (edge_east, edge_west, edge_north, edge_south)
    apply(padded, halo_north, halo_south, storage, inner, outer, image)
    total = f1_g1 = jnp.zeros((8, LANES), jnp.float32)
    for x in range(storage.shape[0]):
        g1 = image[x]
        total = total + fold(g1)
        f1_g1 = f1_g1 + fold(f1_ref[x] * g1)
    me = lax.axis_index("group")
    scalars = dots[...] + placed(((IMAGE * groups + me, total_of(total)), (DOTS + 3, total_of(f1_g1))))
    core = lax.axis_index("core")
    cores = out.shape[1] // LANES
    out[...] = jnp.concatenate([jnp.where(core == at, scalars, 0.0) for at in range(cores)], axis=1)


def last_kernel(
    steps, groups, table, u0_ref, f1_ref, image, storage, edge_east, edge_west, edge_north, edge_south,
    scale, w_east, w_west, w_north, w_south, w_upper, w_lower, pressure_out, precond_out,
    first, work, pressure, precond, sems,
):
    cx, cy, cz = storage.shape
    t = table[...]
    members = t.shape[0]
    lane = lax.broadcasted_iota(jnp.int32, t.shape, 1)
    mine = (rows_of(t.shape) == (my_sub() + members - 14) % members) & (lane == lax.axis_index("group"))

    def column(at):
        return shift(t, -at * groups, 1)

    def pick(value):
        return total_of(jnp.where(mine, value, 0.0))

    def to_the_east(value):
        return jnp.where(lane == groups - 1, shift(value, groups - 1, 1), shift(value, -1, 1))

    def to_the_west(value):
        return jnp.where(lane == 0, shift(value, 1 - groups, 1), shift(value, 1, 1))

    against, image_sum, stored, after, right = (column(at) for at in (AGAINST, IMAGE, STORED, COUPLING, EAST))
    factors, last = reduce_rows(stored / members, after * members, steps)
    c1 = solve_rows(factors, last, against)
    c_east, c_west, c_north, c_south = to_the_east(c1), to_the_west(c1), shift(c1, -1, 0), shift(c1, 1, 0)
    coupled = (
        stored * c1 + after * (c1 - c_north) + shift(after, 1, 0) * (c1 - c_south)
        + right * (c1 - c_east) + to_the_west(right) * (c1 - c_west)
    )
    c2 = solve_rows(factors, last, image_sum + coupled)
    valid = lane < groups
    sums = jnp.sum(t, axis=0, keepdims=True)
    r_u0, u0_v0, v0_u1, u1_v1 = (sums[:, DOTS + at : DOTS + at + 1] for at in range(4))
    v0_u1 = v0_u1 + total_of(jnp.where(valid, c1 * against, 0.0))
    u1_v1 = u1_v1 + total_of(jnp.where(valid, c1 * (2.0 * image_sum + coupled), 0.0))
    c1, c_east, c_west, c_north, c_south, c2 = (pick(c) for c in (c1, c_east, c_west, c_north, c_south, c2))

    a0 = r_u0 / u0_v0
    rz = a0 * a0 * v0_u1 - r_u0
    keep = 1.0 + rz / r_u0
    a1 = rz / (keep * keep * u0_v0 - 2.0 * keep * a0 * v0_u1 + a0 * a0 * u1_v1)
    p0, p1 = a0 + a1 * keep, a1 * a0

    def send(at, x):
        src, dst = ((pressure, pressure_out), (precond, precond_out))[at]
        copy = pltpu.make_async_copy(src.at[x], dst.at[x], sems.at[at, x])
        copy.start()
        return copy

    copies = []
    row = rows_of((cy, cz))
    for x in range(cx):
        pressure[x] = p0 * u0_ref[x] - p1 * (f1_ref[x] + c1)
        copies.append(send(0, x))
        one = slice(x, x + 1)
        edge = jnp.where(row == 0, edge_south[one] * (c1 - c_south), 0.0)
        edge = jnp.where(row == cy - 1, edge_north[one] * (c1 - c_north), edge)
        v1 = image[x] + storage[x] * c1 + edge
        if x == 0:
            v1 = v1 + edge_west[...] * (c1 - c_west)
        if x == cx - 1:
            v1 = v1 + edge_east[...] * (c1 - c_east)
        s = scale[x] * v1
        first[x] = s
        work[0, x + 1] = s
    clear_ends(work)
    smooth(first, work, (w_east, w_west, w_north, w_south, w_upper, w_lower))
    for x in range(cx):
        precond[x] = u0_ref[x] - p0 * (f1_ref[x] + c1) + p1 * (work[1, x + 1] + c2)
        copies.append(send(1, x))
    for copy in copies:
        copy.wait()


def call(body, outs, scratch, *operands, cost=0, hbm=False):
    space = pl.BlockSpec(memory_space=pltpu.VMEM)
    return pl.pallas_call(
        body,
        out_shape=[jax.ShapeDtypeStruct(s, jnp.float32) for s in outs],
        in_specs=[space] * len(operands),
        out_specs=[pl.BlockSpec(memory_space=pl.ANY) if hbm else space] * len(outs),
        scratch_shapes=[pltpu.VMEM(s, jnp.float32) if isinstance(s, tuple) else s for s in scratch],
        compiler_params=pltpu.CompilerParams(vmem_limit_bytes=VMEM),
        cost_estimate=pl.CostEstimate(flops=cost, bytes_accessed=4 * cost, transcendentals=0) if cost else None,
    )(*operands)


def over_group(to_a, to_b):
    groups = lax.axis_size("group")
    a = lax.ppermute(to_a, "group", [(i, (((i + 1) ^ 1) - 1) % groups) for i in range(groups)])
    b = lax.ppermute(to_b, "group", [(i, i ^ 1) for i in range(groups)])
    return a, b


def over_sub(to_north, to_south):
    peers = lax.axis_size(SUB)
    up = [(i, (i + 1) % peers) for i in range(peers)]
    south = lax.ppermute(to_north, SUB, up)
    north = lax.ppermute(to_south, SUB, [(j, i) for i, j in up])
    return north, south


def gather(row, axis, first=0):
    peers = lax.axis_size(axis)
    order = [[(first + i) % peers for i in range(peers)]] if first else None
    rows = jnp.broadcast_to(row, (peers, row.shape[1]))[:, None]
    return lax.all_to_all(rows, axis, 0, 0, axis_index_groups=order).reshape(peers, row.shape[1])


def shards(source, perm, storage):
    cx, cy, cz = source.shape
    groups, members = lax.axis_size("group"), lax.axis_size(SUB)
    steps = members.bit_length() - 1
    full, wide, layer, edge, row = (cx, cy, cz), (cx + 2, cy, cz), (cy, cz), (cx, cz), (1, LANES)
    rounds = [full, (2,) + wide]
    strip_north, strip_south = call(strips_kernel, [edge, edge], [], perm)
    halos = over_sub(strip_north, strip_south)
    source, storage, west, east, *inner, diagonal, sums = call(
        inner_kernel,
        [full, full, layer, layer, (cx + 1, cy, cz)] + [full] * 5 + [row],
        [],
        source, perm, storage, cost=2**21,
    )
    edge_north, edge_south, to_a, to_b, scalars = call(
        edge_kernel,
        [edge, edge, layer, layer, (members, LANES)],
        [],
        *halos, strip_north, strip_south, west, east, sums,
    )
    table = gather(scalars, SUB, 28)
    edge_east, edge_west, *weights, u0, to_a, to_b, to_north, to_south = call(
        functools.partial(assemble_kernel, steps),
        [layer, layer] + [full] * 8 + [layer, layer, edge, edge],
        rounds,
        *over_group(to_a, to_b), table, source, west, east, *inner, diagonal, edge_north, edge_south,
    )
    outer = [edge_east, edge_west, edge_north, edge_south]
    halos = over_group(to_a, to_b) + over_sub(to_north, to_south)
    v0, f1, to_north, to_south = call(
        first_kernel, [full, full, edge, edge], [wide] + rounds, *halos, u0, storage, *inner, *outer, *weights
    )
    to_a, to_b = call(layers_kernel, [layer, layer], [], f1)
    halos = over_group(to_a, to_b) + over_sub(to_north, to_south)
    (dots,) = call(
        functools.partial(dots_kernel, groups), [row], [],
        source, u0, v0, f1, edge_east, edge_north, sums, cost=2**20,
    )
    cores = lax.axis_size("core")
    g1, scalars = call(
        functools.partial(second_kernel, groups),
        [full, (1, cores * LANES)],
        [wide],
        *halos, f1, dots, storage, *inner, *outer,
    )
    scalars = gather(scalars, ("group", "core"), groups * 5 // 8 * cores)
    scalars = sum(scalars[i : i + 1] for i in range(groups * cores))
    table = gather(scalars, "z", 7).reshape(members, LANES)
    return tuple(
        call(
            functools.partial(last_kernel, steps, groups),
            [full, full],
            rounds + [full, full, pltpu.SemaphoreType.DMA((2, cx))],
            table, u0, f1, g1, storage, *outer, *weights, hbm=True,
        )
    )


def solution(mesh):
    groups, members = (mesh.shape[axis] for axis in ("group", "sub"))
    cores = 2
    mesh = jax.sharding.Mesh(mesh.devices.reshape(groups, members // cores, cores), ("group", "z", "core"))
    spec = P("group", SUB, None)
    return jax.shard_map(shards, mesh=mesh, in_specs=(spec,) * 3, out_specs=(spec,) * 2, check_vma=False)
```

```python
import functools

import jax
import jax.numpy as jnp
from jax import lax
from jax.experimental import pallas as pl
from jax.experimental.pallas import tpu as pltpu
from jax.sharding import PartitionSpec as P

OMEGA = 0.8
LANES = 128
VMEM = 16 * 2**20
UNROLL = True
SUB = ("z", "core")
LEAD_COARSE, LEAD_GROUP, LEAD_LAST = 28, 10, 7
AGAINST, IMAGE, STORED, COUPLING, EAST = range(5)
DOTS = 120


def harmonic(left, right):
    return 2.0 * left * right / (left + right)


def shift(value, by, axis):
    return pltpu.roll(value, by % value.shape[axis], axis)


def my_sub():
    return lax.axis_index("z") * lax.axis_size("core") + lax.axis_index("core")


def rows_of(shape):
    return lax.broadcasted_iota(jnp.int32, shape, 0)


def fold(value):
    total = None
    for y in range(0, value.shape[0], 8):
        for z in range(0, value.shape[1], LANES):
            tile = value[y : y + 8, z : z + LANES]
            total = tile if total is None else total + tile
    return total


def total_of(value):
    return jnp.sum(value, axis=(0, 1), keepdims=True)


def placed(totals):
    lane = lax.broadcasted_iota(jnp.int32, (1, LANES), 1)
    row = jnp.zeros((1, LANES), jnp.float32)
    for at, total in totals:
        row = jnp.where(lane == at, total, row)
    return row


def smooth(first, work, weights):
    cx = first.shape[0]
    east, west, north, south, upper, lower = weights

    def sweep(src, dst):
        def slab(x, carry):
            s = src[x + 1]
            total = (1.0 - OMEGA) * s + first[x]
            total = total + east[x] * src[x + 2] + west[x] * src[x]
            total = total + north[x] * shift(s, -1, 0) + south[x] * shift(s, 1, 0)
            total = total + upper[x] * shift(s, -1, 1) + lower[x] * shift(s, 1, 1)
            dst[x + 1] = total
            return carry

        lax.fori_loop(0, cx, slab, 0, unroll=UNROLL)

    sweep(work.at[0], work.at[1])
    sweep(work.at[1], work.at[0])
    sweep(work.at[0], work.at[1])


def clear_ends(work):
    for at in range(2):
        for end in (0, work.shape[1] - 1):
            work[at, end] = jnp.zeros(work.shape[2:], jnp.float32)


def apply(padded, north_halo, south_halo, storage, inner, edges, out):
    cx, cy = storage.shape[:2]
    east_t, north_t, south_t, upper_t, lower_t = inner
    edge_east, edge_west, edge_north, edge_south = edges

    def slab(x, carry):
        u = padded[x + 1]
        row = rows_of(u.shape)
        total = storage[x] * u
        total = total + east_t[x + 1] * (u - padded[x + 2]) + east_t[x] * (u - padded[x])
        total = total + north_t[x] * (u - shift(u, -1, 0)) + south_t[x] * (u - shift(u, 1, 0))
        total = total + upper_t[x] * (u - shift(u, -1, 1)) + lower_t[x] * (u - shift(u, 1, 1))
        one = pl.ds(x, 1)
        north = jnp.where(row == cy - 1, edge_north[one] * (u - north_halo[one]), 0.0)
        total = total + jnp.where(row == 0, edge_south[one] * (u - south_halo[one]), north)
        out[x] = total
        return carry

    lax.fori_loop(0, cx, slab, 0, unroll=UNROLL)
    out[0] = out[0] + edge_west[...] * (padded[1] - padded[0])
    out[cx - 1] = out[cx - 1] + edge_east[...] * (padded[cx] - padded[cx + 1])


def strips_kernel(field, to_north, to_south):
    for x in range(field.shape[0]):
        to_north[x : x + 1] = field[x, field.shape[1] - 1 :]
        to_south[x : x + 1] = field[x, 0:1]


def inner_kernel(
    source, perm, storage,
    source_out, storage_out, west_out, east_out, east_t, north_t, south_t, upper_t, lower_t, diagonal, sums,
):
    cx, cy, cz = source.shape
    west_out[...] = perm[0]
    east_out[...] = perm[cx - 1]
    row = rows_of((cy, cz))
    west = jnp.zeros((cy, cz), jnp.float32)
    east_t[0] = west
    stored = total_r = jnp.zeros((8, LANES), jnp.float32)
    for x in range(cx):
        k = perm[x]
        east = harmonic(k, perm[x + 1]) if x + 1 < cx else jnp.zeros((cy, cz), jnp.float32)
        north = jnp.where(row == cy - 1, 0.0, harmonic(k, shift(k, -1, 0)))
        south = shift(north, 1, 0)
        upper = harmonic(k, shift(k, -1, 1))
        lower = shift(upper, 1, 1)
        east_t[x + 1] = east
        north_t[x] = north
        south_t[x] = south
        upper_t[x] = upper
        lower_t[x] = lower
        w, r = storage[x], source[x]
        diagonal[x] = w + east + west + north + south + upper + lower
        storage_out[x] = w
        source_out[x] = r
        stored = stored + fold(w)
        total_r = total_r + fold(r)
        west = east
    sums[...] = placed(((0, total_of(stored)), (2, total_of(total_r))))


def edge_kernel(perm_north, strip_north, west, east, sums, edge_north, to_a, to_b, out):
    north = harmonic(strip_north[...], perm_north[...])
    edge_north[...] = north
    out[...] = jnp.broadcast_to(sums[...] + placed(((1, total_of(north)),)), out.shape)
    by_side(west[...], east[...], to_a, to_b)


def by_side(west, east, to_a, to_b):
    odd = lax.axis_index("group") % 2 == 1
    to_a[...] = jnp.where(odd, east, west)
    to_b[...] = jnp.where(odd, west, east)


def layers_kernel(field, to_a, to_b):
    by_side(field[0], field[field.shape[0] - 1], to_a, to_b)


def reduce_rows(margin, coupling, steps):
    before, after = shift(coupling, 1, 0), coupling
    factors = []
    for step in range(steps):
        h = 2**step
        inverse = 1.0 / (margin + before + after)
        from_before = before * shift(inverse, h, 0)
        from_after = after * shift(inverse, -h, 0)
        margin = margin + from_before * shift(margin, h, 0) + from_after * shift(margin, -h, 0)
        before, after = from_before * shift(before, h, 0), from_after * shift(after, -h, 0)
        factors.append((from_before, from_after))
    return factors, 1.0 / margin


def solve_rows(factors, last, right):
    for step, (from_before, from_after) in enumerate(factors):
        h = 2**step
        right = right + from_before * shift(right, h, 0) + from_after * shift(right, -h, 0)
    return right * last


def assemble_kernel(
    steps, perm_a, perm_b, table, source, perm_west, perm_east,
    east_in, north_in, south_in, upper_t, lower_t, diagonal, edge_north, perm_south, strip_south,
    edge_east, edge_west, edge_south, scale, w_east, w_west, w_north, w_south, w_upper, w_lower,
    u0_ref, to_a, to_b, to_north, to_south, first, work,
):
    cx, cy, cz = source.shape
    odd = lax.axis_index("group") % 2 == 1
    row = rows_of((cy, cz))
    a, b = perm_a[...], perm_b[...]
    edge_east[...] = harmonic(perm_east[...], jnp.where(odd, a, b))
    edge_west[...] = harmonic(jnp.where(odd, b, a), perm_west[...])
    edge_south[...] = harmonic(perm_south[...], strip_south[...])
    for x in range(cx):
        d = diagonal[x]
        d = d + jnp.where(row == cy - 1, edge_north[x : x + 1], jnp.where(row == 0, edge_south[x : x + 1], 0.0))
        if x == 0:
            d = d + edge_west[...]
        if x == cx - 1:
            d = d + edge_east[...]
        q = OMEGA / d
        scale[x] = q
        w_east[x] = q * east_in[x + 1]
        w_west[x] = q * east_in[x]
        w_north[x] = q * north_in[x]
        w_south[x] = q * south_in[x]
        w_upper[x] = q * upper_t[x]
        w_lower[x] = q * lower_t[x]
        s = q * source[x]
        first[x] = s
        work[0, x + 1] = s
    clear_ends(work)
    smooth(first, work, (w_east, w_west, w_north, w_south, w_upper, w_lower))

    t = table[...]
    members = t.shape[0]
    factors, last = reduce_rows(t / members, shift(t, -1, 1) * members, steps)
    c0 = solve_rows(factors, last, shift(t, -2, 1))
    lane = lax.broadcasted_iota(jnp.int32, t.shape, 1)
    c0 = total_of(jnp.where((rows_of(t.shape) == (my_sub() + members - LEAD_COARSE) % members) & (lane == 0), c0, 0.0))
    for x in range(cx):
        u = work[1, x + 1] + c0
        u0_ref[x] = u
        to_north[x : x + 1] = u[cy - 1 : cy]
        to_south[x : x + 1] = u[0:1]
    layers_kernel(u0_ref, to_a, to_b)


def fill(padded, field, halo_a, halo_b):
    odd = lax.axis_index("group") % 2 == 1
    cx = field.shape[0]
    a, b = halo_a[...], halo_b[...]
    padded[0] = jnp.where(odd, b, a)
    padded[cx + 1] = jnp.where(odd, a, b)
    for x in range(cx):
        padded[x + 1] = field[x]


def first_kernel(
    halo_a, halo_b, halo_north, halo_south, u0_ref, storage,
    east_t, north_t, south_t, upper_t, lower_t, edge_east, edge_west, edge_north, edge_south,
    scale, w_east, w_west, w_north, w_south, w_upper, w_lower,
    image, result, to_north, to_south, padded, first, work,
):
    cx, cy, cz = storage.shape
    fill(padded, u0_ref, halo_a, halo_b)
    inner, outer = (east_t, north_t, south_t, upper_t, lower_t), (edge_east, edge_west, edge_north, edge_south)
    apply(padded, halo_north, halo_south, storage, inner, outer, image)
    for x in range(cx):
        s = scale[x] * image[x]
        first[x] = s
        work[0, x + 1] = s
    clear_ends(work)
    smooth(first, work, (w_east, w_west, w_north, w_south, w_upper, w_lower))
    for x in range(cx):
        f1 = work[1, x + 1]
        result[x] = f1
        to_north[x : x + 1] = f1[cy - 1 : cy]
        to_south[x : x + 1] = f1[0:1]


def dots_kernel(groups, source, u0_ref, image, f1_ref, edge_east, edge_north, sums, out):
    r_u0 = u0_v0 = v0_f1 = total = jnp.zeros((8, LANES), jnp.float32)
    for x in range(source.shape[0]):
        r, u0, v0, f1 = source[x], u0_ref[x], image[x], f1_ref[x]
        r_u0 = r_u0 + fold(r * u0)
        u0_v0 = u0_v0 + fold(u0 * v0)
        v0_f1 = v0_f1 + fold(v0 * f1)
        total = total + fold(v0)
    me = lax.axis_index("group")
    totals = (
        (AGAINST * groups + me, total_of(total)),
        (STORED * groups + me, sums[0:1, 0:1]),
        (COUPLING * groups + me, total_of(edge_north[...])),
        (EAST * groups + me, total_of(fold(edge_east[...]))),
        (DOTS, total_of(r_u0)),
        (DOTS + 1, total_of(u0_v0)),
        (DOTS + 2, total_of(v0_f1)),
    )
    out[...] = placed(totals)


def second_kernel(
    groups, halo_a, halo_b, halo_north, halo_south, f1_ref, dots, storage,
    east_t, north_t, south_t, upper_t, lower_t, edge_east, edge_west, edge_north, edge_south,
    image, out, padded,
):
    fill(padded, f1_ref, halo_a, halo_b)
    inner, outer = (east_t, north_t, south_t, upper_t, lower_t), (edge_east, edge_west, edge_north, edge_south)
    apply(padded, halo_north, halo_south, storage, inner, outer, image)
    total = f1_g1 = jnp.zeros((8, LANES), jnp.float32)
    for x in range(storage.shape[0]):
        g1 = image[x]
        total = total + fold(g1)
        f1_g1 = f1_g1 + fold(f1_ref[x] * g1)
    me = lax.axis_index("group")
    scalars = dots[...] + placed(((IMAGE * groups + me, total_of(total)), (DOTS + 3, total_of(f1_g1))))
    core = lax.axis_index("core")
    cores = out.shape[1] // LANES
    out[...] = jnp.concatenate([jnp.where(core == at, scalars, 0.0) for at in range(cores)], axis=1)


def last_kernel(
    steps, groups, table, u0_ref, f1_ref, image, storage, edge_east, edge_west, edge_north, edge_south,
    scale, w_east, w_west, w_north, w_south, w_upper, w_lower, pressure_out, precond_out,
    first, work, pressure, precond, sems,
):
    cx, cy, cz = storage.shape
    t = table[...]
    members = t.shape[0]
    lane = lax.broadcasted_iota(jnp.int32, t.shape, 1)
    mine = (rows_of(t.shape) == (my_sub() + members - LEAD_LAST * lax.axis_size("core")) % members) & (lane == lax.axis_index("group"))

    def column(at):
        return shift(t, -at * groups, 1)

    def pick(value):
        return total_of(jnp.where(mine, value, 0.0))

    def to_the_east(value):
        return jnp.where(lane == groups - 1, shift(value, groups - 1, 1), shift(value, -1, 1))

    def to_the_west(value):
        return jnp.where(lane == 0, shift(value, 1 - groups, 1), shift(value, 1, 1))

    against, image_sum, stored, after, right = (column(at) for at in (AGAINST, IMAGE, STORED, COUPLING, EAST))
    factors, last = reduce_rows(stored / members, after * members, steps)
    c1 = solve_rows(factors, last, against)
    c_east, c_west, c_north, c_south = to_the_east(c1), to_the_west(c1), shift(c1, -1, 0), shift(c1, 1, 0)
    coupled = (
        stored * c1 + after * (c1 - c_north) + shift(after, 1, 0) * (c1 - c_south)
        + right * (c1 - c_east) + to_the_west(right) * (c1 - c_west)
    )
    c2 = solve_rows(factors, last, image_sum + coupled)
    valid = lane < groups
    sums = jnp.sum(t, axis=0, keepdims=True)
    r_u0, u0_v0, v0_u1, u1_v1 = (sums[:, DOTS + at : DOTS + at + 1] for at in range(4))
    v0_u1 = v0_u1 + total_of(jnp.where(valid, c1 * against, 0.0))
    u1_v1 = u1_v1 + total_of(jnp.where(valid, c1 * (2.0 * image_sum + coupled), 0.0))
    c1, c_east, c_west, c_north, c_south, c2 = (pick(c) for c in (c1, c_east, c_west, c_north, c_south, c2))

    a0 = r_u0 / u0_v0
    rz = a0 * a0 * v0_u1 - r_u0
    keep = 1.0 + rz / r_u0
    a1 = rz / (keep * keep * u0_v0 - 2.0 * keep * a0 * v0_u1 + a0 * a0 * u1_v1)
    p0, p1 = a0 + a1 * keep, a1 * a0

    def send(at, x):
        src, dst = ((pressure, pressure_out), (precond, precond_out))[at]
        copy = pltpu.make_async_copy(src.at[x], dst.at[x], sems.at[at, x])
        copy.start()
        return copy

    copies = []
    row = rows_of((cy, cz))
    for x in range(cx):
        pressure[x] = p0 * u0_ref[x] - p1 * (f1_ref[x] + c1)
        copies.append(send(0, x))
        one = slice(x, x + 1)
        edge = jnp.where(row == 0, edge_south[one] * (c1 - c_south), 0.0)
        edge = jnp.where(row == cy - 1, edge_north[one] * (c1 - c_north), edge)
        v1 = image[x] + storage[x] * c1 + edge
        if x == 0:
            v1 = v1 + edge_west[...] * (c1 - c_west)
        if x == cx - 1:
            v1 = v1 + edge_east[...] * (c1 - c_east)
        s = scale[x] * v1
        first[x] = s
        work[0, x + 1] = s
    clear_ends(work)
    smooth(first, work, (w_east, w_west, w_north, w_south, w_upper, w_lower))
    for x in range(cx):
        precond[x] = u0_ref[x] - p0 * (f1_ref[x] + c1) + p1 * (work[1, x + 1] + c2)
        copies.append(send(1, x))
    for copy in copies:
        copy.wait()


def call(body, outs, scratch, *operands, cost=0, hbm=False):
    space = pl.BlockSpec(memory_space=pltpu.VMEM)
    return pl.pallas_call(
        body,
        out_shape=[jax.ShapeDtypeStruct(s, jnp.float32) for s in outs],
        in_specs=[space] * len(operands),
        out_specs=[pl.BlockSpec(memory_space=pl.ANY) if hbm else space] * len(outs),
        scratch_shapes=[pltpu.VMEM(s, jnp.float32) if isinstance(s, tuple) else s for s in scratch],
        compiler_params=pltpu.CompilerParams(vmem_limit_bytes=VMEM),
        cost_estimate=pl.CostEstimate(flops=cost, bytes_accessed=4 * cost, transcendentals=0) if cost else None,
    )(*operands)


def over_group(to_a, to_b):
    groups = lax.axis_size("group")
    a = lax.ppermute(to_a, "group", [(i, (((i + 1) ^ 1) - 1) % groups) for i in range(groups)])
    b = lax.ppermute(to_b, "group", [(i, i ^ 1) for i in range(groups)])
    return a, b


def over_sub(to_north, to_south):
    peers = lax.axis_size(SUB)
    up = [(i, (i + 1) % peers) for i in range(peers)]
    south = lax.ppermute(to_north, SUB, up)
    north = lax.ppermute(to_south, SUB, [(j, i) for i, j in up])
    return north, south


def gather(row, axis, first=0):
    peers = lax.axis_size(axis)
    order = [[(first + i) % peers for i in range(peers)]]
    rows = jnp.broadcast_to(row, (peers, row.shape[1]))[:, None]
    return lax.all_to_all(rows, axis, 0, 0, axis_index_groups=order).reshape(peers, row.shape[1])


def shards(source, perm, storage):
    cx, cy, cz = source.shape
    groups, members = lax.axis_size("group"), lax.axis_size(SUB)
    steps = members.bit_length() - 1
    full, wide, layer, edge, row = (cx, cy, cz), (cx + 2, cy, cz), (cy, cz), (cx, cz), (1, LANES)
    rounds = [full, (2,) + wide]
    strip_north, strip_south = call(strips_kernel, [edge, edge], [], perm)
    perm_north, perm_south = over_sub(strip_north, strip_south)
    source, storage, west, east, *inner, diagonal, sums = call(
        inner_kernel,
        [full, full, layer, layer, (cx + 1, cy, cz)] + [full] * 5 + [row],
        [],
        source, perm, storage, cost=2**21,
    )
    edge_north, to_a, to_b, scalars = call(
        edge_kernel,
        [edge, layer, layer, (members, LANES)],
        [],
        perm_north, strip_north, west, east, sums,
    )
    table = gather(scalars, SUB, LEAD_COARSE)
    edge_east, edge_west, edge_south, *weights, u0, to_a, to_b, to_north, to_south = call(
        functools.partial(assemble_kernel, steps),
        [layer, layer, edge] + [full] * 7 + [full, layer, layer, edge, edge],
        rounds,
        *over_group(to_a, to_b), table, source, west, east, *inner, diagonal, edge_north, perm_south, strip_south,
    )
    outer = [edge_east, edge_west, edge_north, edge_south]
    halos = over_group(to_a, to_b) + over_sub(to_north, to_south)
    v0, f1, to_north, to_south = call(
        first_kernel, [full, full, edge, edge], [wide] + rounds, *halos, u0, storage, *inner, *outer, *weights
    )
    to_a, to_b = call(layers_kernel, [layer, layer], [], f1)
    halos = over_group(to_a, to_b) + over_sub(to_north, to_south)
    (dots,) = call(
        functools.partial(dots_kernel, groups), [row], [],
        source, u0, v0, f1, edge_east, edge_north, sums, cost=2**20,
    )
    cores = lax.axis_size("core")
    g1, scalars = call(
        functools.partial(second_kernel, groups),
        [full, (1, cores * LANES)],
        [wide],
        *halos, f1, dots, storage, *inner, *outer,
    )
    scalars = gather(scalars, ("group", "core"), LEAD_GROUP * cores)
    scalars = sum(scalars[i : i + 1] for i in range(groups * cores))
    table = gather(scalars, "z", LEAD_LAST).reshape(members, LANES)
    return tuple(
        call(
            functools.partial(last_kernel, steps, groups),
            [full, full],
            rounds + [full, full, pltpu.SemaphoreType.DMA((2, cx))],
            table, u0, f1, g1, storage, *outer, *weights, hbm=True,
        )
    )


def solution(mesh):
    groups, members = (mesh.shape[axis] for axis in ("group", "sub"))
    cores = 2
    mesh = jax.sharding.Mesh(mesh.devices.reshape(groups, members // cores, cores), ("group", "z", "core"))
    spec = P("group", SUB, None)
    return jax.shard_map(shards, mesh=mesh, in_specs=(spec,) * 3, out_specs=(spec,) * 2, check_vma=False)
```

```python
import functools

import jax
import jax.numpy as jnp
from jax import lax
from jax.experimental import pallas as pl
from jax.experimental.pallas import tpu as pltpu
from jax.sharding import PartitionSpec as P

OMEGA = 0.8
LANES = 128
VMEM = 16 * 2**20
UNROLL = True
SUB = ("z", "core")
LEAD_COARSE, LEAD_GROUP, LEAD_LAST = 28, 10, 7
AGAINST, IMAGE, STORED, COUPLING, EAST = range(5)
DOTS = 120


def harmonic(left, right):
    return 2.0 * left * right / (left + right)


def shift(value, by, axis):
    return pltpu.roll(value, by % value.shape[axis], axis)


def my_sub():
    return lax.axis_index("z") * lax.axis_size("core") + lax.axis_index("core")


def rows_of(shape):
    return lax.broadcasted_iota(jnp.int32, shape, 0)


def fold(value):
    total = None
    for y in range(0, value.shape[0], 8):
        for z in range(0, value.shape[1], LANES):
            tile = value[y : y + 8, z : z + LANES]
            total = tile if total is None else total + tile
    return total


def total_of(value):
    return jnp.sum(value, axis=(0, 1), keepdims=True)


def placed(totals):
    lane = lax.broadcasted_iota(jnp.int32, (1, LANES), 1)
    row = jnp.zeros((1, LANES), jnp.float32)
    for at, total in totals:
        row = jnp.where(lane == at, total, row)
    return row


def smooth(first, work, weights):
    cx = first.shape[0]
    east, west, north, south, upper, lower = weights

    def sweep(src, dst):
        def slab(x, carry):
            s = src[x + 1]
            total = (1.0 - OMEGA) * s + first[x]
            total = total + east[x] * src[x + 2] + west[x] * src[x]
            total = total + north[x] * shift(s, -1, 0) + south[x] * shift(s, 1, 0)
            total = total + upper[x] * shift(s, -1, 1) + lower[x] * shift(s, 1, 1)
            dst[x + 1] = total
            return carry

        lax.fori_loop(0, cx, slab, 0, unroll=UNROLL)

    sweep(work.at[0], work.at[1])
    sweep(work.at[1], work.at[0])
    sweep(work.at[0], work.at[1])


def clear_ends(work):
    for at in range(2):
        for end in (0, work.shape[1] - 1):
            work[at, end] = jnp.zeros(work.shape[2:], jnp.float32)


def apply(padded, north_halo, south_halo, storage, inner, edges, out):
    cx, cy = storage.shape[:2]
    east_t, north_t, _, upper_t, _ = inner
    edge_east, edge_west, edge_north, edge_south = edges

    def slab(x, carry):
        u = padded[x + 1]
        row = rows_of(u.shape)
        total = storage[x] * u
        total = total + east_t[x + 1] * (u - padded[x + 2]) + east_t[x] * (u - padded[x])
        flux = north_t[x] * (u - shift(u, -1, 0))
        total = total + flux - shift(flux, 1, 0)
        flux = upper_t[x] * (u - shift(u, -1, 1))
        total = total + flux - shift(flux, 1, 1)
        one = pl.ds(x, 1)
        north = jnp.where(row == cy - 1, edge_north[one] * (u - north_halo[one]), 0.0)
        total = total + jnp.where(row == 0, edge_south[one] * (u - south_halo[one]), north)
        out[x] = total
        return carry

    lax.fori_loop(0, cx, slab, 0, unroll=UNROLL)
    out[0] = out[0] + edge_west[...] * (padded[1] - padded[0])
    out[cx - 1] = out[cx - 1] + edge_east[...] * (padded[cx] - padded[cx + 1])


def strips_kernel(field, to_north, to_south):
    for x in range(field.shape[0]):
        to_north[x : x + 1] = field[x, field.shape[1] - 1 :]
        to_south[x : x + 1] = field[x, 0:1]


def inner_kernel(
    source, perm, storage,
    source_out, storage_out, west_out, east_out, east_t, north_t, south_t, upper_t, lower_t, diagonal, sums,
):
    cx, cy, cz = source.shape
    west_out[...] = perm[0]
    east_out[...] = perm[cx - 1]
    row = rows_of((cy, cz))
    west = jnp.zeros((cy, cz), jnp.float32)
    east_t[0] = west
    stored = total_r = jnp.zeros((8, LANES), jnp.float32)
    for x in range(cx):
        k = perm[x]
        east = harmonic(k, perm[x + 1]) if x + 1 < cx else jnp.zeros((cy, cz), jnp.float32)
        north = jnp.where(row == cy - 1, 0.0, harmonic(k, shift(k, -1, 0)))
        south = shift(north, 1, 0)
        upper = harmonic(k, shift(k, -1, 1))
        lower = shift(upper, 1, 1)
        east_t[x + 1] = east
        north_t[x] = north
        south_t[x] = south
        upper_t[x] = upper
        lower_t[x] = lower
        w, r = storage[x], source[x]
        diagonal[x] = w + east + west + north + south + upper + lower
        storage_out[x] = w
        source_out[x] = r
        stored = stored + fold(w)
        total_r = total_r + fold(r)
        west = east
    sums[...] = placed(((0, total_of(stored)), (2, total_of(total_r))))


def edge_kernel(perm_north, strip_north, west, east, sums, edge_north, to_a, to_b, out):
    north = harmonic(strip_north[...], perm_north[...])
    edge_north[...] = north
    out[...] = jnp.broadcast_to(sums[...] + placed(((1, total_of(north)),)), out.shape)
    by_side(west[...], east[...], to_a, to_b)


def by_side(west, east, to_a, to_b):
    odd = lax.axis_index("group") % 2 == 1
    to_a[...] = jnp.where(odd, east, west)
    to_b[...] = jnp.where(odd, west, east)


def layers_kernel(field, to_a, to_b):
    by_side(field[0], field[field.shape[0] - 1], to_a, to_b)


def reduce_rows(margin, coupling, steps):
    before, after = shift(coupling, 1, 0), coupling
    factors = []
    for step in range(steps):
        h = 2**step
        inverse = 1.0 / (margin + before + after)
        from_before = before * shift(inverse, h, 0)
        from_after = after * shift(inverse, -h, 0)
        margin = margin + from_before * shift(margin, h, 0) + from_after * shift(margin, -h, 0)
        before, after = from_before * shift(before, h, 0), from_after * shift(after, -h, 0)
        factors.append((from_before, from_after))
    return factors, 1.0 / margin


def solve_rows(factors, last, right):
    for step, (from_before, from_after) in enumerate(factors):
        h = 2**step
        right = right + from_before * shift(right, h, 0) + from_after * shift(right, -h, 0)
    return right * last


def assemble_kernel(
    steps, perm_a, perm_b, table, source, perm_west, perm_east,
    east_in, north_in, south_in, upper_t, lower_t, diagonal, edge_north, perm_south, strip_south,
    edge_east, edge_west, edge_south, scale, w_east, w_west, w_north, w_south, w_upper, w_lower,
    u0_ref, to_a, to_b, to_north, to_south, first, work,
):
    cx, cy, cz = source.shape
    odd = lax.axis_index("group") % 2 == 1
    row = rows_of((cy, cz))
    a, b = perm_a[...], perm_b[...]
    edge_east[...] = harmonic(perm_east[...], jnp.where(odd, a, b))
    edge_west[...] = harmonic(jnp.where(odd, b, a), perm_west[...])
    edge_south[...] = harmonic(perm_south[...], strip_south[...])
    for x in range(cx):
        d = diagonal[x]
        d = d + jnp.where(row == cy - 1, edge_north[x : x + 1], jnp.where(row == 0, edge_south[x : x + 1], 0.0))
        if x == 0:
            d = d + edge_west[...]
        if x == cx - 1:
            d = d + edge_east[...]
        q = OMEGA / d
        scale[x] = q
        w_east[x] = q * east_in[x + 1]
        w_west[x] = q * east_in[x]
        w_north[x] = q * north_in[x]
        w_south[x] = q * south_in[x]
        w_upper[x] = q * upper_t[x]
        w_lower[x] = q * lower_t[x]
        s = q * source[x]
        first[x] = s
        work[0, x + 1] = s
    clear_ends(work)
    smooth(first, work, (w_east, w_west, w_north, w_south, w_upper, w_lower))

    t = table[...]
    members = t.shape[0]
    factors, last = reduce_rows(t / members, shift(t, -1, 1) * members, steps)
    c0 = solve_rows(factors, last, shift(t, -2, 1))
    lane = lax.broadcasted_iota(jnp.int32, t.shape, 1)
    c0 = total_of(jnp.where((rows_of(t.shape) == (my_sub() + members - LEAD_COARSE) % members) & (lane == 0), c0, 0.0))
    for x in range(cx):
        u = work[1, x + 1] + c0
        u0_ref[x] = u
        to_north[x : x + 1] = u[cy - 1 : cy]
        to_south[x : x + 1] = u[0:1]
    layers_kernel(u0_ref, to_a, to_b)


def fill(padded, field, halo_a, halo_b):
    odd = lax.axis_index("group") % 2 == 1
    cx = field.shape[0]
    a, b = halo_a[...], halo_b[...]
    padded[0] = jnp.where(odd, b, a)
    padded[cx + 1] = jnp.where(odd, a, b)
    for x in range(cx):
        padded[x + 1] = field[x]


def first_kernel(
    halo_a, halo_b, halo_north, halo_south, u0_ref, storage,
    east_t, north_t, south_t, upper_t, lower_t, edge_east, edge_west, edge_north, edge_south,
    scale, w_east, w_west, w_north, w_south, w_upper, w_lower,
    image, result, to_north, to_south, padded, first, work,
):
    cx, cy, cz = storage.shape
    fill(padded, u0_ref, halo_a, halo_b)
    inner, outer = (east_t, north_t, south_t, upper_t, lower_t), (edge_east, edge_west, edge_north, edge_south)
    apply(padded, halo_north, halo_south, storage, inner, outer, image)
    for x in range(cx):
        s = scale[x] * image[x]
        first[x] = s
        work[0, x + 1] = s
    clear_ends(work)
    smooth(first, work, (w_east, w_west, w_north, w_south, w_upper, w_lower))
    for x in range(cx):
        f1 = work[1, x + 1]
        result[x] = f1
        to_north[x : x + 1] = f1[cy - 1 : cy]
        to_south[x : x + 1] = f1[0:1]


def dots_kernel(groups, source, u0_ref, image, f1_ref, edge_east, edge_north, sums, out):
    r_u0 = u0_v0 = v0_f1 = total = jnp.zeros((8, LANES), jnp.float32)
    for x in range(source.shape[0]):
        r, u0, v0, f1 = source[x], u0_ref[x], image[x], f1_ref[x]
        r_u0 = r_u0 + fold(r * u0)
        u0_v0 = u0_v0 + fold(u0 * v0)
        v0_f1 = v0_f1 + fold(v0 * f1)
        total = total + fold(v0)
    me = lax.axis_index("group")
    totals = (
        (AGAINST * groups + me, total_of(total)),
        (STORED * groups + me, sums[0:1, 0:1]),
        (COUPLING * groups + me, total_of(edge_north[...])),
        (EAST * groups + me, total_of(fold(edge_east[...]))),
        (DOTS, total_of(r_u0)),
        (DOTS + 1, total_of(u0_v0)),
        (DOTS + 2, total_of(v0_f1)),
    )
    out[...] = placed(totals)


def second_kernel(
    groups, halo_a, halo_b, halo_north, halo_south, f1_ref, dots, storage,
    east_t, north_t, south_t, upper_t, lower_t, edge_east, edge_west, edge_north, edge_south,
    image, out, padded,
):
    fill(padded, f1_ref, halo_a, halo_b)
    inner, outer = (east_t, north_t, south_t, upper_t, lower_t), (edge_east, edge_west, edge_north, edge_south)
    apply(padded, halo_north, halo_south, storage, inner, outer, image)
    total = f1_g1 = jnp.zeros((8, LANES), jnp.float32)
    for x in range(storage.shape[0]):
        g1 = image[x]
        total = total + fold(g1)
        f1_g1 = f1_g1 + fold(f1_ref[x] * g1)
    me = lax.axis_index("group")
    scalars = dots[...] + placed(((IMAGE * groups + me, total_of(total)), (DOTS + 3, total_of(f1_g1))))
    core = lax.axis_index("core")
    cores = out.shape[1] // LANES
    out[...] = jnp.concatenate([jnp.where(core == at, scalars, 0.0) for at in range(cores)], axis=1)


def last_kernel(
    steps, groups, table, u0_ref, f1_ref, image, storage, edge_east, edge_west, edge_north, edge_south,
    scale, w_east, w_west, w_north, w_south, w_upper, w_lower, pressure_out, precond_out,
    first, work, pressure, precond, sems,
):
    cx, cy, cz = storage.shape
    t = table[...]
    members = t.shape[0]
    lane = lax.broadcasted_iota(jnp.int32, t.shape, 1)
    mine = (rows_of(t.shape) == (my_sub() + members - LEAD_LAST * lax.axis_size("core")) % members) & (lane == lax.axis_index("group"))

    def column(at):
        return shift(t, -at * groups, 1)

    def pick(value):
        return total_of(jnp.where(mine, value, 0.0))

    def to_the_east(value):
        return jnp.where(lane == groups - 1, shift(value, groups - 1, 1), shift(value, -1, 1))

    def to_the_west(value):
        return jnp.where(lane == 0, shift(value, 1 - groups, 1), shift(value, 1, 1))

    against, image_sum, stored, after, right = (column(at) for at in (AGAINST, IMAGE, STORED, COUPLING, EAST))
    factors, last = reduce_rows(stored / members, after * members, steps)
    c1 = solve_rows(factors, last, against)
    c_east, c_west, c_north, c_south = to_the_east(c1), to_the_west(c1), shift(c1, -1, 0), shift(c1, 1, 0)
    coupled = (
        stored * c1 + after * (c1 - c_north) + shift(after, 1, 0) * (c1 - c_south)
        + right * (c1 - c_east) + to_the_west(right) * (c1 - c_west)
    )
    c1_all = c1
    c1, c_east, c_west, c_north, c_south = (pick(c) for c in (c1, c_east, c_west, c_north, c_south))
    def send(at, x):
        src, dst = ((pressure, pressure_out), (precond, precond_out))[at]
        copy = pltpu.make_async_copy(src.at[x], dst.at[x], sems.at[at, x])
        copy.start()
        return copy

    copies = []
    row = rows_of((cy, cz))
    for x in range(cx):
        one = slice(x, x + 1)
        edge = jnp.where(row == 0, edge_south[one] * (c1 - c_south), 0.0)
        edge = jnp.where(row == cy - 1, edge_north[one] * (c1 - c_north), edge)
        v1 = image[x] + storage[x] * c1 + edge
        if x == 0:
            v1 = v1 + edge_west[...] * (c1 - c_west)
        if x == cx - 1:
            v1 = v1 + edge_east[...] * (c1 - c_east)
        s = scale[x] * v1
        first[x] = s
        work[0, x + 1] = s
    clear_ends(work)
    smooth(first, work, (w_east, w_west, w_north, w_south, w_upper, w_lower))
    c2 = solve_rows(factors, last, image_sum + coupled)
    valid = lane < groups
    sums = jnp.sum(t, axis=0, keepdims=True)
    r_u0, u0_v0, v0_u1, u1_v1 = (sums[:, DOTS + at : DOTS + at + 1] for at in range(4))
    v0_u1 = v0_u1 + total_of(jnp.where(valid, c1_all * against, 0.0))
    u1_v1 = u1_v1 + total_of(jnp.where(valid, c1_all * (2.0 * image_sum + coupled), 0.0))

    c2 = pick(c2)
    a0 = r_u0 / u0_v0
    rz = a0 * a0 * v0_u1 - r_u0
    keep = 1.0 + rz / r_u0
    a1 = rz / (keep * keep * u0_v0 - 2.0 * keep * a0 * v0_u1 + a0 * a0 * u1_v1)
    p0, p1 = a0 + a1 * keep, a1 * a0

    for x in range(cx):
        pressure[x] = p0 * u0_ref[x] - p1 * (f1_ref[x] + c1)
        copies.append(send(0, x))
        precond[x] = u0_ref[x] - p0 * (f1_ref[x] + c1) + p1 * (work[1, x + 1] + c2)
        copies.append(send(1, x))
    for copy in copies:
        copy.wait()


def call(body, outs, scratch, *operands, cost=0, hbm=False):
    space = pl.BlockSpec(memory_space=pltpu.VMEM)
    return pl.pallas_call(
        body,
        out_shape=[jax.ShapeDtypeStruct(s, jnp.float32) for s in outs],
        in_specs=[space] * len(operands),
        out_specs=[pl.BlockSpec(memory_space=pl.ANY) if hbm else space] * len(outs),
        scratch_shapes=[pltpu.VMEM(s, jnp.float32) if isinstance(s, tuple) else s for s in scratch],
        compiler_params=pltpu.CompilerParams(vmem_limit_bytes=VMEM),
        cost_estimate=pl.CostEstimate(flops=cost, bytes_accessed=4 * cost, transcendentals=0) if cost else None,
    )(*operands)


def over_group(to_a, to_b):
    groups = lax.axis_size("group")
    a = lax.ppermute(to_a, "group", [(i, (((i + 1) ^ 1) - 1) % groups) for i in range(groups)])
    b = lax.ppermute(to_b, "group", [(i, i ^ 1) for i in range(groups)])
    return a, b


def over_sub(to_north, to_south):
    peers = lax.axis_size(SUB)
    up = [(i, (i + 1) % peers) for i in range(peers)]
    south = lax.ppermute(to_north, SUB, up)
    north = lax.ppermute(to_south, SUB, [(j, i) for i, j in up])
    return north, south


def gather(row, axis, first=0):
    peers = lax.axis_size(axis)
    order = [[(first + i) % peers for i in range(peers)]]
    rows = jnp.broadcast_to(row, (peers, row.shape[1]))[:, None]
    return lax.all_to_all(rows, axis, 0, 0, axis_index_groups=order).reshape(peers, row.shape[1])


def shards(source, perm, storage):
    cx, cy, cz = source.shape
    groups, members = lax.axis_size("group"), lax.axis_size(SUB)
    steps = members.bit_length() - 1
    full, wide, layer, edge, row = (cx, cy, cz), (cx + 2, cy, cz), (cy, cz), (cx, cz), (1, LANES)
    rounds = [full, (2,) + wide]
    strip_north, strip_south = call(strips_kernel, [edge, edge], [], perm)
    perm_north, perm_south = over_sub(strip_north, strip_south)
    source, storage, west, east, *inner, diagonal, sums = call(
        inner_kernel,
        [full, full, layer, layer, (cx + 1, cy, cz)] + [full] * 5 + [row],
        [],
        source, perm, storage, cost=2**21,
    )
    edge_north, to_a, to_b, scalars = call(
        edge_kernel,
        [edge, layer, layer, (members, LANES)],
        [],
        perm_north, strip_north, west, east, sums,
    )
    table = gather(scalars, SUB, LEAD_COARSE)
    edge_east, edge_west, edge_south, *weights, u0, to_a, to_b, to_north, to_south = call(
        functools.partial(assemble_kernel, steps),
        [layer, layer, edge] + [full] * 7 + [full, layer, layer, edge, edge],
        rounds,
        *over_group(to_a, to_b), table, source, west, east, *inner, diagonal, edge_north, perm_south, strip_south,
    )
    outer = [edge_east, edge_west, edge_north, edge_south]
    halos = over_group(to_a, to_b) + over_sub(to_north, to_south)
    v0, f1, to_north, to_south = call(
        first_kernel, [full, full, edge, edge], [wide] + rounds, *halos, u0, storage, *inner, *outer, *weights
    )
    to_a, to_b = call(layers_kernel, [layer, layer], [], f1)
    halos = over_group(to_a, to_b) + over_sub(to_north, to_south)
    (dots,) = call(
        functools.partial(dots_kernel, groups), [row], [],
        source, u0, v0, f1, edge_east, edge_north, sums, cost=2**20,
    )
    cores = lax.axis_size("core")
    g1, scalars = call(
        functools.partial(second_kernel, groups),
        [full, (1, cores * LANES)],
        [wide],
        *halos, f1, dots, storage, *inner, *outer,
    )
    scalars = gather(scalars, ("group", "core"), LEAD_GROUP * cores)
    scalars = sum(scalars[i : i + 1] for i in range(groups * cores))
    table = gather(scalars, "z", LEAD_LAST).reshape(members, LANES)
    return tuple(
        call(
            functools.partial(last_kernel, steps, groups),
            [full, full],
            rounds + [full, full, pltpu.SemaphoreType.DMA((2, cx))],
            table, u0, f1, g1, storage, *outer, *weights, hbm=True,
        )
    )


def solution(mesh):
    groups, members = (mesh.shape[axis] for axis in ("group", "sub"))
    cores = 2
    mesh = jax.sharding.Mesh(mesh.devices.reshape(groups, members // cores, cores), ("group", "z", "core"))
    spec = P("group", SUB, None)
    return jax.shard_map(shards, mesh=mesh, in_specs=(spec,) * 3, out_specs=(spec,) * 2, check_vma=False)
```
